256 devices in a mesh: seq: 32 (over z, x), head: 8 (over y, core).
Axes of the slice: x: 4, y: 4, z: 8, core: 2. Of those that a mesh axis runs over, the one named last changes fastest.
Arguments:
- tokens: bfloat16 [8192, 2048], P('seq', 'head'), may hold values from -6 to 6
- in_weight: bfloat16 [2048, 12288], P(None, 'head'), may hold values from -0.125 to 0.125
- gate_weight: bfloat16 [2048, 64], P(None, 'head'), may hold values from -0.125 to 0.125
- conv_weight: bfloat16 [4, 16, 512], P(None, 'head'), may hold values from -3 to 3
- decay_scale: float32 [32], P('head'), may hold values from 1e-05 to 0.1
- dt_bias: float32 [32], P('head'), may hold values from -3 to 1
- beta_shift: float32 [32], P('head'), may hold values from -1 to 6
- norm_gain: float32 [128], replicated, may hold values from 0.1 to 1.9
- out_weight: bfloat16 [4096, 2048], P('head'), may hold values from -0.09375 to 0.09375
Outputs:
- layer_out: bfloat16 [8192, 2048], P('seq', 'head')
The draws below stay inside these ranges and needn't reach their ends.
All inputs are finite; a program needn't handle non-finite values.
Results may differ from the reference program's by a relative error of at most 0.02.
Values may be sent and summed in bfloat16 or wider, within the bound.
A program may use at most 128 MiB of HBM per device.

```python
import math
import jax
import jax.numpy as jnp
from jax import lax

D = 2048
QK_HEADS = 16
V_HEADS = 32
DK = 128
DV = 128
KERNEL = 4
TOKENS = 8192
N_HEAD = 8


def block_scale(key, shape, split, smallest, top_value):
    gain = 1.0
    for position, parts in split:
        draws = jax.random.uniform(jax.random.fold_in(jax.random.fold_in(key, 6), position), (parts,), jnp.float32, smallest / len(split), top_value / len(split))
        gain = gain * jnp.repeat(jnp.exp(draws), shape[position] // parts).reshape((-1,) + (1,) * (len(shape) - 1 - position))
    return gain


def scatter_about(key, dims, width, most, pieces=(), kind=jnp.bfloat16):
    array = jax.random.normal(key, dims, jnp.float32) * width
    if len(pieces) > 0:
        array = block_scale(key, dims, pieces, -0.22, 0.18) * array
    return jnp.clip(array, min=-most, max=most).astype(kind)


def setup_inputs(seed: int = 0) -> dict:
    splits = jax.random.split(jax.random.key(seed), 10)
    tokens = scatter_about(splits[0], (TOKENS, D), 1.0, 6.0, ((0, 32), (1, 8)))
    in_weight = scatter_about(splits[1], (D, QK_HEADS * (2 * DK + 4 * DV)), D ** -0.5, 0.125, ((1, 8),))
    gate_weight = scatter_about(splits[2], (D, QK_HEADS * 4), D ** -0.5, 0.125, ((1, 8),))
    conv_weight = scatter_about(splits[3], (KERNEL, QK_HEADS, 2 * DK + 2 * DV), KERNEL ** -0.5, 3.0, ((1, 8),))
    decay_scale = jnp.clip(jnp.exp(math.log(0.1) - 9.2103404 * jax.random.uniform(splits[4], (V_HEADS,), jnp.float32) ** block_scale(splits[4], (V_HEADS,), ((0, 8),), -0.2, 0.2)), 9.999999747378752e-06, 0.1)
    dt_bias = jnp.clip(-3.0 + 4.0 * jax.random.uniform(splits[5], (V_HEADS,), jnp.float32) ** block_scale(splits[5], (V_HEADS,), ((0, 8),), -0.2, 0.2), -3.0, 1.0)
    beta_shift = jnp.clip(-1.0 + 7.0 * jax.random.uniform(splits[6], (V_HEADS,), jnp.float32) ** block_scale(splits[6], (V_HEADS,), ((0, 8),), -0.2, 0.2), -1.0, 6.0)
    norm_gain = jnp.clip(1.0 + 0.18 * jax.random.normal(splits[7], (DV,), jnp.float32), 0.1, 1.9)
    out_weight = scatter_about(splits[8], (V_HEADS * DV, D), (V_HEADS * DV) ** -0.5, 0.09375, ((0, 8),))
    return dict(tokens=tokens, in_weight=in_weight, gate_weight=gate_weight, conv_weight=conv_weight, decay_scale=decay_scale, dt_bias=dt_bias, beta_shift=beta_shift, norm_gain=norm_gain, out_weight=out_weight)


PRECISE = lax.Precision.HIGHEST
epsilon = 1e-06

def reference(tokens, in_weight, gate_weight, conv_weight, decay_scale, dt_bias, beta_shift, norm_gain, out_weight):
    length = tokens.shape[0]
    group_width = 2 * DK + 4 * DV
    conv_width = 2 * DK + 2 * DV
    projected = jnp.dot(tokens, in_weight, preferred_element_type=jnp.float32).astype(jnp.bfloat16)
    gating = jnp.dot(tokens, gate_weight, preferred_element_type=jnp.float32)
    mixed = projected.reshape(length, QK_HEADS, group_width)
    conv_part = mixed[:, :, :conv_width].astype(jnp.float32)
    gate_part = mixed[:, :, conv_width:]
    extended = jnp.concatenate([jnp.zeros((KERNEL - 1, QK_HEADS, conv_width), jnp.float32), conv_part], 0)
    filters = conv_weight.astype(jnp.float32)
    summed = filters[0] * extended[0:length]
    for offset in range(1, KERNEL):
        summed = summed + filters[offset] * extended[offset:offset + length]
    filtered = jax.nn.silu(summed)
    query_rows = filtered[:, :, :DK]
    key_rows = filtered[:, :, DK:2 * DK]
    value_rows = filtered[:, :, 2 * DK:].reshape(length, V_HEADS, DV)
    query_rows = query_rows / jnp.sqrt(lax.optimization_barrier(jnp.sum(query_rows * query_rows, -1, keepdims=True)) + epsilon) * DK ** (-0.5)
    key_rows = key_rows / jnp.sqrt(lax.optimization_barrier(jnp.sum(key_rows * key_rows, -1, keepdims=True)) + epsilon)
    query_rows = jnp.repeat(query_rows, 2, axis=1)
    key_rows = jnp.repeat(key_rows, 2, axis=1)
    grouped = gating.reshape(length, QK_HEADS, 4)
    beta_rate = jax.nn.sigmoid(grouped[:, :, :2].reshape(length, V_HEADS) - beta_shift)
    log_gate = -decay_scale * jax.nn.softplus(grouped[:, :, 2:].reshape(length, V_HEADS) + dt_bias)

    def advance(current, inputs):
        query_now, key_now, value_now, gate_now, beta_now = inputs
        current = current * jnp.exp(gate_now)[:, None, None]
        predicted = jnp.einsum('hwd,hd->hw', current, key_now, precision=PRECISE)
        current = current + (beta_now[:, None] * (value_now - predicted))[:, :, None] * key_now[:, None, :]
        return (current, jnp.einsum('hwd,hd->hw', current, query_now, precision=PRECISE))
    initial = jnp.zeros((V_HEADS, DV, DK), jnp.float32)
    _, attended = lax.scan(advance, initial, (query_rows, key_rows, value_rows, log_gate, beta_rate))
    output_gate = gate_part.reshape(length, V_HEADS, DV).astype(jnp.float32)
    scale_back = 1.0 / jnp.sqrt(lax.optimization_barrier(jnp.mean(attended * attended, -1, keepdims=True)) + epsilon)
    hidden = (attended * scale_back * norm_gain * jax.nn.silu(output_gate)).astype(jnp.bfloat16)
    hidden = hidden.reshape(length, V_HEADS * DV)
    block_cols = V_HEADS * DV // N_HEAD
    total = jnp.zeros((length, D), jnp.float32)
    for block in range(N_HEAD):
        partial_value = jnp.dot(hidden[:, block * block_cols:(block + 1) * block_cols], out_weight[block * block_cols:(block + 1) * block_cols], preferred_element_type=jnp.float32).astype(jnp.bfloat16)
        partial_value = lax.optimization_barrier(partial_value)
        total = total + partial_value.astype(jnp.float32)
    return total.astype(jnp.bfloat16)
```

```python
import functools

import jax
import jax.numpy as jnp
from jax import lax
from jax.experimental import pallas as pl
from jax.experimental.pallas import tpu as pltpu
from jax.sharding import PartitionSpec as P

F32 = jnp.float32
BF16 = jnp.bfloat16
EPSILON = 1e-06

ROWS = 256
HALF = 128
HEAD = 128
FEATURES = 256
GROUPS = 2
VALUE_HEADS = 4
CONV = 512
GROUP = 768
HALO = 16
NX = 4
NZ = 8
NY = 4

ORDER = ((0, 0), (0, 1), (1, 0), (1, 1), (3, 0), (3, 1), (2, 0), (2, 1))
SLOT = {pair: slot for slot, pair in enumerate(ORDER)}


def matmul(a, b):
    return jnp.dot(a, b, preferred_element_type=F32)


def matmul_t(a, b):
    return lax.dot_general(a, b, (((1,), (1,)), ((), ())), preferred_element_type=F32)


def silu(v):
    return 0.5 * v * (1.0 + jnp.tanh(0.5 * v))


def kernel(
    tokens_hbm,
    in_weight_hbm,
    gate_weight,
    conv_weight,
    decay_scale,
    dt_bias,
    beta_shift,
    norm_gain,
    out_weight_hbm,
    out_ref,
    tok,
    w_in,
    w_out,
    acc,
    ext,
    halo_out,
    halo_in,
    gates,
    qn,
    kn,
    vn,
    maps,
    row_maps,
    row_total,
    all_totals,
    fold_states,
    state_in,
    row_states,
    states,
    loc,
    qeff,
    own,
    sib_out,
    sib_in,
    far_out,
    far_in,
    near_out,
    near_in,
    load_sem,
    win_sem,
    wout_sem,
    tok_send,
    tok_recv,
    halo_sem,
    row_send,
    row_recv,
    tot_send,
    tot_recv,
    fold_send,
    fold_recv,
    back_send,
    back_recv,
    sib_send,
    sib_recv,
    ring_send,
    ring_recv,
):
    seq = lax.axis_index("seq")
    head = lax.axis_index("head")
    z, x = lax.div(seq, NX), lax.rem(seq, NX)
    y, c = lax.div(head, 2), lax.rem(head, 2)

    def head_at(r, other):
        core = c if other == 0 else 1 - c
        return lax.rem(y + r, NY) * 2 + core

    above = (seq, head_at(1, 0))
    below = (seq, head_at(3, 0))
    sibling = (seq, head_at(0, 1))

    def remote(src, dst, send, recv, device):
        return pltpu.make_async_remote_copy(
            src_ref=src,
            dst_ref=dst,
            send_sem=send,
            recv_sem=recv,
            device_id=device,
            device_id_type=pl.DeviceIdType.MESH,
        )

    load_tok = pltpu.make_async_copy(tokens_hbm, tok.at[:, pl.ds(0, FEATURES)], load_sem)
    load_tok.start()
    load_in = []
    for slot, (r, other) in enumerate(ORDER):
        rows = pl.ds(pl.multiple_of(head_at(r, other) * FEATURES, FEATURES), FEATURES)
        copy = pltpu.make_async_copy(
            in_weight_hbm.at[rows], w_in.at[pl.ds(slot * FEATURES, FEATURES)], win_sem.at[slot]
        )
        copy.start()
        load_in.append(copy)
    load_out = []
    for slot, (r, other) in enumerate(ORDER):
        columns = pl.ds(pl.multiple_of(head_at(r, other) * FEATURES, FEATURES), FEATURES)
        copy = pltpu.make_async_copy(out_weight_hbm.at[:, columns], w_out.at[slot], wout_sem.at[slot])
        copy.start()
        load_out.append(copy)

    barrier = pltpu.get_barrier_semaphore()
    next_seq = lax.rem(seq + 1, NX * NZ)
    prev_seq = lax.rem(seq + NX * NZ - 1, NX * NZ)
    partners = [above, below, sibling, (next_seq, head), (prev_seq, head)]
    partners += [(z * NX + lax.rem(x + r, NX), head) for r in range(1, NX)]
    partners += [(lax.rem(z + r, NZ) * NX + x, head) for r in range(1, NZ)]
    for device in partners:
        pl.semaphore_signal(barrier, inc=1, device_id=device, device_id_type=pl.DeviceIdType.MESH)
    pl.semaphore_wait(barrier, len(partners))
    load_tok.wait()

    def tok_part(slot, half):
        return tok.at[pl.ds(half * HALF, HALF), pl.ds(slot * FEATURES, FEATURES)]

    sends = []

    def send_tok(src_slot, dst_slot, half, device):
        copy = remote(
            tok_part(src_slot, half),
            tok_part(dst_slot, half),
            tok_send.at[len(sends)],
            tok_recv.at[2 * dst_slot + half],
            device,
        )
        copy.start()
        sends.append(copy)

    def wait_tok(slot, half):
        remote(
            tok_part(slot, half), tok_part(slot, half), tok_send.at[0], tok_recv.at[2 * slot + half], sibling
        ).wait_recv()

    up, down, far = SLOT[(1, 0)], SLOT[(3, 0)], SLOT[(2, 0)]
    send_tok(0, down, 0, above)
    send_tok(0, up, 1, below)
    send_tok(0, down, 1, above)
    send_tok(0, up, 0, below)
    send_tok(0, 1, 0, sibling)
    send_tok(0, 1, 1, sibling)
    wait_tok(down, 0)
    send_tok(down, far, 0, above)
    wait_tok(up, 1)
    send_tok(up, far, 1, below)
    send_tok(down, down + 1, 0, sibling)
    send_tok(up, up + 1, 1, sibling)

    def project(first, count, start):
        depth = count * FEATURES
        rows = pl.ds(first * FEATURES, depth)

        def tile(j, carry):
            columns = pl.ds(pl.multiple_of(j * 256, 256), 256)
            part = matmul(tok[:, rows], w_in[rows, columns])
            if start:
                acc[:, columns] = part
            else:
                acc[:, columns] += part
            return carry

        lax.fori_loop(0, GROUPS * GROUP // 256, tile, 0)

    wait_tok(1, 0)
    wait_tok(1, 1)
    load_in[0].wait()
    load_in[1].wait()
    project(0, 2, True)
    wait_tok(down, 1)
    send_tok(down, down + 1, 1, sibling)
    wait_tok(up, 0)
    send_tok(up, up + 1, 0, sibling)
    for slot in (up + 1, down + 1):
        wait_tok(slot, 0)
        wait_tok(slot, 1)
    for slot in range(2, 6):
        load_in[slot].wait()
    project(2, 4, False)
    wait_tok(far, 0)
    send_tok(far, far + 1, 0, sibling)
    wait_tok(far, 1)
    send_tok(far, far + 1, 1, sibling)
    wait_tok(far + 1, 0)
    wait_tok(far + 1, 1)
    load_in[6].wait()
    load_in[7].wait()
    project(6, 2, False)
    for copy in sends:
        copy.wait_send()

    for g in range(GROUPS):
        columns = acc[:, g * GROUP : g * GROUP + CONV].astype(BF16)
        halo_out[:, g * CONV : (g + 1) * CONV] = columns[ROWS - HALO :]
        ext[8:, g * CONV : (g + 1) * CONV] = columns.astype(F32)
    send_halo = remote(halo_out, halo_in, halo_sem.at[0], halo_sem.at[1], (next_seq, head))
    send_halo.start()

    gating = jnp.zeros((ROWS, HEAD), F32)
    for slot, (r, other) in enumerate(ORDER):
        rows = pl.ds(pl.multiple_of(head_at(r, other) * FEATURES, FEATURES), FEATURES)
        weight = gate_weight[rows, :]
        weight = jnp.concatenate([weight, jnp.zeros((FEATURES, HEAD - weight.shape[1]), BF16)], 1)
        gating = gating + matmul(tok[:, slot * FEATURES : (slot + 1) * FEATURES], weight)
    lane = lax.broadcasted_iota(jnp.int32, (1, HEAD), 1)
    shift = jnp.zeros((1, HEAD), F32)
    bias = jnp.zeros((1, HEAD), F32)
    scale = jnp.zeros((1, HEAD), F32)
    for h in range(VALUE_HEADS):
        g, r = divmod(h, 2)
        shift = jnp.where(lane == 4 * g + r, beta_shift[h], shift)
        bias = jnp.where(lane == 4 * g + 2 + r, dt_bias[h], bias)
        scale = jnp.where(lane == 4 * g + 2 + r, decay_scale[h], scale)
    strength = jax.nn.sigmoid(gating - shift)
    shifted = gating + bias
    softplus = jnp.maximum(shifted, 0.0) + jnp.log1p(jnp.exp(-jnp.abs(shifted)))
    log_gate = -scale * softplus
    row_id = lax.broadcasted_iota(jnp.int32, (ROWS, ROWS), 0)
    col_id = lax.broadcasted_iota(jnp.int32, (ROWS, ROWS), 1)
    ones = jnp.where(col_id <= row_id, 1.0, 0.0).astype(BF16)
    cumulative = jnp.zeros((ROWS, HEAD), F32)
    rest = log_gate
    for _ in range(3):
        piece = rest.astype(BF16)
        cumulative = cumulative + matmul(ones, piece)
        rest = rest - piece.astype(F32)
    cumulative_t = jnp.transpose(cumulative)
    gates[0] = strength
    gates[1] = cumulative

    def convolve(first, count):
        for g in range(GROUPS):
            for block in range(CONV // HEAD):
                lanes = pl.ds(g * CONV + block * HEAD, HEAD)
                total = jnp.zeros((count, HEAD), F32)
                for tap in range(4):
                    weight = conv_weight[tap, g : g + 1, block * HEAD : (block + 1) * HEAD].astype(F32)
                    total = total + weight * ext[pl.ds(first + 5 + tap, count), lanes]
                value = silu(total)
                rows = pl.ds(first, count)
                if block < 2:
                    norm = lax.rsqrt(jnp.sum(value * value, -1, keepdims=True) + EPSILON)
                    if block == 0:
                        qn[g, rows, :] = (value * (norm * HEAD**-0.5)).astype(BF16)
                    else:
                        kn[g, rows, :] = (value * norm).astype(BF16)
                else:
                    vn[2 * g + block - 2, rows, :] = value.astype(BF16)

    convolve(HALO, ROWS - HALO)
    send_halo.wait_recv()
    before = jnp.where(seq > 0, halo_in[...].astype(F32), 0.0)
    ext[0:8, :] = before[HALO - 8 :]
    convolve(0, HALO)

    row = lax.broadcasted_iota(jnp.int32, (HEAD, HEAD), 0)
    col = lax.broadcasted_iota(jnp.int32, (HEAD, HEAD), 1)
    on_lower = col <= row
    below_diag = col < row
    unit = jnp.where(col == row, 1.0, 0.0)
    unit_b = unit.astype(BF16)
    masks = []
    b = 1
    while b < HEAD:
        keep = (lax.div(row, 2 * b) == lax.div(col, 2 * b)) & (lax.div(row, b) != lax.div(col, b)) & below_diag
        masks.append(jnp.where(keep, 1.0, 0.0).astype(BF16))
        b *= 2

    parts = [pl.ds(0, HEAD), pl.ds(HEAD, HEAD)]
    inner = []
    for g in range(GROUPS):
        inner.append(matmul_t(jnp.concatenate([kn[g], qn[g]], 0), kn[g]))
    systems, scores = [], []
    for h in range(VALUE_HEADS):
        g, r = divmod(h, 2)
        lane_b, lane_c = 4 * g + r, 4 * g + 2 + r
        beta = gates[0][:, lane_b : lane_b + 1]
        cum = gates[1][:, lane_c : lane_c + 1]
        cum_t = cumulative_t[lane_c : lane_c + 1, :]
        system, score = {}, {}
        for i, j in ((0, 0), (1, 0), (1, 1)):
            ri, cj = slice(i * HEAD, (i + 1) * HEAD), slice(j * HEAD, (j + 1) * HEAD)
            gap = cum[ri] - cum_t[:, cj]
            if i == j:
                ratio = jnp.where(on_lower, jnp.exp(jnp.where(on_lower, gap, 0.0)), 0.0)
            else:
                ratio = jnp.exp(gap)
            system[i, j] = (beta[ri] * ratio * inner[g][ri, cj]).astype(BF16)
            score[i, j] = (ratio * inner[g][ROWS + i * HEAD : ROWS + (i + 1) * HEAD, cj]).astype(BF16)
        systems.append(system)
        scores.append(score)
    inverses = {(h, i): unit_b - masks[0] * systems[h][i, i] for h in range(VALUE_HEADS) for i in range(2)}
    for mask in masks[1:]:
        halves = {
            key: matmul(mask * systems[key[0]][key[1], key[1]], inverses[key]).astype(BF16) for key in inverses
        }
        inverses = {key: inverses[key] - matmul(inverses[key], halves[key]).astype(BF16) for key in inverses}

    solved = []
    for h in range(VALUE_HEADS):
        g, r = divmod(h, 2)
        lane_b, lane_c = 4 * g + r, 4 * g + 2 + r
        beta = gates[0][:, lane_b : lane_b + 1]
        cum = gates[1][:, lane_c : lane_c + 1]
        right = jnp.concatenate(
            [beta * jnp.exp(cum) * kn[g].astype(F32), beta * vn[h].astype(F32)], 1
        )
        first = matmul(inverses[h, 0], right[:HEAD].astype(BF16)).astype(BF16)
        second = right[HEAD:] - matmul(systems[h][1, 0], first)
        second = matmul(inverses[h, 1], second.astype(BF16)).astype(BF16)
        both = jnp.concatenate([first, second], 0)
        solved.append(both)
        last = cum[ROWS - 1 :, :]
        end_keys = (jnp.exp(last - cum) * kn[g].astype(F32)).astype(BF16)
        grown = lax.dot_general(end_keys, both, (((0,), (0,)), ((), ())), preferred_element_type=F32)
        change = (jnp.exp(last) - 1.0) * unit - grown[:, :HEAD]
        maps[h] = jnp.concatenate([change, grown[:, HEAD:]], 1).astype(BF16)

    def row_device(r):
        return (z * NX + lax.rem(x + r, NX), head)

    row_copies = []
    for r in range(1, NX):
        there = lax.rem(x + r, NX)
        copy = remote(maps.at[there], row_maps.at[x], row_send.at[r - 1], row_recv.at[r - 1], row_device(r))
        copy.start()
        row_copies.append(copy)
    row_maps[pl.ds(x, 1)] = maps[pl.ds(x, 1)]

    for h in range(VALUE_HEADS):
        g, r = divmod(h, 2)
        lane_c = 4 * g + 2 + r
        cum = gates[1][:, lane_c : lane_c + 1]
        top = matmul(scores[h][0, 0], solved[h][:HEAD])
        low = matmul(jnp.concatenate([scores[h][1, 0], scores[h][1, 1]], 1), solved[h])
        out = jnp.concatenate([top, low], 0)
        qeff[h] = (jnp.exp(cum) * qn[g].astype(F32) - out[:, :HEAD]).astype(BF16)
        loc[h] = out[:, HEAD:]

    for r in range(1, NX):
        here = lax.rem(x + NX - r, NX)
        remote(maps.at[0], row_maps.at[here], row_send.at[r - 1], row_recv.at[r - 1], row_device(r)).wait_recv()

    prefix = [row_maps[0].astype(F32)]
    for i in range(1, NX):
        previous = prefix[-1]
        change = row_maps[i]
        prefix.append(previous + change.astype(F32) + matmul(change[:, :HEAD], previous.astype(BF16)))
    row_total[...] = prefix[-1].astype(BF16)

    center = 3 + 4 * c
    is_center = z == center

    def column_device(there):
        return (there * NX + x, head)

    @pl.when(jnp.logical_and(jnp.logical_not(is_center), z != NZ - 1))
    def _():
        remote(
            row_total, all_totals.at[z], tot_send.at[0], tot_recv.at[z], column_device(center)
        ).start()

    @pl.when(is_center)
    def _():
        all_totals[pl.ds(z, 1)] = row_total[...][None]
        fold = jnp.zeros((HEAD, HEAD), F32)
        for k in range(NZ - 1):
            arrival = remote(
                row_total, all_totals.at[k], tot_send.at[0], tot_recv.at[k], column_device(0 * z)
            )
            if k == 3:
                pl.when(c == 1)(arrival.wait_recv)
            else:
                arrival.wait_recv()
            total = all_totals[k]
            if k == 0:
                fold = total[:, HEAD:].astype(F32)
            else:
                fold = (
                    fold + total[:, HEAD:].astype(F32) + matmul(total[:, :HEAD], fold.astype(BF16))
                )
            fold_states[k + 1] = fold.astype(BF16)
            leave = remote(
                fold_states.at[k + 1], state_in, fold_send.at[k + 1], fold_recv, column_device(k + 1)
            )
            if k + 1 == 3:
                pl.when(c == 1)(leave.start)
            elif k + 1 == 7:
                pl.when(c == 0)(leave.start)
            else:
                leave.start()
        state_in[...] = fold_states[pl.ds(z, 1)][0]

    @pl.when(z == 0)
    def _():
        state_in[...] = jnp.zeros_like(state_in)

    @pl.when(jnp.logical_and(jnp.logical_not(is_center), z != 0))
    def _():
        remote(
            fold_states.at[0], state_in, fold_send.at[0], fold_recv, column_device(center)
        ).wait_recv()

    state = state_in[...]
    row_states[0] = state
    for i in range(1, NX):
        before_i = prefix[i - 1]
        row_states[i] = (
            state.astype(F32) + before_i[:, HEAD:] + matmul(before_i[:, :HEAD].astype(BF16), state)
        ).astype(BF16)
    back_copies = []
    for r in range(1, NX):
        there = lax.rem(x + r, NX)
        copy = remote(row_states.at[there], states.at[x], back_send.at[r - 1], back_recv.at[r - 1], row_device(r))
        copy.start()
        back_copies.append(copy)
    states[pl.ds(x, 1)] = row_states[pl.ds(x, 1)]
    for r in range(1, NX):
        here = lax.rem(x + NX - r, NX)
        remote(
            row_states.at[0], states.at[here], back_send.at[r - 1], back_recv.at[r - 1], row_device(r)
        ).wait_recv()

    gain = norm_gain[...].reshape(1, HEAD)
    hidden = []
    for h in range(VALUE_HEADS):
        g, r = divmod(h, 2)
        first = g * GROUP + CONV + r * HEAD
        attended = loc[h] + matmul(qeff[h], states[h])
        back = lax.rsqrt(jnp.mean(attended * attended, -1, keepdims=True) + EPSILON)
        gate = acc[:, first : first + HEAD].astype(BF16).astype(F32)
        hidden.append((attended * back * gain * silu(gate)).astype(BF16))
    hidden = jnp.concatenate(hidden, 1)

    for r in (2, 1, 3, 0):
        slot = SLOT[(r, 1)]
        load_out[slot].wait()
        sib_out[r] = matmul(hidden, w_out[slot]).astype(BF16)
        remote(sib_out.at[r], sib_in.at[r], sib_send.at[r], sib_recv.at[r], sibling).start()
    for r in (2, 1, 3, 0):
        slot = SLOT[(r, 0)]
        load_out[slot].wait()
        own[r] = matmul(hidden, w_out[slot])

    def wait_sibling(r):
        remote(sib_out.at[r], sib_in.at[r], sib_send.at[r], sib_recv.at[r], sibling).wait_recv()

    top, low = pl.ds(0, HALF), pl.ds(HALF, HALF)
    far_up = remote(far_out.at[top], far_in.at[top], ring_send.at[0], ring_recv.at[0], above)
    far_down = remote(far_out.at[low], far_in.at[low], ring_send.at[1], ring_recv.at[1], below)
    up_low = remote(near_out.at[0, low], near_in.at[0, low], ring_send.at[2], ring_recv.at[2], above)
    down_top = remote(near_out.at[1, top], near_in.at[1, top], ring_send.at[3], ring_recv.at[3], below)
    up_top = remote(near_out.at[0, top], near_in.at[0, top], ring_send.at[4], ring_recv.at[4], above)
    down_low = remote(near_out.at[1, low], near_in.at[1, low], ring_send.at[5], ring_recv.at[5], below)
    wait_sibling(2)
    far_out[...] = (own[2] + sib_in[2].astype(F32)).astype(BF16)
    far_up.start()
    far_down.start()
    wait_sibling(1)
    near_out[0, HALF:] = (own[1, HALF:] + sib_in[1, HALF:].astype(F32)).astype(BF16)
    up_low.start()
    wait_sibling(3)
    near_out[1, :HALF] = (own[3, :HALF] + sib_in[3, :HALF].astype(F32)).astype(BF16)
    down_top.start()
    far_up.wait_recv()
    near_out[0, :HALF] = (
        own[1, :HALF] + sib_in[1, :HALF].astype(F32) + far_in[:HALF].astype(F32)
    ).astype(BF16)
    up_top.start()
    far_down.wait_recv()
    near_out[1, HALF:] = (
        own[3, HALF:] + sib_in[3, HALF:].astype(F32) + far_in[HALF:].astype(F32)
    ).astype(BF16)
    down_low.start()
    wait_sibling(0)
    mine = own[0] + sib_in[0].astype(F32)
    for copy in (up_low, down_top, up_top, down_low):
        copy.wait_recv()
    out_ref[...] = (mine + near_in[0].astype(F32) + near_in[1].astype(F32)).astype(BF16)

    send_halo.wait_send()
    for copy in row_copies + back_copies:
        copy.wait_send()

    @pl.when(jnp.logical_and(jnp.logical_not(is_center), z != NZ - 1))
    def _():
        remote(
            row_total, all_totals.at[z], tot_send.at[0], tot_recv.at[z], column_device(center)
        ).wait_send()

    @pl.when(is_center)
    def _():
        for k in range(1, NZ):
            leave = remote(fold_states.at[k], state_in, fold_send.at[k], fold_recv, column_device(k))
            if k == 3:
                pl.when(c == 1)(leave.wait_send)
            elif k == 7:
                pl.when(c == 0)(leave.wait_send)
            else:
                leave.wait_send()

    for r in range(NY):
        remote(sib_out.at[r], sib_in.at[r], sib_send.at[r], sib_recv.at[r], sibling).wait_send()
    for copy in (far_up, far_down, up_low, down_top, up_top, down_low):
        copy.wait_send()


def per_device(*args):
    anywhere = pl.BlockSpec(memory_space=pl.ANY)
    vmem = pl.BlockSpec(memory_space=pltpu.VMEM)
    smem = pl.BlockSpec(memory_space=pltpu.SMEM)
    dma = pltpu.SemaphoreType.DMA
    return pl.pallas_call(
        kernel,
        out_shape=jax.ShapeDtypeStruct((ROWS, FEATURES), BF16),
        in_specs=[anywhere, anywhere, vmem, vmem, smem, smem, smem, vmem, anywhere],
        out_specs=vmem,
        scratch_shapes=[
            pltpu.VMEM((ROWS, 8 * FEATURES), BF16),
            pltpu.VMEM((8 * FEATURES, GROUPS * GROUP), BF16),
            pltpu.VMEM((8, VALUE_HEADS * HEAD, FEATURES), BF16),
            pltpu.VMEM((ROWS, GROUPS * GROUP), F32),
            pltpu.VMEM((8 + ROWS, GROUPS * CONV), F32),
            pltpu.VMEM((HALO, GROUPS * CONV), BF16),
            pltpu.VMEM((HALO, GROUPS * CONV), BF16),
            pltpu.VMEM((2, ROWS, HEAD), F32),
            pltpu.VMEM((GROUPS, ROWS, HEAD), BF16),
            pltpu.VMEM((GROUPS, ROWS, HEAD), BF16),
            pltpu.VMEM((VALUE_HEADS, ROWS, HEAD), BF16),
            pltpu.VMEM((VALUE_HEADS, HEAD, 2 * HEAD), BF16),
            pltpu.VMEM((NX, HEAD, 2 * HEAD), BF16),
            pltpu.VMEM((HEAD, 2 * HEAD), BF16),
            pltpu.VMEM((NZ, HEAD, 2 * HEAD), BF16),
            pltpu.VMEM((NZ, HEAD, HEAD), BF16),
            pltpu.VMEM((HEAD, HEAD), BF16),
            pltpu.VMEM((NX, HEAD, HEAD), BF16),
            pltpu.VMEM((VALUE_HEADS, HEAD, HEAD), BF16),
            pltpu.VMEM((VALUE_HEADS, ROWS, HEAD), F32),
            pltpu.VMEM((VALUE_HEADS, ROWS, HEAD), BF16),
            pltpu.VMEM((NY, ROWS, FEATURES), F32),
            pltpu.VMEM((NY, ROWS, FEATURES), BF16),
            pltpu.VMEM((NY, ROWS, FEATURES), BF16),
            pltpu.VMEM((ROWS, FEATURES), BF16),
            pltpu.VMEM((ROWS, FEATURES), BF16),
            pltpu.VMEM((2, ROWS, FEATURES), BF16),
            pltpu.VMEM((2, ROWS, FEATURES), BF16),
            dma,
            dma((8,)),
            dma((8,)),
            dma((14,)),
            dma((16,)),
            dma((2,)),
            dma((NX - 1,)),
            dma((NX - 1,)),
            dma((1,)),
            dma((NZ,)),
            dma((NZ,)),
            dma,
            dma((NX - 1,)),
            dma((NX - 1,)),
            dma((NY,)),
            dma((NY,)),
            dma((6,)),
            dma((6,)),
        ],
        compiler_params=pltpu.CompilerParams(
            collective_id=0, has_side_effects=True, vmem_limit_bytes=48 * 1024 * 1024
        ),
    )(*args)


def solution(mesh):
    in_specs = (
        P("seq", "head"),
        P(None, "head"),
        P(None, "head"),
        P(None, "head", None),
        P("head"),
        P("head"),
        P("head"),
        P(),
        P("head", None),
    )
    out_specs = P("seq", "head")
    return jax.shard_map(
        per_device, mesh=mesh, in_specs=in_specs, out_specs=out_specs, check_vma=False
    )
```

```python
import functools

import jax
import jax.numpy as jnp
from jax import lax
from jax.experimental import pallas as pl
from jax.experimental.pallas import tpu as pltpu
from jax.sharding import PartitionSpec as P

F32 = jnp.float32
BF16 = jnp.bfloat16
EPSILON = 1e-06

ROWS = 256
HEAD = 128
FEATURES = 256
GROUPS = 2
VALUE_HEADS = 4
TILES = 6
CONV = 512
GROUP = 768
HALO = 16
NX = 4
NZ = 8
QUAD = 4
NY = 4

ORDER = ((0, 0), (0, 1), (1, 0), (1, 1), (3, 0), (3, 1), (2, 0), (2, 1))
SLOT = {pair: slot for slot, pair in enumerate(ORDER)}


def matmul(a, b):
    return jnp.dot(a, b, preferred_element_type=F32)


def matmul_t(a, b):
    return lax.dot_general(a, b, (((1,), (1,)), ((), ())), preferred_element_type=F32)


def silu(v):
    return 0.5 * v * (1.0 + jnp.tanh(0.5 * v))


def kernel(
    tokens_hbm,
    in_weight_hbm,
    gate_weight_hbm,
    conv_weight_hbm,
    decay_scale_hbm,
    dt_bias_hbm,
    beta_shift_hbm,
    norm_gain_hbm,
    out_weight_hbm,
    out_ref,
    gate_weight,
    conv_weight,
    decay_scale,
    dt_bias,
    beta_shift,
    norm_gain,
    tok,
    w_in,
    w_out,
    acc,
    ext,
    halo_out,
    halo_in,
    gates,
    qn,
    kn,
    vn,
    maps,
    row_maps,
    row_total,
    totals_in,
    state_in,
    state_out,
    state_before,
    out_gate,
    row_states,
    states,
    loc,
    qeff,
    own,
    sib_out,
    sib_in,
    ring_out,
    ring_in,
    load_sem,
    small_sem,
    win_sem,
    wout_sem,
    tok_send,
    tok_recv,
    halo_sem,
    row_send,
    row_recv,
    total_send,
    total_recv,
    state_send,
    state_recv,
    ready_sem,
    halo_ready_sem,
    back_send,
    back_recv,
    sib_send,
    sib_recv,
    ring_send,
    ring_recv,
):
    seq = lax.axis_index("seq")
    head = lax.axis_index("head")
    z, x = lax.div(seq, NX), lax.rem(seq, NX)
    y, c = lax.div(head, 2), lax.rem(head, 2)

    def head_at(r, other):
        core = c if other == 0 else 1 - c
        return lax.rem(y + r, NY) * 2 + core

    above = (seq, head_at(1, 0))
    below = (seq, head_at(3, 0))
    across = (seq, head_at(2, 0))
    sibling = (seq, head_at(0, 1))

    def remote(src, dst, send, recv, device):
        return pltpu.make_async_remote_copy(
            src_ref=src,
            dst_ref=dst,
            send_sem=send,
            recv_sem=recv,
            device_id=device,
            device_id_type=pl.DeviceIdType.MESH,
        )

    load_tok = pltpu.make_async_copy(tokens_hbm, tok.at[0], load_sem)
    load_tok.start()
    load_in = []
    for slot, (r, other) in enumerate(ORDER):
        rows = pl.ds(pl.multiple_of(head_at(r, other) * FEATURES, FEATURES), FEATURES)
        copy = pltpu.make_async_copy(
            in_weight_hbm.at[rows], w_in.at[pl.ds(slot * FEATURES, FEATURES)], win_sem.at[slot]
        )
        copy.start()
        load_in.append(copy)
    load_out = []
    for slot, (r, other) in enumerate(ORDER):
        columns = pl.ds(pl.multiple_of(head_at(r, other) * FEATURES, FEATURES), FEATURES)
        copy = pltpu.make_async_copy(out_weight_hbm.at[:, columns], w_out.at[slot], wout_sem.at[slot])
        copy.start()
        load_out.append(copy)

    load_small = []
    for i, (source, target) in enumerate(
        (
            (gate_weight_hbm, gate_weight),
            (conv_weight_hbm, conv_weight),
            (decay_scale_hbm, decay_scale),
            (dt_bias_hbm, dt_bias),
            (beta_shift_hbm, beta_shift),
            (norm_gain_hbm, norm_gain),
        )
    ):
        copy = pltpu.make_async_copy(source, target, small_sem.at[i])
        copy.start()
        load_small.append(copy)

    barrier = pltpu.get_barrier_semaphore()
    def row_device(r):
        return (z * NX + lax.rem(x + r, NX), head)

    def column_device(there):
        return (there * NX + x, head)

    def signal(semaphore, device):
        pl.semaphore_signal(semaphore, inc=1, device_id=device, device_id_type=pl.DeviceIdType.MESH)

    place = lax.rem(z, QUAD)
    upper = z >= QUAD
    base_row = z == QUAD - 1
    last_x = x == NX - 1
    not_top = z < NZ - 1
    next_row = ((z + 1) * NX, head)
    for device in [above, below, across, sibling] + [row_device(r) for r in range(1, NX)]:
        signal(barrier, device)

    for d in range(1, QUAD):
        pl.when(place + d < QUAD)(functools.partial(signal, barrier, column_device(z + d)))
    for d in range(1, QUAD + 1):
        pl.when(base_row)(functools.partial(signal, barrier, column_device(z + d)))

    @pl.when(jnp.logical_and(last_x, not_top))
    def _():
        signal(barrier, next_row)

    greeted = 7 + place + jnp.where(upper, 1, 0)
    greeted = greeted + jnp.where(jnp.logical_and(x == 0, z > 0), 1, 0)
    pl.semaphore_wait(barrier, greeted)

    for d in range(1, QUAD):
        pl.when(place >= d)(functools.partial(signal, ready_sem, column_device(z - d)))
    pl.when(upper)(functools.partial(signal, ready_sem, column_device(QUAD - 1)))

    @pl.when(jnp.logical_and(x == 0, z > 0))
    def _():
        signal(halo_ready_sem, ((z - 1) * NX + NX - 1, head))

    load_tok.wait()

    pending = []

    def finish():
        for wait in pending:
            wait()

    sends = []

    def send_tok(source, target, device):
        copy = remote(tok.at[source], tok.at[target], tok_send.at[len(sends)], tok_recv.at[target], device)
        copy.start()
        sends.append(copy)

    def wait_tok(slot):
        remote(tok.at[slot], tok.at[slot], tok_send.at[0], tok_recv.at[slot], sibling).wait_recv()

    up, down, far = SLOT[(1, 0)], SLOT[(3, 0)], SLOT[(2, 0)]
    send_tok(0, down, above)
    send_tok(0, up, below)
    send_tok(0, 1, sibling)
    send_tok(0, far, across)

    def tokens_of(first, count):
        return jnp.concatenate([tok[slot] for slot in range(first, first + count)], 1)

    def project(first, count, start):
        rows = pl.ds(first * FEATURES, count * FEATURES)

        def tile(j, carry):
            columns = pl.ds(pl.multiple_of(j * 256, 256), 256)
            part = matmul(tokens_of(first, count), w_in[rows, columns])
            if start:
                acc[j] = part
            else:
                acc[j] += part
            return carry

        lax.fori_loop(0, TILES, tile, 0)

    wait_tok(1)
    load_in[0].wait()
    load_in[1].wait()
    project(0, 2, True)
    for slot in (up, down):
        wait_tok(slot)
        send_tok(slot, slot + 1, sibling)
    for slot in range(2, 6):
        load_in[slot].wait()
    wait_tok(up + 1)
    wait_tok(down + 1)
    project(2, 4, False)
    wait_tok(far)
    send_tok(far, far + 1, sibling)
    wait_tok(far + 1)
    load_in[6].wait()
    load_in[7].wait()
    pending.extend(copy.wait_send for copy in sends)

    for g in range(GROUPS):
        for i in range(2):
            j = 3 * g + i
            weight = w_in[6 * FEATURES :, j * 256 : (j + 1) * 256]
            part = (acc[j] + matmul(tokens_of(6, 2), weight)).astype(BF16)
            first = 4 * g + 2 * i
            for block in range(2):
                columns = part[:, block * HEAD : (block + 1) * HEAD]
                halo_out[:, (first + block) * HEAD : (first + block + 1) * HEAD] = columns[ROWS - HALO :]
                ext[first + block, 8:, :] = columns.astype(F32)

    next_seq = lax.rem(seq + 1, NX * NZ)
    send_halo = remote(halo_out, halo_in, halo_sem.at[0], halo_sem.at[1], (next_seq, head))

    @pl.when(jnp.logical_and(last_x, not_top))
    def _():
        pl.semaphore_wait(halo_ready_sem, 1)

    pl.when(seq < NX * NZ - 1)(send_halo.start)
    pending.append(lambda: pl.when(seq < NX * NZ - 1)(send_halo.wait_send))

    for copy in load_small:
        copy.wait()
    gating = jnp.zeros((ROWS, HEAD), F32)
    for slot, (r, other) in enumerate(ORDER):
        columns = pl.ds(pl.multiple_of(head_at(r, other) * FEATURES, FEATURES), FEATURES)
        weight = gate_weight[:, columns]
        weight = jnp.concatenate([weight, jnp.zeros((HEAD - weight.shape[0], FEATURES), BF16)], 0)
        gating = gating + matmul_t(tok[slot], weight)
    lane = lax.broadcasted_iota(jnp.int32, (1, HEAD), 1)
    shift = jnp.zeros((1, HEAD), F32)
    bias = jnp.zeros((1, HEAD), F32)
    scale = jnp.zeros((1, HEAD), F32)
    for h in range(VALUE_HEADS):
        g, r = divmod(h, 2)
        shift = jnp.where(lane == 4 * g + r, beta_shift[h], shift)
        bias = jnp.where(lane == 4 * g + 2 + r, dt_bias[h], bias)
        scale = jnp.where(lane == 4 * g + 2 + r, decay_scale[h], scale)
    strength = jax.nn.sigmoid(gating - shift)
    shifted = gating + bias
    softplus = jnp.maximum(shifted, 0.0) + jnp.log1p(jnp.exp(-jnp.abs(shifted)))
    log_gate = -scale * softplus
    row_id = lax.broadcasted_iota(jnp.int32, (ROWS, ROWS), 0)
    col_id = lax.broadcasted_iota(jnp.int32, (ROWS, ROWS), 1)
    ones = jnp.where(col_id <= row_id, 1.0, 0.0).astype(BF16)
    cumulative = jnp.zeros((ROWS, HEAD), F32)
    rest = log_gate
    for _ in range(3):
        piece = rest.astype(BF16)
        cumulative = cumulative + matmul(ones, piece)
        rest = rest - piece.astype(F32)
    cumulative_t = jnp.transpose(cumulative)
    gates[0] = strength
    gates[1] = cumulative

    def convolve(first, count):
        for g in range(GROUPS):
            for block in range(CONV // HEAD):
                total = jnp.zeros((count, HEAD), F32)
                for tap in range(4):
                    weight = conv_weight[tap, g : g + 1, block * HEAD : (block + 1) * HEAD].astype(F32)
                    total = total + weight * ext[4 * g + block, pl.ds(first + 5 + tap, count), :]
                value = silu(total)
                rows = pl.ds(first, count)
                if block < 2:
                    norm = lax.rsqrt(jnp.sum(value * value, -1, keepdims=True) + EPSILON)
                    if block == 0:
                        qn[g, rows, :] = (value * (norm * HEAD**-0.5)).astype(BF16)
                    else:
                        kn[g, rows, :] = (value * norm).astype(BF16)
                else:
                    vn[2 * g + block - 2, rows, :] = value.astype(BF16)

    convolve(HALO, ROWS - HALO)
    pl.when(seq > 0)(send_halo.wait_recv)

    @pl.when(seq == 0)
    def _():
        halo_in[...] = jnp.zeros_like(halo_in)

    for block in range(8):
        ext[block, 0:8, :] = halo_in[:, block * HEAD : (block + 1) * HEAD].astype(F32)[HALO - 8 :]
    convolve(0, HALO)

    row = lax.broadcasted_iota(jnp.int32, (HEAD, HEAD), 0)
    col = lax.broadcasted_iota(jnp.int32, (HEAD, HEAD), 1)
    on_lower = col <= row
    below_diag = col < row
    unit = jnp.where(col == row, 1.0, 0.0)
    unit_b = unit.astype(BF16)
    masks = []
    b = 1
    while b < HEAD:
        keep = (lax.div(row, 2 * b) == lax.div(col, 2 * b)) & (lax.div(row, b) != lax.div(col, b)) & below_diag
        masks.append(jnp.where(keep, 1.0, 0.0).astype(BF16))
        b *= 2

    parts = [pl.ds(0, HEAD), pl.ds(HEAD, HEAD)]
    inner = []
    for g in range(GROUPS):
        inner.append(matmul_t(jnp.concatenate([kn[g], qn[g]], 0), kn[g]))
    systems, scores = [], []
    for h in range(VALUE_HEADS):
        g, r = divmod(h, 2)
        lane_b, lane_c = 4 * g + r, 4 * g + 2 + r
        beta = gates[0][:, lane_b : lane_b + 1]
        cum = gates[1][:, lane_c : lane_c + 1]
        cum_t = cumulative_t[lane_c : lane_c + 1, :]
        system, score = {}, {}
        for i, j in ((0, 0), (1, 0), (1, 1)):
            ri, cj = slice(i * HEAD, (i + 1) * HEAD), slice(j * HEAD, (j + 1) * HEAD)
            gap = cum[ri] - cum_t[:, cj]
            if i == j:
                ratio = jnp.where(on_lower, jnp.exp(jnp.where(on_lower, gap, 0.0)), 0.0)
            else:
                ratio = jnp.exp(gap)
            system[i, j] = (beta[ri] * ratio * inner[g][ri, cj]).astype(BF16)
            score[i, j] = (ratio * inner[g][ROWS + i * HEAD : ROWS + (i + 1) * HEAD, cj]).astype(BF16)
        systems.append(system)
        scores.append(score)
    inverses = {(h, i): unit_b - masks[0] * systems[h][i, i] for h in range(VALUE_HEADS) for i in range(2)}
    for mask in masks[1:]:
        halves = {
            key: matmul(mask * systems[key[0]][key[1], key[1]], inverses[key]).astype(BF16) for key in inverses
        }
        inverses = {key: inverses[key] - matmul(inverses[key], halves[key]).astype(BF16) for key in inverses}

    solved = []
    for h in range(VALUE_HEADS):
        g, r = divmod(h, 2)
        lane_b, lane_c = 4 * g + r, 4 * g + 2 + r
        beta = gates[0][:, lane_b : lane_b + 1]
        cum = gates[1][:, lane_c : lane_c + 1]
        right = jnp.concatenate(
            [beta * jnp.exp(cum) * kn[g].astype(F32), beta * vn[h].astype(F32)], 1
        )
        first = matmul(inverses[h, 0], right[:HEAD].astype(BF16)).astype(BF16)
        second = right[HEAD:] - matmul(systems[h][1, 0], first)
        second = matmul(inverses[h, 1], second.astype(BF16)).astype(BF16)
        both = jnp.concatenate([first, second], 0)
        solved.append(both)
        last = cum[ROWS - 1 :, :]
        end_keys = (jnp.exp(last - cum) * kn[g].astype(F32)).astype(BF16)
        grown = lax.dot_general(end_keys, both, (((0,), (0,)), ((), ())), preferred_element_type=F32)
        change = (jnp.exp(last) - 1.0) * unit - grown[:, :HEAD]
        maps[h] = jnp.concatenate([change, grown[:, HEAD:]], 1).astype(BF16)
        row_copy = remote(
            maps.at[h], row_maps.at[x], row_send.at[h], row_recv.at[x], (z * NX + h, head)
        )
        pl.when(x != h)(row_copy.start)
        pending.append(functools.partial(pl.when(x != h), row_copy.wait_send))

        @pl.when(x == h)
        def _():
            row_maps[h] = maps[h]


    for h in range(VALUE_HEADS):
        g, r = divmod(h, 2)
        lane_c = 4 * g + 2 + r
        cum = gates[1][:, lane_c : lane_c + 1]
        top = matmul(scores[h][0, 0], solved[h][:HEAD])
        low = matmul(jnp.concatenate([scores[h][1, 0], scores[h][1, 1]], 1), solved[h])
        out = jnp.concatenate([top, low], 0)
        qeff[h] = (jnp.exp(cum) * qn[g].astype(F32) - out[:, :HEAD]).astype(BF16)
        loc[h] = out[:, HEAD:]

    for g in range(GROUPS):
        j = 3 * g + 2
        part = acc[j] + matmul(tokens_of(6, 2), w_in[6 * FEATURES :, j * 256 : (j + 1) * 256])
        gate = part.astype(BF16).astype(F32)
        out_gate[g] = silu(gate)

    for i in range(NX):
        row_copy = remote(maps.at[0], row_maps.at[i], row_send.at[0], row_recv.at[i], row_device(1))
        pl.when(x != i)(row_copy.wait_recv)

    prefix = [row_maps[0].astype(F32)]
    for i in range(1, NX):
        previous = prefix[-1]
        change = row_maps[i]
        prefix.append(previous + change.astype(F32) + matmul(change[:, :HEAD], previous.astype(BF16)))
    total = prefix[-1].astype(BF16)
    row_total[0] = total[:, :HEAD]
    row_total[1] = total[:, HEAD:]

    def apply(change, shift, before):
        return before + shift.astype(F32) + matmul(change, before.astype(BF16))

    def total_copy(d):
        return remote(
            row_total, totals_in.at[place], total_send.at[d - 1], total_recv.at[place], column_device(z + d)
        )

    def shift_copy(d):
        return remote(
            row_total.at[1], totals_in.at[0, 1], total_send.at[d - 1], total_recv.at[0], column_device(d)
        )

    def arrived(k):
        return remote(
            row_total, totals_in.at[k], total_send.at[0], total_recv.at[k], column_device(z)
        )

    def state_copy(d):
        return remote(
            state_out, state_in, state_send.at[d - 1], state_recv, column_device(z + d)
        )

    sends_total = {d: jnp.logical_and(place + d < QUAD, z > 0) for d in range(1, QUAD)}

    @pl.when(place < QUAD - 1)
    def _():
        pl.semaphore_wait(ready_sem, QUAD - 1 - place)

    for d in reversed(range(1, QUAD)):
        pl.when(z == 0)(shift_copy(d).start)
        pl.when(sends_total[d])(total_copy(d).start)
        pending.append(functools.partial(pl.when(z == 0), shift_copy(d).wait_send))
        pending.append(functools.partial(pl.when(sends_total[d]), total_copy(d).wait_send))

    def advance(k):
        arrived(k).wait_recv()
        state_before[...] = apply(totals_in[k, 0], totals_in[k, 1], state_before[...])

    @pl.when(z == 0)
    def _():
        state_before[...] = jnp.zeros_like(state_before)

    @pl.when(jnp.logical_and(z > 0, z < QUAD))
    def _():
        shift_copy(1).wait_recv()
        state_before[...] = totals_in[0, 1].astype(F32)
        for k in range(1, QUAD - 1):
            pl.when(place > k)(functools.partial(advance, k))

    @pl.when(base_row)
    def _():
        state_out[...] = apply(row_total[0], row_total[1], state_before[...]).astype(BF16)
        pl.semaphore_wait(ready_sem, QUAD)
        for d in range(1, QUAD + 1):
            state_copy(d).start()

    @pl.when(upper)
    def _():
        state_copy(1).wait_recv()
        state_before[...] = state_in[...].astype(F32)
        for k in range(QUAD - 1):
            pl.when(place > k)(functools.partial(advance, k))

    for d in range(1, QUAD + 1):
        pending.append(functools.partial(pl.when(base_row), state_copy(d).wait_send))
    state = state_before[...]
    row_states[0] = state.astype(BF16)
    for i in range(1, NX):
        before_i = prefix[i - 1]
        row_states[i] = apply(before_i[:, :HEAD].astype(BF16), before_i[:, HEAD:], state).astype(BF16)
    for r in range(1, NX):
        there = lax.rem(x + r, NX)
        copy = remote(row_states.at[there], states.at[x], back_send.at[r - 1], back_recv.at[r - 1], row_device(r))
        copy.start()
        pending.append(copy.wait_send)
    states[pl.ds(x, 1)] = row_states[pl.ds(x, 1)]
    for r in range(1, NX):
        here = lax.rem(x + NX - r, NX)
        remote(
            row_states.at[0], states.at[here], back_send.at[r - 1], back_recv.at[r - 1], row_device(r)
        ).wait_recv()

    gain = norm_gain[...]
    hidden = []
    for h in range(VALUE_HEADS):
        g, r = divmod(h, 2)
        attended = loc[h] + matmul(qeff[h], states[h])
        back = lax.rsqrt(jnp.mean(attended * attended, -1, keepdims=True) + EPSILON)
        gate = out_gate[g, :, r * HEAD : (r + 1) * HEAD]
        hidden.append((attended * back * gain * gate).astype(BF16))
    hidden = jnp.concatenate(hidden, 1)

    for r in (2, 1, 3, 0):
        slot = SLOT[(r, 1)]
        load_out[slot].wait()
        sib_out[r] = matmul(hidden, w_out[slot]).astype(BF16)
        remote(sib_out.at[r], sib_in.at[r], sib_send.at[r], sib_recv.at[r], sibling).start()
    for r in (2, 1, 3, 0):
        slot = SLOT[(r, 0)]
        load_out[slot].wait()
        own[r] = matmul(hidden, w_out[slot])

    def wait_sibling(r):
        remote(sib_out.at[r], sib_in.at[r], sib_send.at[r], sib_recv.at[r], sibling).wait_recv()

    ring = {
        r: remote(ring_out.at[r - 1], ring_in.at[r - 1], ring_send.at[r - 1], ring_recv.at[r - 1], device)
        for r, device in ((1, above), (2, across), (3, below))
    }
    for r in (2, 1, 3):
        wait_sibling(r)
        ring_out[r - 1] = (own[r] + sib_in[r].astype(F32)).astype(BF16)
        ring[r].start()
    wait_sibling(0)
    total = own[0] + sib_in[0].astype(F32)
    for r in (1, 3, 2):
        ring[r].wait_recv()
        total = total + ring_in[r - 1].astype(F32)
    out_ref[...] = total.astype(BF16)

    finish()
    for r in range(NY):
        remote(sib_out.at[r], sib_in.at[r], sib_send.at[r], sib_recv.at[r], sibling).wait_send()
    for copy in ring.values():
        copy.wait_send()


def per_device(
    tokens,
    in_weight,
    gate_weight,
    conv_weight,
    decay_scale,
    dt_bias,
    beta_shift,
    norm_gain,
    out_weight,
):
    anywhere = pl.BlockSpec(memory_space=pltpu.HBM)
    vmem = pl.BlockSpec(memory_space=pltpu.VMEM)
    dma = pltpu.SemaphoreType.DMA
    return pl.pallas_call(
        kernel,
        out_shape=jax.ShapeDtypeStruct((ROWS, FEATURES), BF16),
        in_specs=[anywhere] * 9,
        out_specs=vmem,
        scratch_shapes=[
            pltpu.VMEM((2 * VALUE_HEADS, 8 * FEATURES), BF16),
            pltpu.VMEM((4, GROUPS, CONV), BF16),
            pltpu.SMEM((VALUE_HEADS,), F32),
            pltpu.SMEM((VALUE_HEADS,), F32),
            pltpu.SMEM((VALUE_HEADS,), F32),
            pltpu.VMEM((1, HEAD), F32),
            pltpu.VMEM((8, ROWS, FEATURES), BF16),
            pltpu.VMEM((8 * FEATURES, GROUPS * GROUP), BF16),
            pltpu.VMEM((8, VALUE_HEADS * HEAD, FEATURES), BF16),
            pltpu.VMEM((TILES, ROWS, 256), F32),
            pltpu.VMEM((8, 8 + ROWS, HEAD), F32),
            pltpu.VMEM((HALO, GROUPS * CONV), BF16),
            pltpu.VMEM((HALO, GROUPS * CONV), BF16),
            pltpu.VMEM((2, ROWS, HEAD), F32),
            pltpu.VMEM((GROUPS, ROWS, HEAD), BF16),
            pltpu.VMEM((GROUPS, ROWS, HEAD), BF16),
            pltpu.VMEM((VALUE_HEADS, ROWS, HEAD), BF16),
            pltpu.VMEM((VALUE_HEADS, HEAD, 2 * HEAD), BF16),
            pltpu.VMEM((NX, HEAD, 2 * HEAD), BF16),
            pltpu.VMEM((2, HEAD, HEAD), BF16),
            pltpu.VMEM((QUAD - 1, 2, HEAD, HEAD), BF16),
            pltpu.VMEM((HEAD, HEAD), BF16),
            pltpu.VMEM((HEAD, HEAD), BF16),
            pltpu.VMEM((HEAD, HEAD), F32),
            pltpu.VMEM((GROUPS, ROWS, 2 * HEAD), F32),
            pltpu.VMEM((NX, HEAD, HEAD), BF16),
            pltpu.VMEM((VALUE_HEADS, HEAD, HEAD), BF16),
            pltpu.VMEM((VALUE_HEADS, ROWS, HEAD), F32),
            pltpu.VMEM((VALUE_HEADS, ROWS, HEAD), BF16),
            pltpu.VMEM((NY, ROWS, FEATURES), F32),
            pltpu.VMEM((NY, ROWS, FEATURES), BF16),
            pltpu.VMEM((NY, ROWS, FEATURES), BF16),
            pltpu.VMEM((NY - 1, ROWS, FEATURES), BF16),
            pltpu.VMEM((NY - 1, ROWS, FEATURES), BF16),
            dma,
            dma((6,)),
            dma((8,)),
            dma((8,)),
            dma((7,)),
            dma((8,)),
            dma((2,)),
            dma((NX,)),
            dma((NX,)),
            dma((QUAD - 1,)),
            dma((QUAD - 1,)),
            dma((QUAD,)),
            dma,
            pltpu.SemaphoreType.REGULAR,
            pltpu.SemaphoreType.REGULAR,
            dma((NX - 1,)),
            dma((NX - 1,)),
            dma((NY,)),
            dma((NY,)),
            dma((NY - 1,)),
            dma((NY - 1,)),
        ],
        compiler_params=pltpu.CompilerParams(
            collective_id=0, has_side_effects=True, vmem_limit_bytes=60 * 1024 * 1024
        ),
    )(
        tokens,
        in_weight,
        gate_weight.T,
        conv_weight,
        decay_scale,
        dt_bias,
        beta_shift,
        norm_gain.reshape(1, HEAD),
        out_weight,
    )


def solution(mesh):
    in_specs = (
        P("seq", "head"),
        P(None, "head"),
        P(None, "head"),
        P(None, "head", None),
        P("head"),
        P("head"),
        P("head"),
        P(),
        P("head", None),
    )
    out_specs = P("seq", "head")
    return jax.shard_map(
        per_device, mesh=mesh, in_specs=in_specs, out_specs=out_specs, check_vma=False
    )
```

```python
import functools

import jax
import jax.numpy as jnp
from jax import lax
from jax.experimental import pallas as pl
from jax.experimental.pallas import tpu as pltpu
from jax.sharding import PartitionSpec as P

F32 = jnp.float32
BF16 = jnp.bfloat16
EPSILON = 1e-06

ROWS = 256
HEAD = 128
FEATURES = 256
GROUPS = 2
VALUE_HEADS = 4
BLOCKS = ((0, 0), (1, 0), (1, 1))
TILES = 6
CONV = 512
GROUP = 768
HALO = 16
NX = 4
NZ = 8
NY = 4

CHIPS = (0, 1, 3, 2)


def matmul(a, b):
    return jnp.dot(a, b, preferred_element_type=F32)


def matmul_t(a, b):
    return lax.dot_general(a, b, (((1,), (1,)), ((), ())), preferred_element_type=F32)


def silu(v):
    return 0.5 * v * (1.0 + jnp.tanh(0.5 * v))


def kernel(
    tokens_hbm,
    in_weight_hbm,
    gate_weight_hbm,
    conv_weight_hbm,
    decay_scale_hbm,
    dt_bias_hbm,
    beta_shift_hbm,
    norm_gain_hbm,
    out_weight_hbm,
    out_ref,
    gate_weight,
    conv_weight,
    decay_scale,
    dt_bias,
    beta_shift,
    norm_gain,
    tok,
    w_in,
    w_out,
    acc,
    ext,
    halo_out,
    halo_in,
    gates,
    qn,
    kn,
    vn,
    maps,
    row_maps,
    prefix,
    row_total,
    total_in,
    pair_in,
    pair_out,
    state_in,
    state_out,
    state_before,
    out_gate,
    decays,
    row_states,
    states,
    loc,
    qeff,
    sib_out,
    sib_in,
    ring_out,
    ring_in,
    load_sem,
    small_sem,
    win_sem,
    wout_sem,
    tok_send,
    tok_recv,
    halo_sem,
    row_send,
    row_recv,
    total_send,
    total_recv,
    pair_send,
    pair_recv,
    state_send,
    state_recv,
    ready_sem,
    halo_ready_sem,
    back_send,
    back_recv,
    sib_send,
    sib_recv,
    ring_send,
    ring_recv,
):
    seq = lax.axis_index("seq")
    head = lax.axis_index("head")
    z, x = lax.div(seq, NX), lax.rem(seq, NX)
    y, c = lax.div(head, 2), lax.rem(head, 2)

    def chip_at(r):
        return lax.rem(y + r, NY)

    above = (seq, chip_at(1) * 2 + c)
    below = (seq, chip_at(3) * 2 + c)
    across = (seq, chip_at(2) * 2 + c)
    sibling = (seq, y * 2 + 1 - c)

    def remote(src, dst, send, recv, device):
        return pltpu.make_async_remote_copy(
            src_ref=src,
            dst_ref=dst,
            send_sem=send,
            recv_sem=recv,
            device_id=device,
            device_id_type=pl.DeviceIdType.MESH,
        )

    load_tok = pltpu.make_async_copy(tokens_hbm, tok.at[0, c], load_sem)
    load_tok.start()

    barrier = pltpu.get_barrier_semaphore()
    owner = c == 1

    def row_device(r, core):
        return (z * NX + lax.rem(x + r, NX), y * 2 + core)

    def column_device(there):
        return (there * NX + x, head)

    def signal(semaphore, device):
        pl.semaphore_signal(semaphore, inc=1, device_id=device, device_id_type=pl.DeviceIdType.MESH)

    odd = lax.rem(z, 2) == 1
    even = jnp.logical_not(odd)
    both_of = jnp.logical_and
    last_x = x == NX - 1
    not_top = z < NZ - 1
    next_row = ((z + 1) * NX, head)
    for device in [above, below, across, sibling] + [row_device(r, 1) for r in range(1, NX)]:
        signal(barrier, device)
    for r in range(1, NX):
        pl.when(owner)(functools.partial(signal, barrier, row_device(r, 0)))

    pl.when(both_of(owner, even))(functools.partial(signal, barrier, column_device(z + 1)))
    for d in (1, 2):
        pl.when(both_of(owner, both_of(odd, not_top)))(functools.partial(signal, barrier, column_device(z + d)))
    pl.when(both_of(owner, z == 4))(functools.partial(signal, barrier, column_device(z + 2)))
    for d in (3, 4):
        pl.when(both_of(owner, z == 3))(functools.partial(signal, barrier, column_device(z + d)))

    @pl.when(jnp.logical_and(last_x, not_top))
    def _():
        signal(barrier, next_row)

    def pair_of(r):
        return pl.ds(pl.multiple_of(chip_at(r) * 2 * FEATURES, 2 * FEATURES), 2 * FEATURES)

    load_in, load_out, load_small = [], [], []
    for i, r in enumerate(CHIPS):
        load_in.append(pltpu.make_async_copy(in_weight_hbm.at[pair_of(r)], w_in.at[i], win_sem.at[i]))
        load_out.append(
            pltpu.make_async_copy(out_weight_hbm.at[:, pair_of(r)], w_out.at[i], wout_sem.at[i])
        )
    for i, (source, target) in enumerate(
        (
            (gate_weight_hbm, gate_weight),
            (conv_weight_hbm, conv_weight),
            (decay_scale_hbm, decay_scale),
            (dt_bias_hbm, dt_bias),
            (beta_shift_hbm, beta_shift),
            (norm_gain_hbm, norm_gain),
        )
    ):
        load_small.append(pltpu.make_async_copy(source, target, small_sem.at[i]))
    for copy in load_in:
        copy.start()

    greeted = 7 + jnp.where(owner, 3 + lax.rem(z, 2) + jnp.where(z >= 2, 1, 0) + jnp.where(z >= 6, 1, 0) + jnp.where(z == 6, 1, 0), 0)
    greeted = greeted + jnp.where(jnp.logical_and(x == 0, z > 0), 1, 0)
    pl.semaphore_wait(barrier, greeted)

    pl.when(both_of(owner, odd))(functools.partial(signal, ready_sem, column_device(z - 1)))
    pl.when(both_of(owner, both_of(z >= 2, z < 4)))(functools.partial(signal, ready_sem, column_device(1)))
    pl.when(both_of(owner, z >= 4))(functools.partial(signal, ready_sem, column_device(3)))
    pl.when(both_of(owner, z >= 6))(functools.partial(signal, ready_sem, column_device(5)))
    pl.when(both_of(owner, z == 6))(functools.partial(signal, ready_sem, column_device(4)))

    @pl.when(jnp.logical_and(x == 0, z > 0))
    def _():
        signal(halo_ready_sem, ((z - 1) * NX + NX - 1, head))

    load_tok.wait()

    pending = []

    def finish():
        for wait in pending:
            wait()

    sends = []

    def send_tok(source, target, device):
        copy = remote(
            tok.at[source, c], tok.at[target, c], tok_send.at[len(sends)], tok_recv.at[target, c], device
        )
        copy.start()
        sends.append(copy)

    def wait_tok(i, core):
        remote(tok.at[i, core], tok.at[i, core], tok_send.at[0], tok_recv.at[i, core], sibling).wait_recv()

    up, down, far = CHIPS.index(1), CHIPS.index(3), CHIPS.index(2)
    send_tok(0, down, above)
    send_tok(0, up, below)
    send_tok(0, far, across)
    send_tok(0, 0, sibling)
    for copy in load_small + load_out:
        copy.start()

    def tokens_of(i):
        return jnp.concatenate([tok[i, 0], tok[i, 1]], 1)

    def project(chips, start):
        def tile(j, carry):
            columns = pl.ds(pl.multiple_of(j * 256, 256), 256)
            part = jnp.zeros((ROWS, 256), F32) if start else acc[j]
            for i in chips:
                part = part + matmul(tokens_of(i), w_in[i, :, columns])
            acc[j] = part
            return carry

        lax.fori_loop(0, TILES, tile, 0)

    wait_tok(0, 1 - c)
    load_in[0].wait()
    project((0,), True)
    for i in (down, up):
        wait_tok(i, c)
        send_tok(i, i, sibling)
    load_in[up].wait()
    load_in[down].wait()
    wait_tok(down, 1 - c)
    wait_tok(up, 1 - c)
    project((up, down), False)
    for copy in load_small:
        copy.wait()

    def gating_of(i):
        weight = gate_weight[:, pair_of(CHIPS[i])]
        weight = jnp.concatenate([weight, jnp.zeros((HEAD - weight.shape[0], 2 * FEATURES), BF16)], 0)
        return matmul_t(tokens_of(i), weight)

    gating = gating_of(0) + gating_of(up) + gating_of(down)
    wait_tok(far, c)
    send_tok(far, far, sibling)
    load_in[far].wait()
    wait_tok(far, 1 - c)
    pending.extend(copy.wait_send for copy in sends)

    def convolved(rows):
        for g in range(GROUPS):
            for i in range(2):
                j = 3 * g + i
                lhs = jnp.concatenate([tok[far, 0, rows], tok[far, 1, rows]], 1)
                part = acc[j, rows] + matmul(lhs, w_in[far, :, j * 256 : (j + 1) * 256])
                for block in range(2):
                    yield 4 * g + 2 * i + block, part[:, block * HEAD : (block + 1) * HEAD].astype(BF16)

    for block, columns in convolved(pl.ds(ROWS - HALO, HALO)):
        halo_out[:, block * HEAD : (block + 1) * HEAD] = columns
    next_seq = lax.rem(seq + 1, NX * NZ)
    send_halo = remote(halo_out, halo_in, halo_sem.at[0], halo_sem.at[1], (next_seq, head))

    @pl.when(jnp.logical_and(last_x, not_top))
    def _():
        pl.semaphore_wait(halo_ready_sem, 1)

    pl.when(seq < NX * NZ - 1)(send_halo.start)
    pending.append(lambda: pl.when(seq < NX * NZ - 1)(send_halo.wait_send))
    for block, columns in convolved(pl.ds(0, ROWS)):
        ext[block, 8:, :] = columns.astype(F32)

    gating = gating + gating_of(far)
    lane = lax.broadcasted_iota(jnp.int32, (1, HEAD), 1)
    shift = jnp.zeros((1, HEAD), F32)
    bias = jnp.zeros((1, HEAD), F32)
    scale = jnp.zeros((1, HEAD), F32)
    for h in range(VALUE_HEADS):
        g, r = divmod(h, 2)
        shift = jnp.where(lane == 4 * g + r, beta_shift[h], shift)
        bias = jnp.where(lane == 4 * g + 2 + r, dt_bias[h], bias)
        scale = jnp.where(lane == 4 * g + 2 + r, decay_scale[h], scale)
    strength = jax.nn.sigmoid(gating - shift)
    shifted = gating + bias
    softplus = jnp.maximum(shifted, 0.0) + jnp.log1p(jnp.exp(-jnp.abs(shifted)))
    log_gate = -scale * softplus
    row_id = lax.broadcasted_iota(jnp.int32, (ROWS, ROWS), 0)
    col_id = lax.broadcasted_iota(jnp.int32, (ROWS, ROWS), 1)
    ones = jnp.where(col_id <= row_id, 1.0, 0.0).astype(BF16)
    cumulative = jnp.zeros((ROWS, HEAD), F32)
    rest = log_gate
    for _ in range(3):
        piece = rest.astype(BF16)
        cumulative = cumulative + matmul(ones, piece)
        rest = rest - piece.astype(F32)
    cumulative_t = jnp.transpose(cumulative)
    gates[0] = strength
    gates[1] = cumulative

    def convolve(first, count):
        for g in range(GROUPS):
            for block in range(CONV // HEAD):
                total = jnp.zeros((count, HEAD), F32)
                for tap in range(4):
                    weight = conv_weight[tap, g : g + 1, block * HEAD : (block + 1) * HEAD].astype(F32)
                    total = total + weight * ext[4 * g + block, pl.ds(first + 5 + tap, count), :]
                value = silu(total)
                rows = pl.ds(first, count)
                if block < 2:
                    norm = lax.rsqrt(jnp.sum(value * value, -1, keepdims=True) + EPSILON)
                    if block == 0:
                        qn[g, rows, :] = (value * (norm * HEAD**-0.5)).astype(BF16)
                    else:
                        kn[g, rows, :] = (value * norm).astype(BF16)
                else:
                    vn[2 * g + block - 2, rows, :] = value.astype(BF16)

    convolve(HALO, ROWS - HALO)
    for g in range(GROUPS):
        j = 3 * g + 2
        part = acc[j] + matmul(tokens_of(far), w_in[far, :, j * 256 : (j + 1) * 256])
        out_gate[g] = silu(part.astype(BF16).astype(F32))
    row = lax.broadcasted_iota(jnp.int32, (HEAD, HEAD), 0)
    col = lax.broadcasted_iota(jnp.int32, (HEAD, HEAD), 1)
    on_lower = col <= row
    below_diag = col < row
    for h in range(VALUE_HEADS):
        g, r = divmod(h, 2)
        lane_c = 4 * g + 2 + r
        cum = cumulative[:, lane_c : lane_c + 1]
        cum_t = cumulative_t[lane_c : lane_c + 1, :]
        for n, (i, j) in enumerate(BLOCKS):
            gap = cum[i * HEAD : (i + 1) * HEAD] - cum_t[:, j * HEAD : (j + 1) * HEAD]
            if i == j:
                decays[h, n] = jnp.where(on_lower, jnp.exp(jnp.where(on_lower, gap, 0.0)), 0.0)
            else:
                decays[h, n] = jnp.exp(gap)

    pl.when(seq > 0)(send_halo.wait_recv)

    @pl.when(seq == 0)
    def _():
        halo_in[...] = jnp.zeros_like(halo_in)

    for block in range(8):
        ext[block, 0:8, :] = halo_in[:, block * HEAD : (block + 1) * HEAD].astype(F32)[HALO - 8 :]
    convolve(0, HALO)

    unit = jnp.where(col == row, 1.0, 0.0)
    unit_b = unit.astype(BF16)
    def within(wide, narrow):
        keep = (lax.div(row, wide) == lax.div(col, wide)) & (lax.div(row, narrow) != lax.div(col, narrow))
        return jnp.where(keep & below_diag, 1.0, 0.0).astype(BF16)

    masks = [within(4 * b, b) for b in (2, 8, 32)]

    parts = [pl.ds(0, HEAD), pl.ds(HEAD, HEAD)]
    inner = []
    for g in range(GROUPS):
        inner.append(matmul_t(jnp.concatenate([kn[g], qn[g]], 0), kn[g]))
    systems, scores = [], []
    for h in range(VALUE_HEADS):
        g, r = divmod(h, 2)
        lane_b, lane_c = 4 * g + r, 4 * g + 2 + r
        beta = gates[0][:, lane_b : lane_b + 1]
        system, score = {}, {}
        for n, (i, j) in enumerate(BLOCKS):
            ri, cj = slice(i * HEAD, (i + 1) * HEAD), slice(j * HEAD, (j + 1) * HEAD)
            ratio = decays[h, n]
            system[i, j] = (beta[ri] * ratio * inner[g][ri, cj]).astype(BF16)
            score[i, j] = (ratio * inner[g][ROWS + i * HEAD : ROWS + (i + 1) * HEAD, cj]).astype(BF16)
        systems.append(system)
        scores.append(score)
    keys = [(h, i) for h in range(VALUE_HEADS) for i in range(2)]
    pairs = within(2, 1)
    inverses = {key: unit_b - pairs * systems[key[0]][key[1], key[1]] for key in keys}
    for mask in masks:
        moved = {k: matmul(inverses[k], mask * systems[k[0]][k[1], k[1]]).astype(BF16) for k in keys}
        once = {k: inverses[k].astype(F32) - matmul(moved[k], inverses[k]) for k in keys}
        twice = {k: matmul(moved[k], moved[k]).astype(BF16) for k in keys}
        inverses = {k: (once[k] + matmul(twice[k], once[k].astype(BF16))).astype(BF16) for k in keys}

    solved = []
    for h in range(VALUE_HEADS):
        g, r = divmod(h, 2)
        lane_b, lane_c = 4 * g + r, 4 * g + 2 + r
        beta = gates[0][:, lane_b : lane_b + 1]
        cum = gates[1][:, lane_c : lane_c + 1]
        right = jnp.concatenate(
            [beta * jnp.exp(cum) * kn[g].astype(F32), beta * vn[h].astype(F32)], 1
        )
        first = matmul(inverses[h, 0], right[:HEAD].astype(BF16)).astype(BF16)
        across_parts = matmul(inverses[h, 1], systems[h][1, 0]).astype(BF16)
        second = matmul(inverses[h, 1], right[HEAD:].astype(BF16))
        second = (second - matmul(across_parts, first)).astype(BF16)
        both = jnp.concatenate([first, second], 0)
        solved.append(both)
        last = cum[ROWS - 1 :, :]
        end_keys = (jnp.exp(last - cum) * kn[g].astype(F32)).astype(BF16)
        grown = lax.dot_general(end_keys, both, (((0,), (0,)), ((), ())), preferred_element_type=F32)
        change = (jnp.exp(last) - 1.0) * unit - grown[:, :HEAD]
        maps[h] = jnp.concatenate([change, grown[:, HEAD:]], 1).astype(BF16)
        stays = jnp.logical_and(x == h, owner)
        row_copy = remote(
            maps.at[h], row_maps.at[c, x], row_send.at[h], row_recv.at[c, x], (z * NX + h, y * 2 + 1)
        )
        pl.when(jnp.logical_not(stays))(row_copy.start)
        pending.append(functools.partial(pl.when(jnp.logical_not(stays)), row_copy.wait_send))

        @pl.when(stays)
        def _():
            row_maps[1, h] = maps[h]

    for h in range(VALUE_HEADS):
        g, r = divmod(h, 2)
        lane_c = 4 * g + 2 + r
        cum = gates[1][:, lane_c : lane_c + 1]
        top = matmul(scores[h][0, 0], solved[h][:HEAD])
        low = matmul(jnp.concatenate([scores[h][1, 0], scores[h][1, 1]], 1), solved[h])
        out = jnp.concatenate([top, low], 0)
        qeff[h] = (jnp.exp(cum) * qn[g].astype(F32) - out[:, :HEAD]).astype(BF16)
        loc[h] = out[:, HEAD:]

    def compose(later, earlier):
        return earlier + later + matmul(later[:, :HEAD].astype(BF16), earlier.astype(BF16))

    def apply(change, shift, before):
        return before + shift.astype(F32) + matmul(change, before.astype(BF16))

    def total_copy(k):
        return remote(row_total.at[k], total_in.at[k], total_send.at[k], total_recv.at[k], column_device(z + 1))

    def shift_copy(k):
        return remote(
            row_total.at[k, 1], total_in.at[k, 1], total_send.at[k], total_recv.at[k], column_device(z + 1)
        )

    def skip_copy(k):
        return remote(row_total.at[k], pair_in.at[k], pair_send.at[k], pair_recv.at[k], column_device(z + 2))

    def pair_copy(k):
        return remote(pair_out.at[k], pair_in.at[k], pair_send.at[k], pair_recv.at[k], column_device(z + 2))

    def state_copy(d, k):
        return remote(
            state_out.at[k], state_in.at[k], state_send.at[k, d - 1], state_recv.at[k], column_device(z + d)
        )

    def back_copy(core, i):
        return remote(
            row_states.at[core, i], states.at[x], back_send.at[core, i], back_recv.at[x], (z * NX + i, y * 2 + core)
        )

    def leaves(core, i):
        return jnp.logical_not(jnp.logical_and(core == 1, x == i))

    @pl.when(owner)
    def _():
        answers = jnp.where(jnp.logical_or(odd, z == 4), 2, 1)

        @pl.when(z != 7)
        def _():
            pl.semaphore_wait(ready_sem, jnp.where(z == 3, 4, answers))


        for core in range(2):
            for i in range(NX):
                row_copy = remote(
                    maps.at[0], row_maps.at[core, i], row_send.at[0], row_recv.at[core, i], sibling
                )
                pl.when(leaves(core, i))(row_copy.wait_recv)
            row_map = [row_maps[core, i].astype(F32) for i in range(NX)]
            first_two = compose(row_map[1], row_map[0])
            last_two = compose(row_map[3], row_map[2])
            prefix[core, 0] = row_map[0]
            prefix[core, 1] = first_two
            prefix[core, 2] = compose(row_map[2], first_two)
            total = compose(last_two, first_two).astype(BF16)
            row_total[core, 0] = total[:, :HEAD]
            row_total[core, 1] = total[:, HEAD:]
            pl.when(z == 0)(shift_copy(core).start)
            pl.when(both_of(z > 0, jnp.logical_or(even, z == 5)))(total_copy(core).start)
            pl.when(z == 4)(skip_copy(core).start)

        def joined(ref, k):
            return jnp.concatenate([ref[k, 0], ref[k, 1]], 1).astype(F32)

        @pl.when(z == 0)
        def _():
            state_before[...] = jnp.zeros_like(state_before)

        @pl.when(z == 1)
        def _():
            for core in range(2):
                shift_copy(core).wait_recv()
                shift = total_in[core, 1].astype(F32)
                state_before[core] = shift
                state_out[core] = apply(row_total[core, 0], row_total[core, 1], shift).astype(BF16)
                state_copy(2, core).start()
                state_copy(1, core).start()

        @pl.when(both_of(even, both_of(z > 0, z < 6)))
        def _():
            for core in range(2):
                state_copy(1, core).wait_recv()
                state_before[core] = state_in[core].astype(F32)

        @pl.when(both_of(odd, both_of(z > 1, z < 6)))
        def _():
            for core in range(2):
                total_copy(core).wait_recv()
                pair = compose(joined(row_total, core), joined(total_in, core)).astype(BF16)
                pair_out[core, 0] = pair[:, :HEAD]
                pair_out[core, 1] = pair[:, HEAD:]
                pl.when(z == 5)(pair_copy(core).start)
            for core in range(2):
                state_copy(1, core).wait_recv()
                state = state_in[core].astype(F32)

                @pl.when(z == 3)
                def _():
                    state_out[core] = apply(pair_out[core, 0], pair_out[core, 1], state).astype(BF16)
                    for d in (3, 2, 4, 1):
                        state_copy(d, core).start()

                state_before[core] = apply(total_in[core, 0], total_in[core, 1], state)

        @pl.when(z == 6)
        def _():
            both = []
            for core in range(2):
                pair_copy(core).wait_recv()
                total_copy(core).wait_recv()
                both.append(compose(joined(total_in, core), joined(pair_in, core)))
            for core in range(2):
                state_copy(1, core).wait_recv()
                change = both[core][:, :HEAD].astype(BF16)
                state_before[core] = apply(change, both[core][:, HEAD:], state_in[core].astype(F32))

        @pl.when(z == 7)
        def _():
            for core in range(2):
                state_copy(1, core).wait_recv()
                pair_copy(core).wait_recv()
                total_copy(core).wait_recv()
                state = apply(pair_in[core, 0], pair_in[core, 1], state_in[core].astype(F32))
                state_before[core] = apply(total_in[core, 0], total_in[core, 1], state)

        for core in range(2):
            state = state_before[core]
            row_states[core, 0] = state.astype(BF16)
            for i in range(1, NX):
                before_i = prefix[core, i - 1]
                row_states[core, i] = apply(
                    before_i[:, :HEAD].astype(BF16), before_i[:, HEAD:], state
                ).astype(BF16)
            for i in range(NX):
                pl.when(leaves(core, i))(back_copy(core, i).start)
        states[pl.ds(x, 1)] = row_states[1, pl.ds(x, 1)]

    def wait_owner():
        for core in range(2):
            pl.when(z == 0)(shift_copy(core).wait_send)
            pl.when(both_of(z > 0, jnp.logical_or(even, z == 5)))(total_copy(core).wait_send)
            pl.when(z == 4)(skip_copy(core).wait_send)
            pl.when(z == 5)(pair_copy(core).wait_send)
            for d in (1, 2):
                pl.when(z == 1)(state_copy(d, core).wait_send)
            for d in range(1, 5):
                pl.when(z == 3)(state_copy(d, core).wait_send)
        for core in range(2):
            for i in range(NX):
                pl.when(leaves(core, i))(back_copy(core, i).wait_send)

    pending.append(lambda: pl.when(owner)(wait_owner))
    for h in range(VALUE_HEADS):
        arrival = remote(
            row_states.at[0, 0], states.at[h], back_send.at[0, 0], back_recv.at[h], sibling
        )
        pl.when(jnp.logical_not(jnp.logical_and(owner, x == h)))(arrival.wait_recv)

    gain = norm_gain[...]
    hidden = []
    for h in range(VALUE_HEADS):
        g, r = divmod(h, 2)
        attended = loc[h] + matmul(qeff[h], states[h])
        back = lax.rsqrt(jnp.mean(attended * attended, -1, keepdims=True) + EPSILON)
        gate = out_gate[g, :, r * HEAD : (r + 1) * HEAD]
        hidden.append((attended * back * gain * gate).astype(BF16))
    hidden = jnp.concatenate(hidden, 1)

    def partial_for(r, core):
        columns = pl.ds(pl.multiple_of(core * FEATURES, FEATURES), FEATURES)
        return matmul(hidden, w_out[CHIPS.index(r), :, columns])

    def sibling_copy(r):
        return remote(sib_out.at[r], sib_in.at[r], sib_send.at[r], sib_recv.at[r], sibling)

    ring = {
        r: remote(ring_out.at[r - 1], ring_in.at[r - 1], ring_send.at[r - 1], ring_recv.at[r - 1], device)
        for r, device in ((1, above), (2, across), (3, below))
    }
    for copy in load_out:
        copy.wait()
    def send_sibling(r):
        sib_out[r] = partial_for(r, 1 - c).astype(BF16)
        sibling_copy(r).start()

    def send_ring(r):
        mine = partial_for(r, c)
        sibling_copy(r).wait_recv()
        ring_out[r - 1] = (mine + sib_in[r].astype(F32)).astype(BF16)
        ring[r].start()

    send_sibling(2)
    send_sibling(1)
    send_ring(2)
    send_sibling(3)
    send_ring(1)
    send_ring(3)
    send_sibling(0)
    total = partial_for(0, c)
    sibling_copy(0).wait_recv()
    total = total + sib_in[0].astype(F32)
    for r in (1, 3, 2):
        ring[r].wait_recv()
        total = total + ring_in[r - 1].astype(F32)
    out_ref[...] = total.astype(BF16)

    finish()
    for r in range(NY):
        sibling_copy(r).wait_send()
    for copy in ring.values():
        copy.wait_send()


def per_device(
    tokens,
    in_weight,
    gate_weight,
    conv_weight,
    decay_scale,
    dt_bias,
    beta_shift,
    norm_gain,
    out_weight,
):
    anywhere = pl.BlockSpec(memory_space=pltpu.HBM)
    vmem = pl.BlockSpec(memory_space=pltpu.VMEM)
    dma = pltpu.SemaphoreType.DMA
    return pl.pallas_call(
        kernel,
        out_shape=pltpu.VMEM((ROWS, FEATURES), BF16),
        in_specs=[anywhere] * 9,
        out_specs=vmem,
        scratch_shapes=[
            pltpu.VMEM((2 * VALUE_HEADS, 8 * FEATURES), BF16),
            pltpu.VMEM((4, GROUPS, CONV), BF16),
            pltpu.SMEM((VALUE_HEADS,), F32),
            pltpu.SMEM((VALUE_HEADS,), F32),
            pltpu.SMEM((VALUE_HEADS,), F32),
            pltpu.VMEM((1, HEAD), F32),
            pltpu.VMEM((NY, 2, ROWS, FEATURES), BF16),
            pltpu.VMEM((NY, 2 * FEATURES, GROUPS * GROUP), BF16),
            pltpu.VMEM((NY, VALUE_HEADS * HEAD, 2 * FEATURES), BF16),
            pltpu.VMEM((TILES, ROWS, 256), F32),
            pltpu.VMEM((8, 8 + ROWS, HEAD), F32),
            pltpu.VMEM((HALO, GROUPS * CONV), BF16),
            pltpu.VMEM((HALO, GROUPS * CONV), BF16),
            pltpu.VMEM((2, ROWS, HEAD), F32),
            pltpu.VMEM((GROUPS, ROWS, HEAD), BF16),
            pltpu.VMEM((GROUPS, ROWS, HEAD), BF16),
            pltpu.VMEM((VALUE_HEADS, ROWS, HEAD), BF16),
            pltpu.VMEM((VALUE_HEADS, HEAD, 2 * HEAD), BF16),
            pltpu.VMEM((2, NX, HEAD, 2 * HEAD), BF16),
            pltpu.VMEM((2, NX - 1, HEAD, 2 * HEAD), F32),
            pltpu.VMEM((2, 2, HEAD, HEAD), BF16),
            pltpu.VMEM((2, 2, HEAD, HEAD), BF16),
            pltpu.VMEM((2, 2, HEAD, HEAD), BF16),
            pltpu.VMEM((2, 2, HEAD, HEAD), BF16),
            pltpu.VMEM((2, HEAD, HEAD), BF16),
            pltpu.VMEM((2, HEAD, HEAD), BF16),
            pltpu.VMEM((2, HEAD, HEAD), F32),
            pltpu.VMEM((GROUPS, ROWS, 2 * HEAD), F32),
            pltpu.VMEM((VALUE_HEADS, len(BLOCKS), HEAD, HEAD), F32),
            pltpu.VMEM((2, NX, HEAD, HEAD), BF16),
            pltpu.VMEM((VALUE_HEADS, HEAD, HEAD), BF16),
            pltpu.VMEM((VALUE_HEADS, ROWS, HEAD), F32),
            pltpu.VMEM((VALUE_HEADS, ROWS, HEAD), BF16),
            pltpu.VMEM((NY, ROWS, FEATURES), BF16),
            pltpu.VMEM((NY, ROWS, FEATURES), BF16),
            pltpu.VMEM((NY - 1, ROWS, FEATURES), BF16),
            pltpu.VMEM((NY - 1, ROWS, FEATURES), BF16),
            dma,
            dma((6,)),
            dma((NY,)),
            dma((NY,)),
            dma((7,)),
            dma((NY, 2)),
            dma((2,)),
            dma((NX,)),
            dma((2, NX)),
            dma((2,)),
            dma((2,)),
            dma((2,)),
            dma((2,)),
            dma((2, 4)),
            dma((2,)),
            pltpu.SemaphoreType.REGULAR,
            pltpu.SemaphoreType.REGULAR,
            dma((2, NX)),
            dma((NX,)),
            dma((NY,)),
            dma((NY,)),
            dma((NY - 1,)),
            dma((NY - 1,)),
        ],
        compiler_params=pltpu.CompilerParams(
            collective_id=0, has_side_effects=True, vmem_limit_bytes=60 * 1024 * 1024
        ),
    )(
        tokens,
        in_weight,
        gate_weight.T,
        conv_weight,
        decay_scale,
        dt_bias,
        beta_shift,
        norm_gain.reshape(1, HEAD),
        out_weight,
    )


def solution(mesh):
    in_specs = (
        P("seq", "head"),
        P(None, "head"),
        P(None, "head"),
        P(None, "head", None),
        P("head"),
        P("head"),
        P("head"),
        P(),
        P("head", None),
    )
    out_specs = P("seq", "head")
    return jax.shard_map(
        per_device, mesh=mesh, in_specs=in_specs, out_specs=out_specs, check_vma=False
    )
```

```python
import functools

import jax
import jax.numpy as jnp
from jax import lax
from jax.experimental import pallas as pl
from jax.experimental.pallas import tpu as pltpu
from jax.sharding import PartitionSpec as P

F32 = jnp.float32
BF16 = jnp.bfloat16
EPSILON = 1e-06

ROWS = 256
HEAD = 128
FEATURES = 256
GROUPS = 2
VALUE_HEADS = 4
BLOCKS = ((0, 0), (1, 0), (1, 1))
TILES = 6
CONV = 512
GROUP = 768
HALO = 16
NX = 4
NZ = 8
NY = 4

CHIPS = (0, 1, 3, 2)


def matmul(a, b):
    return jnp.dot(a, b, preferred_element_type=F32)


def matmul_t(a, b):
    return lax.dot_general(a, b, (((1,), (1,)), ((), ())), preferred_element_type=F32)


def silu(v):
    return 0.5 * v * (1.0 + jnp.tanh(0.5 * v))


def kernel(
    tokens_hbm,
    in_weight_hbm,
    gate_weight_hbm,
    conv_weight_hbm,
    decay_scale_hbm,
    dt_bias_hbm,
    beta_shift_hbm,
    norm_gain_hbm,
    out_weight_hbm,
    out_ref,
    gate_weight,
    conv_weight,
    decay_scale,
    dt_bias,
    beta_shift,
    norm_gain,
    tok,
    w_in,
    w_out,
    acc,
    ext,
    halo_out,
    halo_in,
    gates,
    qn,
    kn,
    vn,
    maps,
    row_maps,
    prefix,
    row_total,
    total_in,
    pair_in,
    pair_out,
    state_in,
    state_out,
    state_before,
    out_gate,
    decays,
    row_states,
    states,
    loc,
    qeff,
    sib_out,
    sib_in,
    ring_out,
    ring_in,
    load_sem,
    small_sem,
    win_sem,
    wout_sem,
    tok_send,
    tok_recv,
    tail_send,
    tail_recv,
    halo_sem,
    row_send,
    row_recv,
    total_send,
    total_recv,
    pair_send,
    pair_recv,
    state_send,
    state_recv,
    ready_sem,
    halo_ready_sem,
    back_send,
    back_recv,
    sib_send,
    sib_recv,
    ring_send,
    ring_recv,
):
    seq = lax.axis_index("seq")
    head = lax.axis_index("head")
    z, x = lax.div(seq, NX), lax.rem(seq, NX)
    y, c = lax.div(head, 2), lax.rem(head, 2)

    def chip_at(r):
        return lax.rem(y + r, NY)

    above = (seq, chip_at(1) * 2 + c)
    below = (seq, chip_at(3) * 2 + c)
    across = (seq, chip_at(2) * 2 + c)
    sibling = (seq, y * 2 + 1 - c)
    others = [(seq, chip_at(r) * 2 + 1 - c) for r in (1, 3, 2)]

    def remote(src, dst, send, recv, device):
        return pltpu.make_async_remote_copy(
            src_ref=src,
            dst_ref=dst,
            send_sem=send,
            recv_sem=recv,
            device_id=device,
            device_id_type=pl.DeviceIdType.MESH,
        )

    load_tok = pltpu.make_async_copy(tokens_hbm, tok.at[0, c], load_sem)
    load_tok.start()

    barrier = pltpu.get_barrier_semaphore()
    owner = c == 1

    def row_device(r, core):
        return (z * NX + lax.rem(x + r, NX), y * 2 + core)

    def column_device(there):
        return (there * NX + x, head)

    def signal(semaphore, device):
        pl.semaphore_signal(semaphore, inc=1, device_id=device, device_id_type=pl.DeviceIdType.MESH)

    odd = lax.rem(z, 2) == 1
    even = jnp.logical_not(odd)
    both_of = jnp.logical_and
    last_x = x == NX - 1
    not_top = z < NZ - 1
    next_row = ((z + 1) * NX, head)
    for device in [above, below, across, sibling] + others + [row_device(r, 1) for r in range(1, NX)]:
        signal(barrier, device)
    for r in range(1, NX):
        pl.when(owner)(functools.partial(signal, barrier, row_device(r, 0)))

    pl.when(both_of(owner, even))(functools.partial(signal, barrier, column_device(z + 1)))
    for d in (1, 2):
        pl.when(both_of(owner, both_of(odd, not_top)))(functools.partial(signal, barrier, column_device(z + d)))
    pl.when(both_of(owner, z == 4))(functools.partial(signal, barrier, column_device(z + 2)))
    for d in (3, 4):
        pl.when(both_of(owner, z == 3))(functools.partial(signal, barrier, column_device(z + d)))

    @pl.when(jnp.logical_and(last_x, not_top))
    def _():
        signal(barrier, next_row)

    def pair_of(r):
        return pl.ds(pl.multiple_of(chip_at(r) * 2 * FEATURES, 2 * FEATURES), 2 * FEATURES)

    load_in, load_out, load_small = [], [], []
    for i, r in enumerate(CHIPS):
        load_in.append(pltpu.make_async_copy(in_weight_hbm.at[pair_of(r)], w_in.at[i], win_sem.at[i]))
        load_out.append(
            pltpu.make_async_copy(out_weight_hbm.at[:, pair_of(r)], w_out.at[i], wout_sem.at[i])
        )
    for i, (source, target) in enumerate(
        (
            (gate_weight_hbm, gate_weight),
            (conv_weight_hbm, conv_weight),
            (decay_scale_hbm, decay_scale),
            (dt_bias_hbm, dt_bias),
            (beta_shift_hbm, beta_shift),
            (norm_gain_hbm, norm_gain),
        )
    ):
        load_small.append(pltpu.make_async_copy(source, target, small_sem.at[i]))
    for copy in load_in:
        copy.start()

    greeted = 10 + jnp.where(owner, 3 + lax.rem(z, 2) + jnp.where(z >= 2, 1, 0) + jnp.where(z >= 6, 1, 0) + jnp.where(z == 6, 1, 0), 0)
    greeted = greeted + jnp.where(jnp.logical_and(x == 0, z > 0), 1, 0)
    pl.semaphore_wait(barrier, greeted)

    pl.when(both_of(owner, odd))(functools.partial(signal, ready_sem, column_device(z - 1)))
    pl.when(both_of(owner, both_of(z >= 2, z < 4)))(functools.partial(signal, ready_sem, column_device(1)))
    pl.when(both_of(owner, z >= 4))(functools.partial(signal, ready_sem, column_device(3)))
    pl.when(both_of(owner, z >= 6))(functools.partial(signal, ready_sem, column_device(5)))
    pl.when(both_of(owner, z == 6))(functools.partial(signal, ready_sem, column_device(4)))

    @pl.when(jnp.logical_and(x == 0, z > 0))
    def _():
        signal(halo_ready_sem, ((z - 1) * NX + NX - 1, head))

    load_tok.wait()

    pending = []

    def finish():
        for wait in pending:
            wait()

    sends = []

    body, tail = pl.ds(0, ROWS - HALO), pl.ds(ROWS - HALO, HALO)

    def send_tok(source, target, device):
        copy = remote(
            tok.at[source, c, body],
            tok.at[target, c, body],
            tok_send.at[len(sends)],
            tok_recv.at[target, c],
            device,
        )
        copy.start()
        sends.append(copy)

    def wait_tok(i, core):
        remote(
            tok.at[i, core, body], tok.at[i, core, body], tok_send.at[0], tok_recv.at[i, core], sibling
        ).wait_recv()

    up, down, far = CHIPS.index(1), CHIPS.index(3), CHIPS.index(2)
    tail_targets = [(down, above), (down, others[0]), (up, below), (up, others[1])]
    tail_targets += [(far, across), (far, others[2]), (0, sibling)]
    for n, (target, device) in enumerate(tail_targets):
        copy = remote(
            tok.at[0, c, tail], tok.at[target, c, tail], tail_send.at[n], tail_recv.at[target, c], device
        )
        copy.start()
        pending.append(copy.wait_send)
    send_tok(0, down, above)
    send_tok(0, up, below)
    send_tok(0, far, across)
    send_tok(0, 0, sibling)
    for copy in load_small + load_out:
        copy.start()

    def tokens_of(i):
        return jnp.concatenate([tok[i, 0], tok[i, 1]], 1)

    def project(chips, start):
        def tile(j, carry):
            columns = pl.ds(pl.multiple_of(j * 256, 256), 256)
            part = jnp.zeros((ROWS, 256), F32) if start else acc[j]
            for i in chips:
                part = part + matmul(tokens_of(i), w_in[i, :, columns])
            acc[j] = part
            return carry

        lax.fori_loop(0, TILES, tile, 0)

    def wait_tail(i, core):
        remote(
            tok.at[i, core, tail], tok.at[i, core, tail], tail_send.at[0], tail_recv.at[i, core], sibling
        ).wait_recv()

    wait_tail(0, 1 - c)
    wait_tok(0, 1 - c)
    load_in[0].wait()
    project((0,), True)
    for i in (up, down, far):
        wait_tail(i, c)
        wait_tail(i, 1 - c)
    for i in (up, down, far):
        load_in[i].wait()
    for g in range(GROUPS):
        for n in range(2):
            columns = pl.ds((3 * g + n) * 256, 256)
            part = jnp.zeros((HALO, 256), F32)
            for i in range(NY):
                rows = jnp.concatenate([tok[i, 0, tail], tok[i, 1, tail]], 1)
                part = part + matmul(rows, w_in[i, :, columns])
            halo_out[:, (2 * g + n) * 256 : (2 * g + n + 1) * 256] = part.astype(BF16)

    for i in (down, up):
        wait_tok(i, c)
        send_tok(i, i, sibling)

    next_seq = lax.rem(seq + 1, NX * NZ)
    send_halo = remote(halo_out, halo_in, halo_sem.at[0], halo_sem.at[1], (next_seq, head))

    @pl.when(jnp.logical_and(last_x, not_top))
    def _():
        pl.semaphore_wait(halo_ready_sem, 1)

    pl.when(seq < NX * NZ - 1)(send_halo.start)
    pending.append(lambda: pl.when(seq < NX * NZ - 1)(send_halo.wait_send))
    wait_tok(down, 1 - c)
    wait_tok(up, 1 - c)
    project((up, down), False)
    for copy in load_small:
        copy.wait()

    def gating_of(i):
        weight = gate_weight[:, pair_of(CHIPS[i])]
        weight = jnp.concatenate([weight, jnp.zeros((HEAD - weight.shape[0], 2 * FEATURES), BF16)], 0)
        return matmul_t(tokens_of(i), weight)

    gating = gating_of(0) + gating_of(up) + gating_of(down)
    wait_tok(far, c)
    send_tok(far, far, sibling)
    wait_tok(far, 1 - c)
    pending.extend(copy.wait_send for copy in sends)

    for g in range(GROUPS):
        for n in range(2):
            j = 3 * g + n
            part = acc[j] + matmul(tokens_of(far), w_in[far, :, j * 256 : (j + 1) * 256])
            for block in range(2):
                columns = part[:, block * HEAD : (block + 1) * HEAD].astype(BF16)
                ext[4 * g + 2 * n + block, 8:, :] = columns.astype(F32)

    gating = gating + gating_of(far)
    lane = lax.broadcasted_iota(jnp.int32, (1, HEAD), 1)
    shift = jnp.zeros((1, HEAD), F32)
    bias = jnp.zeros((1, HEAD), F32)
    scale = jnp.zeros((1, HEAD), F32)
    for h in range(VALUE_HEADS):
        g, r = divmod(h, 2)
        shift = jnp.where(lane == 4 * g + r, beta_shift[h], shift)
        bias = jnp.where(lane == 4 * g + 2 + r, dt_bias[h], bias)
        scale = jnp.where(lane == 4 * g + 2 + r, decay_scale[h], scale)
    strength = jax.nn.sigmoid(gating - shift)
    shifted = gating + bias
    softplus = jnp.maximum(shifted, 0.0) + jnp.log1p(jnp.exp(-jnp.abs(shifted)))
    log_gate = -scale * softplus
    row_id = lax.broadcasted_iota(jnp.int32, (ROWS, ROWS), 0)
    col_id = lax.broadcasted_iota(jnp.int32, (ROWS, ROWS), 1)
    ones = jnp.where(col_id <= row_id, 1.0, 0.0).astype(BF16)
    cumulative = jnp.zeros((ROWS, HEAD), F32)
    rest = log_gate
    for _ in range(3):
        piece = rest.astype(BF16)
        cumulative = cumulative + matmul(ones, piece)
        rest = rest - piece.astype(F32)
    cumulative_t = jnp.transpose(cumulative)
    gates[0] = strength
    gates[1] = cumulative

    def convolve(first, count):
        for g in range(GROUPS):
            for block in range(CONV // HEAD):
                total = jnp.zeros((count, HEAD), F32)
                for tap in range(4):
                    weight = conv_weight[tap, g : g + 1, block * HEAD : (block + 1) * HEAD].astype(F32)
                    total = total + weight * ext[4 * g + block, pl.ds(first + 5 + tap, count), :]
                value = silu(total)
                rows = pl.ds(first, count)
                if block < 2:
                    norm = lax.rsqrt(jnp.sum(value * value, -1, keepdims=True) + EPSILON)
                    if block == 0:
                        qn[g, rows, :] = (value * (norm * HEAD**-0.5)).astype(BF16)
                    else:
                        kn[g, rows, :] = (value * norm).astype(BF16)
                else:
                    vn[2 * g + block - 2, rows, :] = value.astype(BF16)

    pl.when(seq > 0)(send_halo.wait_recv)

    @pl.when(seq == 0)
    def _():
        halo_in[...] = jnp.zeros_like(halo_in)

    for block in range(8):
        ext[block, 0:8, :] = halo_in[:, block * HEAD : (block + 1) * HEAD].astype(F32)[HALO - 8 :]
    convolve(0, ROWS)
    for g in range(GROUPS):
        j = 3 * g + 2
        part = acc[j] + matmul(tokens_of(far), w_in[far, :, j * 256 : (j + 1) * 256])
        out_gate[g] = silu(part.astype(BF16).astype(F32))
    row = lax.broadcasted_iota(jnp.int32, (HEAD, HEAD), 0)
    col = lax.broadcasted_iota(jnp.int32, (HEAD, HEAD), 1)
    on_lower = col <= row
    below_diag = col < row
    for h in range(VALUE_HEADS):
        g, r = divmod(h, 2)
        lane_c = 4 * g + 2 + r
        cum = cumulative[:, lane_c : lane_c + 1]
        cum_t = cumulative_t[lane_c : lane_c + 1, :]
        for n, (i, j) in enumerate(BLOCKS):
            gap = cum[i * HEAD : (i + 1) * HEAD] - cum_t[:, j * HEAD : (j + 1) * HEAD]
            if i == j:
                decays[h, n] = jnp.where(on_lower, jnp.exp(jnp.where(on_lower, gap, 0.0)), 0.0)
            else:
                decays[h, n] = jnp.exp(gap)


    unit = jnp.where(col == row, 1.0, 0.0)
    unit_b = unit.astype(BF16)
    def within(wide, narrow):
        keep = (lax.div(row, wide) == lax.div(col, wide)) & (lax.div(row, narrow) != lax.div(col, narrow))
        return jnp.where(keep & below_diag, 1.0, 0.0).astype(BF16)

    masks = [within(4 * b, b) for b in (2, 8, 32)]

    parts = [pl.ds(0, HEAD), pl.ds(HEAD, HEAD)]
    inner = []
    for g in range(GROUPS):
        inner.append(matmul_t(jnp.concatenate([kn[g], qn[g]], 0), kn[g]))
    systems, scores = [], []
    for h in range(VALUE_HEADS):
        g, r = divmod(h, 2)
        lane_b, lane_c = 4 * g + r, 4 * g + 2 + r
        beta = gates[0][:, lane_b : lane_b + 1]
        system, score = {}, {}
        for n, (i, j) in enumerate(BLOCKS):
            ri, cj = slice(i * HEAD, (i + 1) * HEAD), slice(j * HEAD, (j + 1) * HEAD)
            ratio = decays[h, n]
            system[i, j] = (beta[ri] * ratio * inner[g][ri, cj]).astype(BF16)
            score[i, j] = (ratio * inner[g][ROWS + i * HEAD : ROWS + (i + 1) * HEAD, cj]).astype(BF16)
        systems.append(system)
        scores.append(score)
    keys = [(h, i) for h in range(VALUE_HEADS) for i in range(2)]
    pairs = within(2, 1)
    inverses = {key: unit_b - pairs * systems[key[0]][key[1], key[1]] for key in keys}
    for mask in masks:
        moved = {k: matmul(inverses[k], mask * systems[k[0]][k[1], k[1]]).astype(BF16) for k in keys}
        once = {k: inverses[k].astype(F32) - matmul(moved[k], inverses[k]) for k in keys}
        twice = {k: matmul(moved[k], moved[k]).astype(BF16) for k in keys}
        inverses = {k: (once[k] + matmul(twice[k], once[k].astype(BF16))).astype(BF16) for k in keys}

    solved = []
    for h in range(VALUE_HEADS):
        g, r = divmod(h, 2)
        lane_b, lane_c = 4 * g + r, 4 * g + 2 + r
        beta = gates[0][:, lane_b : lane_b + 1]
        cum = gates[1][:, lane_c : lane_c + 1]
        right = jnp.concatenate(
            [beta * jnp.exp(cum) * kn[g].astype(F32), beta * vn[h].astype(F32)], 1
        )
        first = matmul(inverses[h, 0], right[:HEAD].astype(BF16)).astype(BF16)
        across_parts = matmul(inverses[h, 1], systems[h][1, 0]).astype(BF16)
        second = matmul(inverses[h, 1], right[HEAD:].astype(BF16))
        second = (second - matmul(across_parts, first)).astype(BF16)
        both = jnp.concatenate([first, second], 0)
        solved.append(both)
        last = cum[ROWS - 1 :, :]
        end_keys = (jnp.exp(last - cum) * kn[g].astype(F32)).astype(BF16)
        grown = lax.dot_general(end_keys, both, (((0,), (0,)), ((), ())), preferred_element_type=F32)
        change = (jnp.exp(last) - 1.0) * unit - grown[:, :HEAD]
        maps[h] = jnp.concatenate([change, grown[:, HEAD:]], 1).astype(BF16)
        stays = jnp.logical_and(x == h, owner)
        row_copy = remote(
            maps.at[h], row_maps.at[c, x], row_send.at[h], row_recv.at[c, x], (z * NX + h, y * 2 + 1)
        )
        pl.when(jnp.logical_not(stays))(row_copy.start)
        pending.append(functools.partial(pl.when(jnp.logical_not(stays)), row_copy.wait_send))

        @pl.when(stays)
        def _():
            row_maps[1, h] = maps[h]

    for h in range(VALUE_HEADS):
        g, r = divmod(h, 2)
        lane_c = 4 * g + 2 + r
        cum = gates[1][:, lane_c : lane_c + 1]
        top = matmul(scores[h][0, 0], solved[h][:HEAD])
        low = matmul(jnp.concatenate([scores[h][1, 0], scores[h][1, 1]], 1), solved[h])
        out = jnp.concatenate([top, low], 0)
        qeff[h] = (jnp.exp(cum) * qn[g].astype(F32) - out[:, :HEAD]).astype(BF16)
        loc[h] = out[:, HEAD:]

    def compose(later, earlier):
        return earlier + later + matmul(later[:, :HEAD].astype(BF16), earlier.astype(BF16))

    def apply(change, shift, before):
        return before + shift.astype(F32) + matmul(change, before.astype(BF16))

    def total_copy(k):
        return remote(row_total.at[k], total_in.at[k], total_send.at[k], total_recv.at[k], column_device(z + 1))

    def shift_copy(k):
        return remote(
            row_total.at[k, 1], total_in.at[k, 1], total_send.at[k], total_recv.at[k], column_device(z + 1)
        )

    def skip_copy(k):
        return remote(row_total.at[k], pair_in.at[k], pair_send.at[k], pair_recv.at[k], column_device(z + 2))

    def pair_copy(k):
        return remote(pair_out.at[k], pair_in.at[k], pair_send.at[k], pair_recv.at[k], column_device(z + 2))

    def state_copy(d, k):
        return remote(
            state_out.at[k], state_in.at[k], state_send.at[k, d - 1], state_recv.at[k], column_device(z + d)
        )

    def back_copy(core, i):
        return remote(
            row_states.at[core, i], states.at[x], back_send.at[core, i], back_recv.at[x], (z * NX + i, y * 2 + core)
        )

    def leaves(core, i):
        return jnp.logical_not(jnp.logical_and(core == 1, x == i))

    @pl.when(owner)
    def _():
        answers = jnp.where(jnp.logical_or(odd, z == 4), 2, 1)

        @pl.when(z != 7)
        def _():
            pl.semaphore_wait(ready_sem, jnp.where(z == 3, 4, answers))


        for core in range(2):
            for i in range(NX):
                row_copy = remote(
                    maps.at[0], row_maps.at[core, i], row_send.at[0], row_recv.at[core, i], sibling
                )
                pl.when(leaves(core, i))(row_copy.wait_recv)
        row_map = [[row_maps[core, i].astype(F32) for i in range(NX)] for core in range(2)]
        first_two = [compose(row_map[core][1], row_map[core][0]) for core in range(2)]
        last_two = [compose(row_map[core][3], row_map[core][2]) for core in range(2)]
        for core in range(2):
            total = compose(last_two[core], first_two[core]).astype(BF16)
            row_total[core, 0] = total[:, :HEAD]
            row_total[core, 1] = total[:, HEAD:]
        for core in range(2):
            pl.when(z == 0)(shift_copy(core).start)
            pl.when(both_of(z > 0, jnp.logical_or(even, z == 5)))(total_copy(core).start)
        for core in range(2):
            pl.when(z == 4)(skip_copy(core).start)
        for core in range(2):
            prefix[core, 0] = row_map[core][0]
            prefix[core, 1] = first_two[core]
            prefix[core, 2] = compose(row_map[core][2], first_two[core])

        def joined(ref, k):
            return jnp.concatenate([ref[k, 0], ref[k, 1]], 1).astype(F32)

        @pl.when(z == 0)
        def _():
            state_before[...] = jnp.zeros_like(state_before)

        @pl.when(z == 1)
        def _():
            for core in range(2):
                shift_copy(core).wait_recv()
                shift = total_in[core, 1].astype(F32)
                state_before[core] = shift
                state_out[core] = apply(row_total[core, 0], row_total[core, 1], shift).astype(BF16)
                state_copy(2, core).start()
                state_copy(1, core).start()

        @pl.when(both_of(even, both_of(z > 0, z < 6)))
        def _():
            for core in range(2):
                state_copy(1, core).wait_recv()
                state_before[core] = state_in[core].astype(F32)

        @pl.when(both_of(odd, both_of(z > 1, z < 6)))
        def _():
            for core in range(2):
                total_copy(core).wait_recv()
                pair = compose(joined(row_total, core), joined(total_in, core)).astype(BF16)
                pair_out[core, 0] = pair[:, :HEAD]
                pair_out[core, 1] = pair[:, HEAD:]
                pl.when(z == 5)(pair_copy(core).start)
            for core in range(2):
                state_copy(1, core).wait_recv()
                state = state_in[core].astype(F32)

                @pl.when(z == 3)
                def _():
                    state_out[core] = apply(pair_out[core, 0], pair_out[core, 1], state).astype(BF16)
                    for d in (4, 3, 2, 1):
                        state_copy(d, core).start()

                state_before[core] = apply(total_in[core, 0], total_in[core, 1], state)

        @pl.when(z == 6)
        def _():
            both = []
            for core in range(2):
                pair_copy(core).wait_recv()
                total_copy(core).wait_recv()
                both.append(compose(joined(total_in, core), joined(pair_in, core)))
            for core in range(2):
                state_copy(1, core).wait_recv()
                change = both[core][:, :HEAD].astype(BF16)
                state_before[core] = apply(change, both[core][:, HEAD:], state_in[core].astype(F32))

        @pl.when(z == 7)
        def _():
            for core in range(2):
                state_copy(1, core).wait_recv()
                pair_copy(core).wait_recv()
                total_copy(core).wait_recv()
                state = apply(pair_in[core, 0], pair_in[core, 1], state_in[core].astype(F32))
                state_before[core] = apply(total_in[core, 0], total_in[core, 1], state)

        for core in range(2):
            state = state_before[core]
            row_states[core, 0] = state.astype(BF16)
            for i in range(1, NX):
                before_i = prefix[core, i - 1]
                row_states[core, i] = apply(
                    before_i[:, :HEAD].astype(BF16), before_i[:, HEAD:], state
                ).astype(BF16)
            for i in range(NX):
                pl.when(leaves(core, i))(back_copy(core, i).start)
        states[pl.ds(x, 1)] = row_states[1, pl.ds(x, 1)]

    def wait_owner():
        for core in range(2):
            pl.when(z == 0)(shift_copy(core).wait_send)
            pl.when(both_of(z > 0, jnp.logical_or(even, z == 5)))(total_copy(core).wait_send)
            pl.when(z == 4)(skip_copy(core).wait_send)
            pl.when(z == 5)(pair_copy(core).wait_send)
            for d in (1, 2):
                pl.when(z == 1)(state_copy(d, core).wait_send)
            for d in range(1, 5):
                pl.when(z == 3)(state_copy(d, core).wait_send)
        for core in range(2):
            for i in range(NX):
                pl.when(leaves(core, i))(back_copy(core, i).wait_send)

    pending.append(lambda: pl.when(owner)(wait_owner))
    for h in range(VALUE_HEADS):
        arrival = remote(
            row_states.at[0, 0], states.at[h], back_send.at[0, 0], back_recv.at[h], sibling
        )
        pl.when(jnp.logical_not(jnp.logical_and(owner, x == h)))(arrival.wait_recv)

    gain = norm_gain[...]
    hidden = []
    for h in range(VALUE_HEADS):
        g, r = divmod(h, 2)
        attended = loc[h] + matmul(qeff[h], states[h])
        back = lax.rsqrt(jnp.mean(attended * attended, -1, keepdims=True) + EPSILON)
        gate = out_gate[g, :, r * HEAD : (r + 1) * HEAD]
        hidden.append((attended * back * gain * gate).astype(BF16))
    hidden = jnp.concatenate(hidden, 1)

    def partial_for(r, core):
        columns = pl.ds(pl.multiple_of(core * FEATURES, FEATURES), FEATURES)
        return matmul(hidden, w_out[CHIPS.index(r), :, columns])

    def sibling_copy(r):
        return remote(sib_out.at[r], sib_in.at[r], sib_send.at[r], sib_recv.at[r], sibling)

    ring = {
        r: remote(ring_out.at[r - 1], ring_in.at[r - 1], ring_send.at[r - 1], ring_recv.at[r - 1], device)
        for r, device in ((1, above), (2, across), (3, below))
    }
    for copy in load_out:
        copy.wait()
    def send_sibling(r):
        sib_out[r] = partial_for(r, 1 - c).astype(BF16)
        sibling_copy(r).start()

    def send_ring(r):
        mine = partial_for(r, c)
        sibling_copy(r).wait_recv()
        ring_out[r - 1] = (mine + sib_in[r].astype(F32)).astype(BF16)
        ring[r].start()

    send_sibling(2)
    send_sibling(1)
    send_ring(2)
    send_sibling(3)
    send_ring(1)
    send_ring(3)
    send_sibling(0)
    total = partial_for(0, c)
    sibling_copy(0).wait_recv()
    total = total + sib_in[0].astype(F32)
    for r in (1, 3, 2):
        ring[r].wait_recv()
        total = total + ring_in[r - 1].astype(F32)
    out_ref[...] = total.astype(BF16)

    finish()
    for r in range(NY):
        sibling_copy(r).wait_send()
    for copy in ring.values():
        copy.wait_send()


def per_device(
    tokens,
    in_weight,
    gate_weight,
    conv_weight,
    decay_scale,
    dt_bias,
    beta_shift,
    norm_gain,
    out_weight,
):
    anywhere = pl.BlockSpec(memory_space=pltpu.HBM)
    vmem = pl.BlockSpec(memory_space=pltpu.VMEM)
    dma = pltpu.SemaphoreType.DMA
    return pl.pallas_call(
        kernel,
        out_shape=pltpu.VMEM((ROWS, FEATURES), BF16),
        in_specs=[anywhere] * 9,
        out_specs=vmem,
        scratch_shapes=[
            pltpu.VMEM((2 * VALUE_HEADS, 8 * FEATURES), BF16),
            pltpu.VMEM((4, GROUPS, CONV), BF16),
            pltpu.SMEM((VALUE_HEADS,), F32),
            pltpu.SMEM((VALUE_HEADS,), F32),
            pltpu.SMEM((VALUE_HEADS,), F32),
            pltpu.VMEM((1, HEAD), F32),
            pltpu.VMEM((NY, 2, ROWS, FEATURES), BF16),
            pltpu.VMEM((NY, 2 * FEATURES, GROUPS * GROUP), BF16),
            pltpu.VMEM((NY, VALUE_HEADS * HEAD, 2 * FEATURES), BF16),
            pltpu.VMEM((TILES, ROWS, 256), F32),
            pltpu.VMEM((8, 8 + ROWS, HEAD), F32),
            pltpu.VMEM((HALO, GROUPS * CONV), BF16),
            pltpu.VMEM((HALO, GROUPS * CONV), BF16),
            pltpu.VMEM((2, ROWS, HEAD), F32),
            pltpu.VMEM((GROUPS, ROWS, HEAD), BF16),
            pltpu.VMEM((GROUPS, ROWS, HEAD), BF16),
            pltpu.VMEM((VALUE_HEADS, ROWS, HEAD), BF16),
            pltpu.VMEM((VALUE_HEADS, HEAD, 2 * HEAD), BF16),
            pltpu.VMEM((2, NX, HEAD, 2 * HEAD), BF16),
            pltpu.VMEM((2, NX - 1, HEAD, 2 * HEAD), F32),
            pltpu.VMEM((2, 2, HEAD, HEAD), BF16),
            pltpu.VMEM((2, 2, HEAD, HEAD), BF16),
            pltpu.VMEM((2, 2, HEAD, HEAD), BF16),
            pltpu.VMEM((2, 2, HEAD, HEAD), BF16),
            pltpu.VMEM((2, HEAD, HEAD), BF16),
            pltpu.VMEM((2, HEAD, HEAD), BF16),
            pltpu.VMEM((2, HEAD, HEAD), F32),
            pltpu.VMEM((GROUPS, ROWS, 2 * HEAD), F32),
            pltpu.VMEM((VALUE_HEADS, len(BLOCKS), HEAD, HEAD), F32),
            pltpu.VMEM((2, NX, HEAD, HEAD), BF16),
            pltpu.VMEM((VALUE_HEADS, HEAD, HEAD), BF16),
            pltpu.VMEM((VALUE_HEADS, ROWS, HEAD), F32),
            pltpu.VMEM((VALUE_HEADS, ROWS, HEAD), BF16),
            pltpu.VMEM((NY, ROWS, FEATURES), BF16),
            pltpu.VMEM((NY, ROWS, FEATURES), BF16),
            pltpu.VMEM((NY - 1, ROWS, FEATURES), BF16),
            pltpu.VMEM((NY - 1, ROWS, FEATURES), BF16),
            dma,
            dma((6,)),
            dma((NY,)),
            dma((NY,)),
            dma((7,)),
            dma((NY, 2)),
            dma((7,)),
            dma((NY, 2)),
            dma((2,)),
            dma((NX,)),
            dma((2, NX)),
            dma((2,)),
            dma((2,)),
            dma((2,)),
            dma((2,)),
            dma((2, 4)),
            dma((2,)),
            pltpu.SemaphoreType.REGULAR,
            pltpu.SemaphoreType.REGULAR,
            dma((2, NX)),
            dma((NX,)),
            dma((NY,)),
            dma((NY,)),
            dma((NY - 1,)),
            dma((NY - 1,)),
        ],
        compiler_params=pltpu.CompilerParams(
            collective_id=0, has_side_effects=True, vmem_limit_bytes=60 * 1024 * 1024
        ),
    )(
        tokens,
        in_weight,
        gate_weight.T,
        conv_weight,
        decay_scale,
        dt_bias,
        beta_shift,
        norm_gain.reshape(1, HEAD),
        out_weight,
    )


def solution(mesh):
    in_specs = (
        P("seq", "head"),
        P(None, "head"),
        P(None, "head"),
        P(None, "head", None),
        P("head"),
        P("head"),
        P("head"),
        P(),
        P("head", None),
    )
    out_specs = P("seq", "head")
    return jax.shard_map(
        per_device, mesh=mesh, in_specs=in_specs, out_specs=out_specs, check_vma=False
    )
```

```python
import functools

import jax
import jax.numpy as jnp
from jax import lax
from jax.experimental import pallas as pl
from jax.experimental.pallas import tpu as pltpu
from jax.sharding import PartitionSpec as P

F32 = jnp.float32
BF16 = jnp.bfloat16
EPSILON = 1e-06

ROWS = 256
HEAD = 128
FEATURES = 256
GROUPS = 2
VALUE_HEADS = 4
BLOCKS = ((0, 0), (1, 0), (1, 1))
TILES = 6
CONV = 512
GROUP = 768
HALO = 16
NX = 4
NZ = 8
NY = 4

CHIPS = (0, 1, 3, 2)


def matmul(a, b):
    return jnp.dot(a, b, preferred_element_type=F32)


def matmul_t(a, b):
    return lax.dot_general(a, b, (((1,), (1,)), ((), ())), preferred_element_type=F32)


def silu(v):
    return 0.5 * v * (1.0 + jnp.tanh(0.5 * v))


def kernel(
    tokens_hbm,
    in_weight_hbm,
    gate_weight_hbm,
    conv_weight_hbm,
    decay_scale_hbm,
    dt_bias_hbm,
    beta_shift_hbm,
    norm_gain_hbm,
    out_weight_hbm,
    out_ref,
    gate_weight,
    conv_weight,
    decay_scale,
    dt_bias,
    beta_shift,
    norm_gain,
    tok,
    w_in,
    w_out,
    acc,
    ext,
    halo_out,
    halo_in,
    gates,
    qn,
    kn,
    vn,
    maps,
    row_maps,
    prefix,
    row_total,
    total_in,
    pair_in,
    pair_out,
    state_in,
    state_out,
    state_before,
    out_gate,
    decays,
    row_states,
    states,
    loc,
    qeff,
    sib_out,
    sib_in,
    ring_out,
    ring_in,
    load_sem,
    small_sem,
    win_sem,
    wout_sem,
    tok_send,
    tok_recv,
    tail_send,
    tail_recv,
    halo_sem,
    row_send,
    row_recv,
    total_send,
    total_recv,
    pair_send,
    pair_recv,
    state_send,
    state_recv,
    ready_sem,
    halo_ready_sem,
    back_send,
    back_recv,
    sib_send,
    sib_recv,
    ring_send,
    ring_recv,
):
    seq = lax.axis_index("seq")
    head = lax.axis_index("head")
    z, x = lax.div(seq, NX), lax.rem(seq, NX)
    y, c = lax.div(head, 2), lax.rem(head, 2)

    def chip_at(r):
        return lax.rem(y + r, NY)

    above = (seq, chip_at(1) * 2 + 1 - c)
    below = (seq, chip_at(3) * 2 + 1 - c)
    across = (seq, chip_at(2) * 2 + 1 - c)
    sibling = (seq, y * 2 + 1 - c)

    def remote(src, dst, send, recv, device):
        return pltpu.make_async_remote_copy(
            src_ref=src,
            dst_ref=dst,
            send_sem=send,
            recv_sem=recv,
            device_id=device,
            device_id_type=pl.DeviceIdType.MESH,
        )

    load_tok = pltpu.make_async_copy(tokens_hbm, tok.at[0, c], load_sem)
    load_tok.start()

    barrier = pltpu.get_barrier_semaphore()
    owner = c == 1

    def row_device(r, core):
        return (z * NX + lax.rem(x + r, NX), y * 2 + core)

    def column_device(there):
        return (there * NX + x, head)

    def signal(semaphore, device):
        pl.semaphore_signal(semaphore, inc=1, device_id=device, device_id_type=pl.DeviceIdType.MESH)

    odd = lax.rem(z, 2) == 1
    even = jnp.logical_not(odd)
    both_of = jnp.logical_and
    last_x = x == NX - 1
    not_top = z < NZ - 1
    for device in [above, below, across, sibling] + [row_device(r, 1) for r in range(1, NX)]:
        signal(barrier, device)
    for r in range(1, NX):
        pl.when(owner)(functools.partial(signal, barrier, row_device(r, 0)))

    pl.when(both_of(owner, even))(functools.partial(signal, barrier, column_device(z + 1)))
    for d in (1, 2):
        pl.when(both_of(owner, both_of(odd, not_top)))(functools.partial(signal, barrier, column_device(z + d)))
    pl.when(both_of(owner, z == 4))(functools.partial(signal, barrier, column_device(z + 2)))
    for d in (3, 4):
        pl.when(both_of(owner, z == 3))(functools.partial(signal, barrier, column_device(z + d)))

    @pl.when(both_of(c == 0, both_of(last_x, not_top)))
    def _():
        signal(barrier, ((z + 1) * NX + x, y * 2 + 1))

    def pair_of(r):
        return pl.ds(pl.multiple_of(chip_at(r) * 2 * FEATURES, 2 * FEATURES), 2 * FEATURES)

    load_in, load_out, load_small = [], [], []
    for i, r in enumerate(CHIPS):
        load_in.append(pltpu.make_async_copy(in_weight_hbm.at[pair_of(r)], w_in.at[i], win_sem.at[i]))
        load_out.append(
            pltpu.make_async_copy(out_weight_hbm.at[:, pair_of(r)], w_out.at[i], wout_sem.at[i])
        )
    for i, (source, target) in enumerate(
        (
            (gate_weight_hbm, gate_weight),
            (conv_weight_hbm, conv_weight),
            (decay_scale_hbm, decay_scale),
            (dt_bias_hbm, dt_bias),
            (beta_shift_hbm, beta_shift),
            (norm_gain_hbm, norm_gain),
        )
    ):
        load_small.append(pltpu.make_async_copy(source, target, small_sem.at[i]))
    for copy in load_in:
        copy.start()

    greeted = 7 + jnp.where(owner, 3 + lax.rem(z, 2) + jnp.where(z >= 2, 1, 0) + jnp.where(z >= 6, 1, 0) + jnp.where(z == 6, 1, 0), 0)
    greeted = greeted + jnp.where(both_of(owner, both_of(last_x, z > 0)), 1, 0)
    pl.semaphore_wait(barrier, greeted)

    pl.when(both_of(owner, odd))(functools.partial(signal, ready_sem, column_device(z - 1)))
    pl.when(both_of(owner, both_of(z >= 2, z < 4)))(functools.partial(signal, ready_sem, column_device(1)))
    pl.when(both_of(owner, z >= 4))(functools.partial(signal, ready_sem, column_device(3)))
    pl.when(both_of(owner, z >= 6))(functools.partial(signal, ready_sem, column_device(5)))
    pl.when(both_of(owner, z == 6))(functools.partial(signal, ready_sem, column_device(4)))

    @pl.when(both_of(owner, both_of(last_x, z > 0)))
    def _():
        for core in range(2):
            signal(halo_ready_sem, ((z - 1) * NX + x, y * 2 + core))

    load_tok.wait()

    pending = []

    def finish():
        for wait in pending:
            wait()

    sends = []

    body, tail = pl.ds(0, ROWS - HALO), pl.ds(ROWS - HALO, HALO)

    def send_tok(source, target, core, device):
        copy = remote(
            tok.at[source, core, body],
            tok.at[target, core, body],
            tok_send.at[len(sends)],
            tok_recv.at[target, core],
            device,
        )
        copy.start()
        sends.append(copy)

    def send_tail(n, source, target, core, device):
        copy = remote(
            tok.at[source, core, tail],
            tok.at[target, core, tail],
            tail_send.at[n],
            tail_recv.at[target, core],
            device,
        )
        copy.start()
        pending.append(copy.wait_send)

    def wait_tok(i, core):
        remote(
            tok.at[i, core, body], tok.at[i, core, body], tok_send.at[0], tok_recv.at[i, core], sibling
        ).wait_recv()

    up, down, far = CHIPS.index(1), CHIPS.index(3), CHIPS.index(2)
    away = ((down, above), (up, below), (far, across), (0, sibling))
    for n, (target, device) in enumerate(away):
        send_tail(n, 0, target, c, device)
    for target, device in away:
        send_tok(0, target, c, device)
    for copy in load_small + load_out:
        copy.start()

    def tokens_of(i):
        return jnp.concatenate([tok[i, 0], tok[i, 1]], 1)

    def project(chips, start):
        def tile(j, carry):
            columns = pl.ds(pl.multiple_of(j * 256, 256), 256)
            part = jnp.zeros((ROWS, 256), F32) if start else acc[j]
            for i in chips:
                part = part + matmul(tokens_of(i), w_in[i, :, columns])
            acc[j] = part
            return carry

        lax.fori_loop(0, TILES, tile, 0)

    def wait_tail(i, core):
        remote(
            tok.at[i, core, tail], tok.at[i, core, tail], tail_send.at[0], tail_recv.at[i, core], sibling
        ).wait_recv()

    wait_tail(0, 1 - c)
    wait_tok(0, 1 - c)
    load_in[0].wait()
    project((0,), True)
    for n, i in enumerate((up, down, far)):
        wait_tail(i, 1 - c)
        send_tail(4 + n, i, i, 1 - c, sibling)
    for i in (up, down, far):
        wait_tail(i, c)
    for i in (up, down, far):
        load_in[i].wait()
    for g in range(GROUPS):
        for n in range(2):
            columns = pl.ds((3 * g + n) * 256, 256)
            part = jnp.zeros((HALO, 256), F32)
            for i in range(NY):
                rows = jnp.concatenate([tok[i, 0, tail], tok[i, 1, tail]], 1)
                part = part + matmul(rows, w_in[i, :, columns])
            halo_out[:, (2 * g + n) * 256 : (2 * g + n + 1) * 256] = part.astype(BF16)

    for i in (down, up):
        wait_tok(i, 1 - c)
        send_tok(i, i, 1 - c, sibling)

    next_seq = lax.rem(seq + 1, NX * NZ)
    send_halo = remote(halo_out, halo_in, halo_sem.at[0], halo_sem.at[1], (next_seq, head))

    @pl.when(jnp.logical_and(last_x, not_top))
    def _():
        pl.semaphore_wait(halo_ready_sem, 1)

    pl.when(seq < NX * NZ - 1)(send_halo.start)
    pending.append(lambda: pl.when(seq < NX * NZ - 1)(send_halo.wait_send))
    wait_tok(down, c)
    wait_tok(up, c)
    project((up, down), False)
    for copy in load_small:
        copy.wait()

    def gating_of(i):
        weight = gate_weight[:, pair_of(CHIPS[i])]
        weight = jnp.concatenate([weight, jnp.zeros((HEAD - weight.shape[0], 2 * FEATURES), BF16)], 0)
        return matmul_t(tokens_of(i), weight)

    gating = gating_of(0) + gating_of(up) + gating_of(down)
    wait_tok(far, 1 - c)
    send_tok(far, far, 1 - c, sibling)
    wait_tok(far, c)
    pending.extend(copy.wait_send for copy in sends)

    for g in range(GROUPS):
        for n in range(2):
            j = 3 * g + n
            part = acc[j] + matmul(tokens_of(far), w_in[far, :, j * 256 : (j + 1) * 256])
            for block in range(2):
                columns = part[:, block * HEAD : (block + 1) * HEAD].astype(BF16)
                ext[4 * g + 2 * n + block, 8:, :] = columns.astype(F32)

    gating = gating + gating_of(far)
    lane = lax.broadcasted_iota(jnp.int32, (1, HEAD), 1)
    shift = jnp.zeros((1, HEAD), F32)
    bias = jnp.zeros((1, HEAD), F32)
    scale = jnp.zeros((1, HEAD), F32)
    for h in range(VALUE_HEADS):
        g, r = divmod(h, 2)
        shift = jnp.where(lane == 4 * g + r, beta_shift[h], shift)
        bias = jnp.where(lane == 4 * g + 2 + r, dt_bias[h], bias)
        scale = jnp.where(lane == 4 * g + 2 + r, decay_scale[h], scale)
    strength = jax.nn.sigmoid(gating - shift)
    shifted = gating + bias
    softplus = jnp.maximum(shifted, 0.0) + jnp.log1p(jnp.exp(-jnp.abs(shifted)))
    log_gate = -scale * softplus
    row_id = lax.broadcasted_iota(jnp.int32, (ROWS, ROWS), 0)
    col_id = lax.broadcasted_iota(jnp.int32, (ROWS, ROWS), 1)
    ones = jnp.where(col_id <= row_id, 1.0, 0.0).astype(BF16)
    cumulative = jnp.zeros((ROWS, HEAD), F32)
    rest = log_gate
    for _ in range(3):
        piece = rest.astype(BF16)
        cumulative = cumulative + matmul(ones, piece)
        rest = rest - piece.astype(F32)
    cumulative_t = jnp.transpose(cumulative)
    gates[0] = strength
    gates[1] = cumulative

    def convolve(first, count):
        for g in range(GROUPS):
            for block in range(CONV // HEAD):
                total = jnp.zeros((count, HEAD), F32)
                for tap in range(4):
                    weight = conv_weight[tap, g : g + 1, block * HEAD : (block + 1) * HEAD].astype(F32)
                    total = total + weight * ext[4 * g + block, pl.ds(first + 5 + tap, count), :]
                value = silu(total)
                rows = pl.ds(first, count)
                if block < 2:
                    norm = lax.rsqrt(jnp.sum(value * value, -1, keepdims=True) + EPSILON)
                    if block == 0:
                        qn[g, rows, :] = (value * (norm * HEAD**-0.5)).astype(BF16)
                    else:
                        kn[g, rows, :] = (value * norm).astype(BF16)
                else:
                    vn[2 * g + block - 2, rows, :] = value.astype(BF16)

    pl.when(seq > 0)(send_halo.wait_recv)

    @pl.when(seq == 0)
    def _():
        halo_in[...] = jnp.zeros_like(halo_in)

    for block in range(8):
        ext[block, 0:8, :] = halo_in[:, block * HEAD : (block + 1) * HEAD].astype(F32)[HALO - 8 :]
    convolve(0, ROWS)
    for g in range(GROUPS):
        j = 3 * g + 2
        part = acc[j] + matmul(tokens_of(far), w_in[far, :, j * 256 : (j + 1) * 256])
        out_gate[g] = silu(part.astype(BF16).astype(F32))
    row = lax.broadcasted_iota(jnp.int32, (HEAD, HEAD), 0)
    col = lax.broadcasted_iota(jnp.int32, (HEAD, HEAD), 1)
    on_lower = col <= row
    below_diag = col < row
    for h in range(VALUE_HEADS):
        g, r = divmod(h, 2)
        lane_c = 4 * g + 2 + r
        cum = cumulative[:, lane_c : lane_c + 1]
        cum_t = cumulative_t[lane_c : lane_c + 1, :]
        for n, (i, j) in enumerate(BLOCKS):
            gap = cum[i * HEAD : (i + 1) * HEAD] - cum_t[:, j * HEAD : (j + 1) * HEAD]
            if i == j:
                decays[h, n] = jnp.where(on_lower, jnp.exp(jnp.where(on_lower, gap, 0.0)), 0.0)
            else:
                decays[h, n] = jnp.exp(gap)


    unit = jnp.where(col == row, 1.0, 0.0)
    unit_b = unit.astype(BF16)
    def within(wide, narrow):
        keep = (lax.div(row, wide) == lax.div(col, wide)) & (lax.div(row, narrow) != lax.div(col, narrow))
        return jnp.where(keep & below_diag, 1.0, 0.0).astype(BF16)

    masks = [within(4 * b, b) for b in (2, 8, 32)]

    parts = [pl.ds(0, HEAD), pl.ds(HEAD, HEAD)]
    inner = []
    for g in range(GROUPS):
        inner.append(matmul_t(kn[g], kn[g]))
    systems = []
    for h in range(VALUE_HEADS):
        g, r = divmod(h, 2)
        lane_b, lane_c = 4 * g + r, 4 * g + 2 + r
        beta = gates[0][:, lane_b : lane_b + 1]
        system = {}
        for n, (i, j) in enumerate(BLOCKS):
            ri, cj = slice(i * HEAD, (i + 1) * HEAD), slice(j * HEAD, (j + 1) * HEAD)
            ratio = decays[h, n]
            system[i, j] = (beta[ri] * ratio * inner[g][ri, cj]).astype(BF16)
        systems.append(system)
    keys = [(h, i) for h in range(VALUE_HEADS) for i in range(2)]
    pairs = within(2, 1)
    inverses = {key: unit_b - pairs * systems[key[0]][key[1], key[1]] for key in keys}
    for mask in masks:
        moved = {k: matmul(inverses[k], mask * systems[k[0]][k[1], k[1]]).astype(BF16) for k in keys}
        once = {k: inverses[k].astype(F32) - matmul(moved[k], inverses[k]) for k in keys}
        twice = {k: matmul(moved[k], moved[k]).astype(BF16) for k in keys}
        inverses = {k: (once[k] + matmul(twice[k], once[k].astype(BF16))).astype(BF16) for k in keys}

    solved = []
    for h in range(VALUE_HEADS):
        g, r = divmod(h, 2)
        lane_b, lane_c = 4 * g + r, 4 * g + 2 + r
        beta = gates[0][:, lane_b : lane_b + 1]
        cum = gates[1][:, lane_c : lane_c + 1]
        right = jnp.concatenate(
            [beta * jnp.exp(cum) * kn[g].astype(F32), beta * vn[h].astype(F32)], 1
        )
        first = matmul(inverses[h, 0], right[:HEAD].astype(BF16)).astype(BF16)
        across_parts = matmul(inverses[h, 1], systems[h][1, 0]).astype(BF16)
        second = matmul(inverses[h, 1], right[HEAD:].astype(BF16))
        second = (second - matmul(across_parts, first)).astype(BF16)
        both = jnp.concatenate([first, second], 0)
        solved.append(both)
        last = cum[ROWS - 1 :, :]
        end_keys = (jnp.exp(last - cum) * kn[g].astype(F32)).astype(BF16)
        grown = lax.dot_general(end_keys, both, (((0,), (0,)), ((), ())), preferred_element_type=F32)
        change = (jnp.exp(last) - 1.0) * unit - grown[:, :HEAD]
        maps[h] = jnp.concatenate([change, grown[:, HEAD:]], 1).astype(BF16)
        stays = jnp.logical_and(x == h, owner)
        row_copy = remote(
            maps.at[h], row_maps.at[c, x], row_send.at[h], row_recv.at[c, x], (z * NX + h, y * 2 + 1)
        )
        pl.when(jnp.logical_not(stays))(row_copy.start)
        pending.append(functools.partial(pl.when(jnp.logical_not(stays)), row_copy.wait_send))

        @pl.when(stays)
        def _():
            row_maps[1, h] = maps[h]

    inner = [matmul_t(qn[g], kn[g]) for g in range(GROUPS)]
    for h in range(VALUE_HEADS):
        g, r = divmod(h, 2)
        lane_c = 4 * g + 2 + r
        cum = gates[1][:, lane_c : lane_c + 1]
        score = {}
        for n, (i, j) in enumerate(BLOCKS):
            ri, cj = slice(i * HEAD, (i + 1) * HEAD), slice(j * HEAD, (j + 1) * HEAD)
            score[i, j] = (decays[h, n] * inner[g][ri, cj]).astype(BF16)
        top = matmul(score[0, 0], solved[h][:HEAD])
        low = matmul(jnp.concatenate([score[1, 0], score[1, 1]], 1), solved[h])
        out = jnp.concatenate([top, low], 0)
        qeff[h] = (jnp.exp(cum) * qn[g].astype(F32) - out[:, :HEAD]).astype(BF16)
        loc[h] = out[:, HEAD:]

    def compose(later, earlier):
        return earlier + later + matmul(later[:, :HEAD].astype(BF16), earlier.astype(BF16))

    def apply(change, shift, before):
        return before + shift.astype(F32) + matmul(change, before.astype(BF16))

    def total_copy(k):
        return remote(row_total.at[k], total_in.at[k], total_send.at[k], total_recv.at[k], column_device(z + 1))

    def shift_copy(k):
        return remote(
            row_total.at[k, 1], total_in.at[k, 1], total_send.at[k], total_recv.at[k], column_device(z + 1)
        )

    def skip_copy(k):
        return remote(row_total.at[k], pair_in.at[k], pair_send.at[k], pair_recv.at[k], column_device(z + 2))

    def pair_copy(k):
        return remote(pair_out.at[k], pair_in.at[k], pair_send.at[k], pair_recv.at[k], column_device(z + 2))

    def state_copy(d, k):
        return remote(
            state_out.at[k], state_in.at[k], state_send.at[k, d - 1], state_recv.at[k], column_device(z + d)
        )

    def back_copy(core, i):
        return remote(
            row_states.at[core, i], states.at[x], back_send.at[core, i], back_recv.at[x], (z * NX + i, y * 2 + core)
        )

    def leaves(core, i):
        return jnp.logical_not(jnp.logical_and(core == 1, x == i))

    @pl.when(owner)
    def _():
        answers = jnp.where(jnp.logical_or(odd, z == 4), 2, 1)

        @pl.when(z != 7)
        def _():
            pl.semaphore_wait(ready_sem, jnp.where(z == 3, 4, answers))


        for core in range(2):
            for i in range(NX):
                row_copy = remote(
                    maps.at[0], row_maps.at[core, i], row_send.at[0], row_recv.at[core, i], sibling
                )
                pl.when(leaves(core, i))(row_copy.wait_recv)
        row_map = [[row_maps[core, i].astype(F32) for i in range(NX)] for core in range(2)]
        first_two = [compose(row_map[core][1], row_map[core][0]) for core in range(2)]
        last_two = [compose(row_map[core][3], row_map[core][2]) for core in range(2)]
        for core in range(2):
            total = compose(last_two[core], first_two[core]).astype(BF16)
            row_total[core, 0] = total[:, :HEAD]
            row_total[core, 1] = total[:, HEAD:]
        for core in range(2):
            pl.when(z == 0)(shift_copy(core).start)
            pl.when(both_of(z > 0, jnp.logical_or(even, z == 5)))(total_copy(core).start)
        for core in range(2):
            pl.when(z == 4)(skip_copy(core).start)
        for core in range(2):
            prefix[core, 0] = row_map[core][0]
            prefix[core, 1] = first_two[core]
            prefix[core, 2] = compose(row_map[core][2], first_two[core])

        def joined(ref, k):
            return jnp.concatenate([ref[k, 0], ref[k, 1]], 1).astype(F32)

        @pl.when(z == 0)
        def _():
            state_before[...] = jnp.zeros_like(state_before)

        @pl.when(z == 1)
        def _():
            for core in range(2):
                shift_copy(core).wait_recv()
                shift = total_in[core, 1].astype(F32)
                state_before[core] = shift
                state_out[core] = apply(row_total[core, 0], row_total[core, 1], shift).astype(BF16)
                state_copy(2, core).start()
                state_copy(1, core).start()

        @pl.when(both_of(even, both_of(z > 0, z < 6)))
        def _():
            for core in range(2):
                state_copy(1, core).wait_recv()
                state_before[core] = state_in[core].astype(F32)

        @pl.when(both_of(odd, both_of(z > 1, z < 6)))
        def _():
            for core in range(2):
                total_copy(core).wait_recv()
                pair = compose(joined(row_total, core), joined(total_in, core)).astype(BF16)
                pair_out[core, 0] = pair[:, :HEAD]
                pair_out[core, 1] = pair[:, HEAD:]
                pl.when(z == 5)(pair_copy(core).start)
            for core in range(2):
                state_copy(1, core).wait_recv()
                state = state_in[core].astype(F32)

                @pl.when(z == 3)
                def _():
                    state_out[core] = apply(pair_out[core, 0], pair_out[core, 1], state).astype(BF16)
                    for d in (4, 3, 2, 1):
                        state_copy(d, core).start()

                state_before[core] = apply(total_in[core, 0], total_in[core, 1], state)

        @pl.when(z == 6)
        def _():
            both = []
            for core in range(2):
                pair_copy(core).wait_recv()
                total_copy(core).wait_recv()
                both.append(compose(joined(total_in, core), joined(pair_in, core)))
            for core in range(2):
                state_copy(1, core).wait_recv()
                change = both[core][:, :HEAD].astype(BF16)
                state_before[core] = apply(change, both[core][:, HEAD:], state_in[core].astype(F32))

        @pl.when(z == 7)
        def _():
            for core in range(2):
                state_copy(1, core).wait_recv()
                pair_copy(core).wait_recv()
                total_copy(core).wait_recv()
                state = apply(pair_in[core, 0], pair_in[core, 1], state_in[core].astype(F32))
                state_before[core] = apply(total_in[core, 0], total_in[core, 1], state)

        for core in range(2):
            state = state_before[core]
            row_states[core, 0] = state.astype(BF16)
            pl.when(leaves(core, 0))(back_copy(core, 0).start)
            for i in range(1, NX):
                before_i = prefix[core, i - 1]
                row_states[core, i] = apply(
                    before_i[:, :HEAD].astype(BF16), before_i[:, HEAD:], state
                ).astype(BF16)
            for i in range(1, NX):
                pl.when(leaves(core, i))(back_copy(core, i).start)
        states[pl.ds(x, 1)] = row_states[1, pl.ds(x, 1)]

    def wait_owner():
        for core in range(2):
            pl.when(z == 0)(shift_copy(core).wait_send)
            pl.when(both_of(z > 0, jnp.logical_or(even, z == 5)))(total_copy(core).wait_send)
            pl.when(z == 4)(skip_copy(core).wait_send)
            pl.when(z == 5)(pair_copy(core).wait_send)
            for d in (1, 2):
                pl.when(z == 1)(state_copy(d, core).wait_send)
            for d in range(1, 5):
                pl.when(z == 3)(state_copy(d, core).wait_send)
        for core in range(2):
            for i in range(NX):
                pl.when(leaves(core, i))(back_copy(core, i).wait_send)

    pending.append(lambda: pl.when(owner)(wait_owner))
    for h in range(VALUE_HEADS):
        arrival = remote(
            row_states.at[0, 0], states.at[h], back_send.at[0, 0], back_recv.at[h], sibling
        )
        pl.when(jnp.logical_not(jnp.logical_and(owner, x == h)))(arrival.wait_recv)

    gain = norm_gain[...]
    hidden = []
    for h in range(VALUE_HEADS):
        g, r = divmod(h, 2)
        attended = loc[h] + matmul(qeff[h], states[h])
        back = lax.rsqrt(jnp.mean(attended * attended, -1, keepdims=True) + EPSILON)
        gate = out_gate[g, :, r * HEAD : (r + 1) * HEAD]
        hidden.append((attended * back * gain * gate).astype(BF16))
    hidden = jnp.concatenate(hidden, 1)

    def partial_for(r, core):
        columns = pl.ds(pl.multiple_of(core * FEATURES, FEATURES), FEATURES)
        return matmul(hidden, w_out[CHIPS.index(r), :, columns])

    def sibling_copy(r):
        return remote(sib_out.at[r], sib_in.at[r], sib_send.at[r], sib_recv.at[r], sibling)

    ring = {
        r: remote(ring_out.at[r - 1], ring_in.at[r - 1], ring_send.at[r - 1], ring_recv.at[r - 1], device)
        for r, device in ((1, above), (2, across), (3, below))
    }
    for copy in load_out:
        copy.wait()
    def send_sibling(r):
        sib_out[r] = partial_for(r, 1 - c if r == 0 else c).astype(BF16)
        sibling_copy(r).start()

    def send_ring(r):
        mine = partial_for(r, 1 - c)
        sibling_copy(r).wait_recv()
        ring_out[r - 1] = (mine + sib_in[r].astype(F32)).astype(BF16)
        ring[r].start()

    send_sibling(2)
    send_sibling(1)
    send_ring(2)
    send_sibling(3)
    send_ring(1)
    send_ring(3)
    send_sibling(0)
    total = partial_for(0, c)
    sibling_copy(0).wait_recv()
    total = total + sib_in[0].astype(F32)
    finish()
    for r in (2, 1, 3):
        ring[r].wait_recv()
        total = total + ring_in[r - 1].astype(F32)
    out_ref[...] = total.astype(BF16)

    for r in range(NY):
        sibling_copy(r).wait_send()
    for copy in ring.values():
        copy.wait_send()


def per_device(
    tokens,
    in_weight,
    gate_weight,
    conv_weight,
    decay_scale,
    dt_bias,
    beta_shift,
    norm_gain,
    out_weight,
):
    anywhere = pl.BlockSpec(memory_space=pltpu.HBM)
    vmem = pl.BlockSpec(memory_space=pltpu.VMEM)
    dma = pltpu.SemaphoreType.DMA
    return pl.pallas_call(
        kernel,
        out_shape=pltpu.VMEM((ROWS, FEATURES), BF16),
        in_specs=[anywhere] * 9,
        out_specs=vmem,
        scratch_shapes=[
            pltpu.VMEM((2 * VALUE_HEADS, 8 * FEATURES), BF16),
            pltpu.VMEM((4, GROUPS, CONV), BF16),
            pltpu.SMEM((VALUE_HEADS,), F32),
            pltpu.SMEM((VALUE_HEADS,), F32),
            pltpu.SMEM((VALUE_HEADS,), F32),
            pltpu.VMEM((1, HEAD), F32),
            pltpu.VMEM((NY, 2, ROWS, FEATURES), BF16),
            pltpu.VMEM((NY, 2 * FEATURES, GROUPS * GROUP), BF16),
            pltpu.VMEM((NY, VALUE_HEADS * HEAD, 2 * FEATURES), BF16),
            pltpu.VMEM((TILES, ROWS, 256), F32),
            pltpu.VMEM((8, 8 + ROWS, HEAD), F32),
            pltpu.VMEM((HALO, GROUPS * CONV), BF16),
            pltpu.VMEM((HALO, GROUPS * CONV), BF16),
            pltpu.VMEM((2, ROWS, HEAD), F32),
            pltpu.VMEM((GROUPS, ROWS, HEAD), BF16),
            pltpu.VMEM((GROUPS, ROWS, HEAD), BF16),
            pltpu.VMEM((VALUE_HEADS, ROWS, HEAD), BF16),
            pltpu.VMEM((VALUE_HEADS, HEAD, 2 * HEAD), BF16),
            pltpu.VMEM((2, NX, HEAD, 2 * HEAD), BF16),
            pltpu.VMEM((2, NX - 1, HEAD, 2 * HEAD), F32),
            pltpu.VMEM((2, 2, HEAD, HEAD), BF16),
            pltpu.VMEM((2, 2, HEAD, HEAD), BF16),
            pltpu.VMEM((2, 2, HEAD, HEAD), BF16),
            pltpu.VMEM((2, 2, HEAD, HEAD), BF16),
            pltpu.VMEM((2, HEAD, HEAD), BF16),
            pltpu.VMEM((2, HEAD, HEAD), BF16),
            pltpu.VMEM((2, HEAD, HEAD), F32),
            pltpu.VMEM((GROUPS, ROWS, 2 * HEAD), F32),
            pltpu.VMEM((VALUE_HEADS, len(BLOCKS), HEAD, HEAD), F32),
            pltpu.VMEM((2, NX, HEAD, HEAD), BF16),
            pltpu.VMEM((VALUE_HEADS, HEAD, HEAD), BF16),
            pltpu.VMEM((VALUE_HEADS, ROWS, HEAD), F32),
            pltpu.VMEM((VALUE_HEADS, ROWS, HEAD), BF16),
            pltpu.VMEM((NY, ROWS, FEATURES), BF16),
            pltpu.VMEM((NY, ROWS, FEATURES), BF16),
            pltpu.VMEM((NY - 1, ROWS, FEATURES), BF16),
            pltpu.VMEM((NY - 1, ROWS, FEATURES), BF16),
            dma,
            dma((6,)),
            dma((NY,)),
            dma((NY,)),
            dma((7,)),
            dma((NY, 2)),
            dma((7,)),
            dma((NY, 2)),
            dma((2,)),
            dma((NX,)),
            dma((2, NX)),
            dma((2,)),
            dma((2,)),
            dma((2,)),
            dma((2,)),
            dma((2, 4)),
            dma((2,)),
            pltpu.SemaphoreType.REGULAR,
            pltpu.SemaphoreType.REGULAR,
            dma((2, NX)),
            dma((NX,)),
            dma((NY,)),
            dma((NY,)),
            dma((NY - 1,)),
            dma((NY - 1,)),
        ],
        compiler_params=pltpu.CompilerParams(
            collective_id=0, has_side_effects=True, vmem_limit_bytes=60 * 1024 * 1024
        ),
    )(
        tokens,
        in_weight,
        gate_weight.T,
        conv_weight,
        decay_scale,
        dt_bias,
        beta_shift,
        norm_gain.reshape(1, HEAD),
        out_weight,
    )


def solution(mesh):
    in_specs = (
        P("seq", "head"),
        P(None, "head"),
        P(None, "head"),
        P(None, "head", None),
        P("head"),
        P("head"),
        P("head"),
        P(),
        P("head", None),
    )
    out_specs = P("seq", "head")
    return jax.shard_map(
        per_device, mesh=mesh, in_specs=in_specs, out_specs=out_specs, check_vma=False
    )
```

```python
import functools

import jax
import jax.numpy as jnp
from jax import lax
from jax.experimental import pallas as pl
from jax.experimental.pallas import tpu as pltpu
from jax.sharding import PartitionSpec as P

F32 = jnp.float32
BF16 = jnp.bfloat16
EPSILON = 1e-06

ROWS = 256
HEAD = 128
FEATURES = 256
GROUPS = 2
VALUE_HEADS = 4
BLOCKS = ((0, 0), (1, 0), (1, 1))
TILES = 6
CONV = 512
GROUP = 768
HALO = 16
NX = 4
NZ = 8
NY = 4

CHIPS = (0, 1, 3, 2)


def matmul(a, b):
    return jnp.dot(a, b, preferred_element_type=F32)


def matmul_t(a, b):
    return lax.dot_general(a, b, (((1,), (1,)), ((), ())), preferred_element_type=F32)


def silu(v):
    return 0.5 * v * (1.0 + jnp.tanh(0.5 * v))


def kernel(
    tokens_hbm,
    in_weight_hbm,
    gate_weight_hbm,
    conv_weight_hbm,
    decay_scale_hbm,
    dt_bias_hbm,
    beta_shift_hbm,
    norm_gain_hbm,
    out_weight_hbm,
    out_ref,
    gate_weight,
    conv_weight,
    decay_scale,
    dt_bias,
    beta_shift,
    norm_gain,
    tok,
    w_in,
    w_out,
    acc,
    ext,
    halo_out,
    halo_in,
    gates,
    qn,
    kn,
    vn,
    maps,
    row_maps,
    prefix,
    row_total,
    total_in,
    pair_in,
    pair_out,
    state_in,
    state_out,
    state_before,
    out_gate,
    decays,
    row_states,
    states,
    loc,
    qeff,
    sib_out,
    sib_in,
    ring_out,
    ring_in,
    load_sem,
    small_sem,
    win_sem,
    wout_sem,
    tok_send,
    tok_recv,
    tail_send,
    tail_recv,
    halo_sem,
    row_send,
    row_recv,
    total_send,
    total_recv,
    pair_send,
    pair_recv,
    state_send,
    state_recv,
    ready_sem,
    halo_ready_sem,
    back_send,
    back_recv,
    sib_send,
    sib_recv,
    ring_send,
    ring_recv,
):
    seq = lax.axis_index("seq")
    head = lax.axis_index("head")
    z, x = lax.div(seq, NX), lax.rem(seq, NX)
    y, c = lax.div(head, 2), lax.rem(head, 2)

    def chip_at(r):
        return lax.rem(y + r, NY)

    above = (seq, chip_at(1) * 2 + 1 - c)
    below = (seq, chip_at(3) * 2 + 1 - c)
    across = (seq, chip_at(2) * 2 + 1 - c)
    sibling = (seq, y * 2 + 1 - c)

    def remote(src, dst, send, recv, device):
        return pltpu.make_async_remote_copy(
            src_ref=src,
            dst_ref=dst,
            send_sem=send,
            recv_sem=recv,
            device_id=device,
            device_id_type=pl.DeviceIdType.MESH,
        )

    load_tok = pltpu.make_async_copy(tokens_hbm, tok.at[0, c], load_sem)
    load_tok.start()

    barrier = pltpu.get_barrier_semaphore()
    owner = c == 1

    def row_device(r, core):
        return (z * NX + lax.rem(x + r, NX), y * 2 + core)

    def column_device(there):
        return (there * NX + x, head)

    def signal(semaphore, device):
        pl.semaphore_signal(semaphore, inc=1, device_id=device, device_id_type=pl.DeviceIdType.MESH)

    odd = lax.rem(z, 2) == 1
    even = jnp.logical_not(odd)
    both_of = jnp.logical_and
    last_x = x == NX - 1
    not_top = z < NZ - 1
    for device in [above, below, across, sibling] + [row_device(r, 1) for r in range(1, NX)]:
        signal(barrier, device)
    for r in range(1, NX):
        pl.when(owner)(functools.partial(signal, barrier, row_device(r, 0)))

    pl.when(both_of(owner, even))(functools.partial(signal, barrier, column_device(z + 1)))
    for d in (1, 2):
        pl.when(both_of(owner, both_of(odd, not_top)))(functools.partial(signal, barrier, column_device(z + d)))
    pl.when(both_of(owner, z == 4))(functools.partial(signal, barrier, column_device(z + 2)))
    for d in (3, 4):
        pl.when(both_of(owner, z == 3))(functools.partial(signal, barrier, column_device(z + d)))

    @pl.when(both_of(c == 0, both_of(last_x, not_top)))
    def _():
        signal(barrier, ((z + 1) * NX + x, y * 2 + 1))

    def pair_of(r):
        return pl.ds(pl.multiple_of(chip_at(r) * 2 * FEATURES, 2 * FEATURES), 2 * FEATURES)

    load_in, load_out, load_small = [], [], []
    for i, r in enumerate(CHIPS):
        load_in.append(pltpu.make_async_copy(in_weight_hbm.at[pair_of(r)], w_in.at[i], win_sem.at[i]))
        load_out.append(
            pltpu.make_async_copy(out_weight_hbm.at[:, pair_of(r)], w_out.at[i], wout_sem.at[i])
        )
    for i, (source, target) in enumerate(
        (
            (gate_weight_hbm, gate_weight),
            (conv_weight_hbm, conv_weight),
            (decay_scale_hbm, decay_scale),
            (dt_bias_hbm, dt_bias),
            (beta_shift_hbm, beta_shift),
            (norm_gain_hbm, norm_gain),
        )
    ):
        load_small.append(pltpu.make_async_copy(source, target, small_sem.at[i]))
    for copy in load_in:
        copy.start()

    greeted = 7 + jnp.where(owner, 3 + lax.rem(z, 2) + jnp.where(z >= 2, 1, 0) + jnp.where(z >= 6, 1, 0) + jnp.where(z == 6, 1, 0), 0)
    greeted = greeted + jnp.where(both_of(owner, both_of(last_x, z > 0)), 1, 0)
    pl.semaphore_wait(barrier, greeted)

    pl.when(both_of(owner, odd))(functools.partial(signal, ready_sem, column_device(z - 1)))
    pl.when(both_of(owner, both_of(z >= 2, z < 4)))(functools.partial(signal, ready_sem, column_device(1)))
    pl.when(both_of(owner, z >= 4))(functools.partial(signal, ready_sem, column_device(3)))
    pl.when(both_of(owner, z >= 6))(functools.partial(signal, ready_sem, column_device(5)))
    pl.when(both_of(owner, z == 6))(functools.partial(signal, ready_sem, column_device(4)))

    @pl.when(both_of(owner, both_of(last_x, z > 0)))
    def _():
        for core in range(2):
            signal(halo_ready_sem, ((z - 1) * NX + x, y * 2 + core))

    load_tok.wait()

    pending = []

    def finish():
        for wait in pending:
            wait()

    sends = []

    body, tail = pl.ds(0, ROWS - HALO), pl.ds(ROWS - HALO, HALO)

    def send_tok(source, target, core, device):
        copy = remote(
            tok.at[source, core, body],
            tok.at[target, core, body],
            tok_send.at[len(sends)],
            tok_recv.at[target, core],
            device,
        )
        copy.start()
        sends.append(copy)

    def send_tail(n, source, target, core, device):
        copy = remote(
            tok.at[source, core, tail],
            tok.at[target, core, tail],
            tail_send.at[n],
            tail_recv.at[target, core],
            device,
        )
        copy.start()
        pending.append(copy.wait_send)

    def wait_tok(i, core):
        remote(
            tok.at[i, core, body], tok.at[i, core, body], tok_send.at[0], tok_recv.at[i, core], sibling
        ).wait_recv()

    up, down, far = CHIPS.index(1), CHIPS.index(3), CHIPS.index(2)
    away = ((down, above), (up, below), (far, across), (0, sibling))
    for n, (target, device) in enumerate(away):
        send_tail(n, 0, target, c, device)
    for target, device in away:
        send_tok(0, target, c, device)
    for copy in load_small + load_out:
        copy.start()

    def tokens_of(i):
        return jnp.concatenate([tok[i, 0], tok[i, 1]], 1)

    def project(chips, start):
        def tile(j, carry):
            columns = pl.ds(pl.multiple_of(j * 256, 256), 256)
            part = jnp.zeros((ROWS, 256), F32) if start else acc[j]
            for i in chips:
                part = part + matmul(tokens_of(i), w_in[i, :, columns])
            acc[j] = part
            return carry

        lax.fori_loop(0, TILES, tile, 0)

    def wait_tail(i, core):
        remote(
            tok.at[i, core, tail], tok.at[i, core, tail], tail_send.at[0], tail_recv.at[i, core], sibling
        ).wait_recv()

    wait_tail(0, 1 - c)
    wait_tok(0, 1 - c)
    load_in[0].wait()
    project((0,), True)
    for n, i in enumerate((up, down, far)):
        wait_tail(i, 1 - c)
        send_tail(4 + n, i, i, 1 - c, sibling)
    for i in (up, down, far):
        wait_tail(i, c)
    for i in (up, down, far):
        load_in[i].wait()
    for g in range(GROUPS):
        for n in range(2):
            columns = pl.ds((3 * g + n) * 256, 256)
            part = jnp.zeros((HALO, 256), F32)
            for i in range(NY):
                rows = jnp.concatenate([tok[i, 0, tail], tok[i, 1, tail]], 1)
                part = part + matmul(rows, w_in[i, :, columns])
            halo_out[:, (2 * g + n) * 256 : (2 * g + n + 1) * 256] = part.astype(BF16)

    for i in (down, up):
        wait_tok(i, 1 - c)
        send_tok(i, i, 1 - c, sibling)

    next_seq = lax.rem(seq + 1, NX * NZ)
    send_halo = remote(halo_out, halo_in, halo_sem.at[0], halo_sem.at[1], (next_seq, head))

    @pl.when(jnp.logical_and(last_x, not_top))
    def _():
        pl.semaphore_wait(halo_ready_sem, 1)

    pl.when(seq < NX * NZ - 1)(send_halo.start)
    pending.append(lambda: pl.when(seq < NX * NZ - 1)(send_halo.wait_send))
    wait_tok(down, c)
    wait_tok(up, c)
    project((up, down), False)
    for copy in load_small:
        copy.wait()

    def gating_of(i):
        weight = gate_weight[:, pair_of(CHIPS[i])]
        weight = jnp.concatenate([weight, jnp.zeros((HEAD - weight.shape[0], 2 * FEATURES), BF16)], 0)
        return matmul_t(tokens_of(i), weight)

    gating = gating_of(0) + gating_of(up) + gating_of(down)
    wait_tok(far, 1 - c)
    send_tok(far, far, 1 - c, sibling)
    wait_tok(far, c)
    pending.extend(copy.wait_send for copy in sends)

    for g in range(GROUPS):
        for n in range(2):
            j = 3 * g + n
            part = acc[j] + matmul(tokens_of(far), w_in[far, :, j * 256 : (j + 1) * 256])
            for block in range(2):
                columns = part[:, block * HEAD : (block + 1) * HEAD].astype(BF16)
                ext[4 * g + 2 * n + block, 8:, :] = columns.astype(F32)

    gating = gating + gating_of(far)
    lane = lax.broadcasted_iota(jnp.int32, (1, HEAD), 1)
    shift = jnp.zeros((1, HEAD), F32)
    bias = jnp.zeros((1, HEAD), F32)
    scale = jnp.zeros((1, HEAD), F32)
    for h in range(VALUE_HEADS):
        g, r = divmod(h, 2)
        shift = jnp.where(lane == 4 * g + r, beta_shift[h], shift)
        bias = jnp.where(lane == 4 * g + 2 + r, dt_bias[h], bias)
        scale = jnp.where(lane == 4 * g + 2 + r, decay_scale[h], scale)
    strength = jax.nn.sigmoid(gating - shift)
    shifted = gating + bias
    softplus = jnp.maximum(shifted, 0.0) + jnp.log1p(jnp.exp(-jnp.abs(shifted)))
    log_gate = -scale * softplus
    row_id = lax.broadcasted_iota(jnp.int32, (ROWS, ROWS), 0)
    col_id = lax.broadcasted_iota(jnp.int32, (ROWS, ROWS), 1)
    ones = jnp.where(col_id <= row_id, 1.0, 0.0).astype(BF16)
    cumulative = jnp.zeros((ROWS, HEAD), F32)
    rest = log_gate
    for _ in range(3):
        piece = rest.astype(BF16)
        cumulative = cumulative + matmul(ones, piece)
        rest = rest - piece.astype(F32)
    cumulative_t = jnp.transpose(cumulative)
    gates[0] = strength
    gates[1] = cumulative

    def convolve(first, count):
        for g in range(GROUPS):
            for block in range(CONV // HEAD):
                total = jnp.zeros((count, HEAD), F32)
                for tap in range(4):
                    weight = conv_weight[tap, g : g + 1, block * HEAD : (block + 1) * HEAD].astype(F32)
                    total = total + weight * ext[4 * g + block, pl.ds(first + 5 + tap, count), :]
                value = silu(total)
                rows = pl.ds(first, count)
                if block < 2:
                    norm = lax.rsqrt(jnp.sum(value * value, -1, keepdims=True) + EPSILON)
                    if block == 0:
                        qn[g, rows, :] = (value * (norm * HEAD**-0.5)).astype(BF16)
                    else:
                        kn[g, rows, :] = (value * norm).astype(BF16)
                else:
                    vn[2 * g + block - 2, rows, :] = value.astype(BF16)

    pl.when(seq > 0)(send_halo.wait_recv)

    @pl.when(seq == 0)
    def _():
        halo_in[...] = jnp.zeros_like(halo_in)

    for block in range(8):
        ext[block, 0:8, :] = halo_in[:, block * HEAD : (block + 1) * HEAD].astype(F32)[HALO - 8 :]
    convolve(0, ROWS)
    for g in range(GROUPS):
        j = 3 * g + 2
        part = acc[j] + matmul(tokens_of(far), w_in[far, :, j * 256 : (j + 1) * 256])
        out_gate[g] = silu(part.astype(BF16).astype(F32))
    row = lax.broadcasted_iota(jnp.int32, (HEAD, HEAD), 0)
    col = lax.broadcasted_iota(jnp.int32, (HEAD, HEAD), 1)
    on_lower = col <= row
    below_diag = col < row
    for h in range(VALUE_HEADS):
        g, r = divmod(h, 2)
        lane_c = 4 * g + 2 + r
        cum = cumulative[:, lane_c : lane_c + 1]
        cum_t = cumulative_t[lane_c : lane_c + 1, :]
        for n, (i, j) in enumerate(BLOCKS):
            gap = cum[i * HEAD : (i + 1) * HEAD] - cum_t[:, j * HEAD : (j + 1) * HEAD]
            if i == j:
                decays[h, n] = jnp.where(on_lower, jnp.exp(jnp.where(on_lower, gap, 0.0)), 0.0)
            else:
                decays[h, n] = jnp.exp(gap)


    unit = jnp.where(col == row, 1.0, 0.0)
    unit_b = unit.astype(BF16)

    def within(wide, narrow):
        keep = (lax.div(row, wide) == lax.div(col, wide)) & (lax.div(row, narrow) != lax.div(col, narrow))
        return jnp.where(keep & below_diag, 1.0, 0.0).astype(BF16)

    masks = [within(4 * b, b) for b in (2, 8, 32)]

    inner = []
    for g in range(GROUPS):
        inner.append(matmul_t(kn[g], kn[g]))
    systems = []
    for h in range(VALUE_HEADS):
        g, r = divmod(h, 2)
        lane_b, lane_c = 4 * g + r, 4 * g + 2 + r
        beta = gates[0][:, lane_b : lane_b + 1]
        system = {}
        for n, (i, j) in enumerate(BLOCKS):
            ri, cj = slice(i * HEAD, (i + 1) * HEAD), slice(j * HEAD, (j + 1) * HEAD)
            ratio = decays[h, n]
            system[i, j] = (beta[ri] * ratio * inner[g][ri, cj]).astype(BF16)
        systems.append(system)
    keys = [(h, i) for h in range(VALUE_HEADS) for i in range(2)]
    pairs = within(2, 1)
    inverses = {key: unit_b - pairs * systems[key[0]][key[1], key[1]] for key in keys}
    for mask in masks:
        moved = {k: matmul(inverses[k], mask * systems[k[0]][k[1], k[1]]).astype(BF16) for k in keys}
        once = {k: inverses[k].astype(F32) - matmul(moved[k], inverses[k]) for k in keys}
        twice = {k: matmul(moved[k], moved[k]).astype(BF16) for k in keys}
        inverses = {k: (once[k] + matmul(twice[k], once[k].astype(BF16))).astype(BF16) for k in keys}

    def solve(h):
        g, r = divmod(h, 2)
        lane_b, lane_c = 4 * g + r, 4 * g + 2 + r
        beta = gates[0][:, lane_b : lane_b + 1]
        cum = gates[1][:, lane_c : lane_c + 1]
        right = jnp.concatenate([beta * jnp.exp(cum) * kn[g].astype(F32), beta * vn[h].astype(F32)], 1)
        first = matmul(inverses[h, 0], right[:HEAD].astype(BF16)).astype(BF16)
        across_parts = matmul(inverses[h, 1], systems[h][1, 0]).astype(BF16)
        second = matmul(inverses[h, 1], right[HEAD:].astype(BF16))
        second = (second - matmul(across_parts, first)).astype(BF16)
        both = jnp.concatenate([first, second], 0)
        last = cum[ROWS - 1 :, :]
        end_keys = (jnp.exp(last - cum) * kn[g].astype(F32)).astype(BF16)
        grown = lax.dot_general(end_keys, both, (((0,), (0,)), ((), ())), preferred_element_type=F32)
        change = (jnp.exp(last) - 1.0) * unit - grown[:, :HEAD]
        maps[h] = jnp.concatenate([change, grown[:, HEAD:]], 1).astype(BF16)
        return both

    def hand_over(h):
        stays = jnp.logical_and(x == h, owner)
        row_copy = remote(
            maps.at[h], row_maps.at[c, x], row_send.at[h], row_recv.at[c, x], (z * NX + h, y * 2 + 1)
        )
        pl.when(jnp.logical_not(stays))(row_copy.start)
        pending.append(functools.partial(pl.when(jnp.logical_not(stays)), row_copy.wait_send))

        @pl.when(stays)
        def _():
            row_maps[1, h] = maps[h]

    solved = []
    for heads in ((0, 1), (2, 3)):
        solved += [solve(h) for h in heads]
        for h in heads:
            hand_over(h)

    inner = [matmul_t(qn[g], kn[g]) for g in range(GROUPS)]
    for h in range(VALUE_HEADS):
        g, r = divmod(h, 2)
        lane_c = 4 * g + 2 + r
        cum = gates[1][:, lane_c : lane_c + 1]
        score = {}
        for n, (i, j) in enumerate(BLOCKS):
            ri, cj = slice(i * HEAD, (i + 1) * HEAD), slice(j * HEAD, (j + 1) * HEAD)
            score[i, j] = (decays[h, n] * inner[g][ri, cj]).astype(BF16)
        top = matmul(score[0, 0], solved[h][:HEAD])
        low = matmul(jnp.concatenate([score[1, 0], score[1, 1]], 1), solved[h])
        out = jnp.concatenate([top, low], 0)
        qeff[h] = (jnp.exp(cum) * qn[g].astype(F32) - out[:, :HEAD]).astype(BF16)
        loc[h] = out[:, HEAD:]

    def compose(later, earlier):
        return earlier + later + matmul(later[:, :HEAD].astype(BF16), earlier.astype(BF16))

    def apply(change, shift, before):
        return before + shift.astype(F32) + matmul(change, before.astype(BF16))

    def total_copy(k):
        return remote(row_total.at[k], total_in.at[k], total_send.at[k], total_recv.at[k], column_device(z + 1))

    def shift_copy(k):
        return remote(
            row_total.at[k, 1], total_in.at[k, 1], total_send.at[k], total_recv.at[k], column_device(z + 1)
        )

    def skip_copy(k):
        return remote(row_total.at[k], pair_in.at[k], pair_send.at[k], pair_recv.at[k], column_device(z + 2))

    def pair_copy(k):
        return remote(pair_out.at[k], pair_in.at[k], pair_send.at[k], pair_recv.at[k], column_device(z + 2))

    def state_copy(d, k):
        return remote(
            state_out.at[k], state_in.at[k], state_send.at[k, d - 1], state_recv.at[k], column_device(z + d)
        )

    def back_copy(core, i):
        return remote(
            row_states.at[core, i], states.at[x], back_send.at[core, i], back_recv.at[x], (z * NX + i, y * 2 + core)
        )

    def leaves(core, i):
        return jnp.logical_not(jnp.logical_and(core == 1, x == i))

    @pl.when(owner)
    def _():
        answers = jnp.where(jnp.logical_or(odd, z == 4), 2, 1)

        @pl.when(z != 7)
        def _():
            pl.semaphore_wait(ready_sem, jnp.where(z == 3, 4, answers))


        for core in range(2):
            for i in range(NX):
                row_copy = remote(
                    maps.at[0], row_maps.at[core, i], row_send.at[0], row_recv.at[core, i], sibling
                )
                pl.when(leaves(core, i))(row_copy.wait_recv)
        row_map = [[row_maps[core, i].astype(F32) for i in range(NX)] for core in range(2)]
        first_two = [compose(row_map[core][1], row_map[core][0]) for core in range(2)]
        last_two = [compose(row_map[core][3], row_map[core][2]) for core in range(2)]
        for core in range(2):
            total = compose(last_two[core], first_two[core]).astype(BF16)
            row_total[core, 0] = total[:, :HEAD]
            row_total[core, 1] = total[:, HEAD:]
        for core in range(2):
            pl.when(z == 0)(shift_copy(core).start)
            pl.when(both_of(z > 0, jnp.logical_or(even, z == 5)))(total_copy(core).start)
        for core in range(2):
            pl.when(z == 4)(skip_copy(core).start)
        for core in range(2):
            prefix[core, 0] = row_map[core][0]
            prefix[core, 1] = first_two[core]
            prefix[core, 2] = compose(row_map[core][2], first_two[core])

        def joined(ref, k):
            return jnp.concatenate([ref[k, 0], ref[k, 1]], 1).astype(F32)

        @pl.when(z == 0)
        def _():
            state_before[...] = jnp.zeros_like(state_before)

        @pl.when(z == 1)
        def _():
            for core in range(2):
                shift_copy(core).wait_recv()
                shift = total_in[core, 1].astype(F32)
                state_before[core] = shift
                state_out[core] = apply(row_total[core, 0], row_total[core, 1], shift).astype(BF16)
                state_copy(2, core).start()
                state_copy(1, core).start()

        @pl.when(both_of(even, both_of(z > 0, z < 6)))
        def _():
            for core in range(2):
                state_copy(1, core).wait_recv()
                state_before[core] = state_in[core].astype(F32)

        @pl.when(both_of(odd, both_of(z > 1, z < 6)))
        def _():
            for core in range(2):
                total_copy(core).wait_recv()
                pair = compose(joined(row_total, core), joined(total_in, core)).astype(BF16)
                pair_out[core, 0] = pair[:, :HEAD]
                pair_out[core, 1] = pair[:, HEAD:]
                pl.when(z == 5)(pair_copy(core).start)
            for core in range(2):
                state_copy(1, core).wait_recv()
                state = state_in[core].astype(F32)

                @pl.when(z == 3)
                def _():
                    state_out[core] = apply(pair_out[core, 0], pair_out[core, 1], state).astype(BF16)
                    for d in (4, 3, 2, 1):
                        state_copy(d, core).start()

                state_before[core] = apply(total_in[core, 0], total_in[core, 1], state)

        @pl.when(z == 6)
        def _():
            both = []
            for core in range(2):
                pair_copy(core).wait_recv()
                total_copy(core).wait_recv()
                both.append(compose(joined(total_in, core), joined(pair_in, core)))
            for core in range(2):
                state_copy(1, core).wait_recv()
                change = both[core][:, :HEAD].astype(BF16)
                state_before[core] = apply(change, both[core][:, HEAD:], state_in[core].astype(F32))

        @pl.when(z == 7)
        def _():
            for core in range(2):
                state_copy(1, core).wait_recv()
                pair_copy(core).wait_recv()
                total_copy(core).wait_recv()
                state = apply(pair_in[core, 0], pair_in[core, 1], state_in[core].astype(F32))
                state_before[core] = apply(total_in[core, 0], total_in[core, 1], state)

        for core in range(2):
            state = state_before[core]
            row_states[core, 0] = state.astype(BF16)
            pl.when(leaves(core, 0))(back_copy(core, 0).start)
            for i in range(1, NX):
                before_i = prefix[core, i - 1]
                row_states[core, i] = apply(
                    before_i[:, :HEAD].astype(BF16), before_i[:, HEAD:], state
                ).astype(BF16)
            for i in range(1, NX):
                pl.when(leaves(core, i))(back_copy(core, i).start)
        states[pl.ds(x, 1)] = row_states[1, pl.ds(x, 1)]

    def wait_owner():
        for core in range(2):
            pl.when(z == 0)(shift_copy(core).wait_send)
            pl.when(both_of(z > 0, jnp.logical_or(even, z == 5)))(total_copy(core).wait_send)
            pl.when(z == 4)(skip_copy(core).wait_send)
            pl.when(z == 5)(pair_copy(core).wait_send)
            for d in (1, 2):
                pl.when(z == 1)(state_copy(d, core).wait_send)
            for d in range(1, 5):
                pl.when(z == 3)(state_copy(d, core).wait_send)
        for core in range(2):
            for i in range(NX):
                pl.when(leaves(core, i))(back_copy(core, i).wait_send)

    pending.append(lambda: pl.when(owner)(wait_owner))
    for h in range(VALUE_HEADS):
        arrival = remote(
            row_states.at[0, 0], states.at[h], back_send.at[0, 0], back_recv.at[h], sibling
        )
        pl.when(jnp.logical_not(jnp.logical_and(owner, x == h)))(arrival.wait_recv)

    gain = norm_gain[...]
    hidden = []
    for h in range(VALUE_HEADS):
        g, r = divmod(h, 2)
        attended = loc[h] + matmul(qeff[h], states[h])
        back = lax.rsqrt(jnp.mean(attended * attended, -1, keepdims=True) + EPSILON)
        gate = out_gate[g, :, r * HEAD : (r + 1) * HEAD]
        hidden.append((attended * back * gain * gate).astype(BF16))
    hidden = jnp.concatenate(hidden, 1)

    def partial_for(r, core):
        columns = pl.ds(pl.multiple_of(core * FEATURES, FEATURES), FEATURES)
        return matmul(hidden, w_out[CHIPS.index(r), :, columns])

    def sibling_copy(r):
        return remote(sib_out.at[r], sib_in.at[r], sib_send.at[r], sib_recv.at[r], sibling)

    ring = {
        r: remote(ring_out.at[r - 1], ring_in.at[r - 1], ring_send.at[r - 1], ring_recv.at[r - 1], device)
        for r, device in ((1, above), (2, across), (3, below))
    }
    for copy in load_out:
        copy.wait()
    def send_sibling(r):
        sib_out[r] = partial_for(r, 1 - c if r == 0 else c).astype(BF16)
        sibling_copy(r).start()

    def send_ring(r):
        mine = partial_for(r, 1 - c)
        sibling_copy(r).wait_recv()
        ring_out[r - 1] = (mine + sib_in[r].astype(F32)).astype(BF16)
        ring[r].start()

    send_sibling(2)
    send_sibling(1)
    send_ring(2)
    send_sibling(3)
    send_ring(1)
    send_ring(3)
    send_sibling(0)
    total = partial_for(0, c)
    sibling_copy(0).wait_recv()
    total = total + sib_in[0].astype(F32)
    finish()
    for r in (2, 1, 3):
        ring[r].wait_recv()
        total = total + ring_in[r - 1].astype(F32)
    out_ref[...] = total.astype(BF16)

    for r in range(NY):
        sibling_copy(r).wait_send()
    for copy in ring.values():
        copy.wait_send()


def per_device(
    tokens,
    in_weight,
    gate_weight,
    conv_weight,
    decay_scale,
    dt_bias,
    beta_shift,
    norm_gain,
    out_weight,
):
    anywhere = pl.BlockSpec(memory_space=pltpu.HBM)
    vmem = pl.BlockSpec(memory_space=pltpu.VMEM)
    dma = pltpu.SemaphoreType.DMA
    return pl.pallas_call(
        kernel,
        out_shape=pltpu.VMEM((ROWS, FEATURES), BF16),
        in_specs=[anywhere] * 9,
        out_specs=vmem,
        scratch_shapes=[
            pltpu.VMEM((2 * VALUE_HEADS, 8 * FEATURES), BF16),
            pltpu.VMEM((4, GROUPS, CONV), BF16),
            pltpu.SMEM((VALUE_HEADS,), F32),
            pltpu.SMEM((VALUE_HEADS,), F32),
            pltpu.SMEM((VALUE_HEADS,), F32),
            pltpu.VMEM((1, HEAD), F32),
            pltpu.VMEM((NY, 2, ROWS, FEATURES), BF16),
            pltpu.VMEM((NY, 2 * FEATURES, GROUPS * GROUP), BF16),
            pltpu.VMEM((NY, VALUE_HEADS * HEAD, 2 * FEATURES), BF16),
            pltpu.VMEM((TILES, ROWS, 256), F32),
            pltpu.VMEM((8, 8 + ROWS, HEAD), F32),
            pltpu.VMEM((HALO, GROUPS * CONV), BF16),
            pltpu.VMEM((HALO, GROUPS * CONV), BF16),
            pltpu.VMEM((2, ROWS, HEAD), F32),
            pltpu.VMEM((GROUPS, ROWS, HEAD), BF16),
            pltpu.VMEM((GROUPS, ROWS, HEAD), BF16),
            pltpu.VMEM((VALUE_HEADS, ROWS, HEAD), BF16),
            pltpu.VMEM((VALUE_HEADS, HEAD, 2 * HEAD), BF16),
            pltpu.VMEM((2, NX, HEAD, 2 * HEAD), BF16),
            pltpu.VMEM((2, NX - 1, HEAD, 2 * HEAD), F32),
            pltpu.VMEM((2, 2, HEAD, HEAD), BF16),
            pltpu.VMEM((2, 2, HEAD, HEAD), BF16),
            pltpu.VMEM((2, 2, HEAD, HEAD), BF16),
            pltpu.VMEM((2, 2, HEAD, HEAD), BF16),
            pltpu.VMEM((2, HEAD, HEAD), BF16),
            pltpu.VMEM((2, HEAD, HEAD), BF16),
            pltpu.VMEM((2, HEAD, HEAD), F32),
            pltpu.VMEM((GROUPS, ROWS, 2 * HEAD), F32),
            pltpu.VMEM((VALUE_HEADS, len(BLOCKS), HEAD, HEAD), F32),
            pltpu.VMEM((2, NX, HEAD, HEAD), BF16),
            pltpu.VMEM((VALUE_HEADS, HEAD, HEAD), BF16),
            pltpu.VMEM((VALUE_HEADS, ROWS, HEAD), F32),
            pltpu.VMEM((VALUE_HEADS, ROWS, HEAD), BF16),
            pltpu.VMEM((NY, ROWS, FEATURES), BF16),
            pltpu.VMEM((NY, ROWS, FEATURES), BF16),
            pltpu.VMEM((NY - 1, ROWS, FEATURES), BF16),
            pltpu.VMEM((NY - 1, ROWS, FEATURES), BF16),
            dma,
            dma((6,)),
            dma((NY,)),
            dma((NY,)),
            dma((7,)),
            dma((NY, 2)),
            dma((7,)),
            dma((NY, 2)),
            dma((2,)),
            dma((NX,)),
            dma((2, NX)),
            dma((2,)),
            dma((2,)),
            dma((2,)),
            dma((2,)),
            dma((2, 4)),
            dma((2,)),
            pltpu.SemaphoreType.REGULAR,
            pltpu.SemaphoreType.REGULAR,
            dma((2, NX)),
            dma((NX,)),
            dma((NY,)),
            dma((NY,)),
            dma((NY - 1,)),
            dma((NY - 1,)),
        ],
        compiler_params=pltpu.CompilerParams(
            collective_id=0, has_side_effects=True, vmem_limit_bytes=60 * 1024 * 1024
        ),
    )(
        tokens,
        in_weight,
        gate_weight.T,
        conv_weight,
        decay_scale,
        dt_bias,
        beta_shift,
        norm_gain.reshape(1, HEAD),
        out_weight,
    )


def solution(mesh):
    in_specs = (
        P("seq", "head"),
        P(None, "head"),
        P(None, "head"),
        P(None, "head", None),
        P("head"),
        P("head"),
        P("head"),
        P(),
        P("head", None),
    )
    out_specs = P("seq", "head")
    return jax.shard_map(
        per_device, mesh=mesh, in_specs=in_specs, out_specs=out_specs, check_vma=False
    )
```

```python
import functools

import jax
import jax.numpy as jnp
from jax import lax
from jax.experimental import pallas as pl
from jax.experimental.pallas import tpu as pltpu
from jax.sharding import PartitionSpec as P

F32 = jnp.float32
BF16 = jnp.bfloat16
EPSILON = 1e-06

ROWS = 256
HEAD = 128
FEATURES = 256
GROUPS = 2
VALUE_HEADS = 4
BLOCKS = ((0, 0), (1, 0), (1, 1))
TILES = 6
CONV = 512
GROUP = 768
HALO = 16
NX = 4
NZ = 8
NY = 4

CHIPS = (0, 1, 3, 2)


def matmul(a, b):
    return jnp.dot(a, b, preferred_element_type=F32)


def matmul_t(a, b):
    return lax.dot_general(a, b, (((1,), (1,)), ((), ())), preferred_element_type=F32)


def silu(v):
    return 0.5 * v * (1.0 + jnp.tanh(0.5 * v))


def kernel(
    tokens_hbm,
    in_weight_hbm,
    gate_weight_hbm,
    conv_weight_hbm,
    decay_scale_hbm,
    dt_bias_hbm,
    beta_shift_hbm,
    norm_gain_hbm,
    out_weight_hbm,
    out_ref,
    gate_weight,
    conv_weight,
    decay_scale,
    dt_bias,
    beta_shift,
    norm_gain,
    tok,
    w_in,
    w_out,
    acc,
    ext,
    halo_out,
    halo_in,
    gates,
    qn,
    kn,
    vn,
    maps,
    row_maps,
    prefix,
    row_total,
    total_in,
    pair_in,
    pair_out,
    state_in,
    state_out,
    state_before,
    out_gate,
    decays,
    row_states,
    states,
    loc,
    qeff,
    sib_out,
    sib_in,
    ring_out,
    ring_in,
    load_sem,
    small_sem,
    win_sem,
    wout_sem,
    tok_send,
    tok_recv,
    tail_send,
    tail_recv,
    halo_sem,
    row_send,
    row_recv,
    total_send,
    total_recv,
    pair_send,
    pair_recv,
    state_send,
    state_recv,
    ready_sem,
    halo_ready_sem,
    back_send,
    back_recv,
    sib_send,
    sib_recv,
    ring_send,
    ring_recv,
):
    seq = lax.axis_index("seq")
    head = lax.axis_index("head")
    z, x = lax.div(seq, NX), lax.rem(seq, NX)
    y, c = lax.div(head, 2), lax.rem(head, 2)

    def chip_at(r):
        return lax.rem(y + r, NY)

    above = (seq, chip_at(1) * 2 + 1 - c)
    below = (seq, chip_at(3) * 2 + 1 - c)
    across = (seq, chip_at(2) * 2 + 1 - c)
    sibling = (seq, y * 2 + 1 - c)

    def remote(src, dst, send, recv, device):
        return pltpu.make_async_remote_copy(
            src_ref=src,
            dst_ref=dst,
            send_sem=send,
            recv_sem=recv,
            device_id=device,
            device_id_type=pl.DeviceIdType.MESH,
        )

    load_tok = pltpu.make_async_copy(tokens_hbm, tok.at[0, c], load_sem)
    load_tok.start()

    barrier = pltpu.get_barrier_semaphore()
    owner = c == 1

    def row_device(r, core):
        return (z * NX + lax.rem(x + r, NX), y * 2 + core)

    def column_device(there):
        return (lax.rem(there + NZ, NZ) * NX + x, head)

    def signal(semaphore, device):
        pl.semaphore_signal(semaphore, inc=1, device_id=device, device_id_type=pl.DeviceIdType.MESH)

    odd = lax.rem(z, 2) == 1
    even = jnp.logical_not(odd)
    both_of = jnp.logical_and
    last_x = x == NX - 1
    not_top = z < NZ - 1
    for device in [above, below, across, sibling] + [row_device(r, 1) for r in range(1, NX)]:
        signal(barrier, device)
    for r in range(1, NX):
        pl.when(owner)(functools.partial(signal, barrier, row_device(r, 0)))

    pl.when(both_of(owner, even))(functools.partial(signal, barrier, column_device(z + 1)))
    for d in (1, 2):
        pl.when(both_of(owner, both_of(odd, not_top)))(functools.partial(signal, barrier, column_device(z + d)))
    pl.when(both_of(owner, z == 4))(functools.partial(signal, barrier, column_device(z + 2)))
    for d in (3, 4):
        pl.when(both_of(owner, z == 3))(functools.partial(signal, barrier, column_device(z + d)))

    @pl.when(both_of(c == 0, both_of(last_x, not_top)))
    def _():
        signal(barrier, ((z + 1) * NX + x, y * 2 + 1))

    def pair_of(r):
        return pl.ds(pl.multiple_of(chip_at(r) * 2 * FEATURES, 2 * FEATURES), 2 * FEATURES)

    load_in, load_out, load_small = [], [], []
    for i, r in enumerate(CHIPS):
        load_in.append(pltpu.make_async_copy(in_weight_hbm.at[pair_of(r)], w_in.at[i], win_sem.at[i]))
        load_out.append(
            pltpu.make_async_copy(out_weight_hbm.at[:, pair_of(r)], w_out.at[i], wout_sem.at[i])
        )
    for i, (source, target) in enumerate(
        (
            (gate_weight_hbm, gate_weight),
            (conv_weight_hbm, conv_weight),
            (decay_scale_hbm, decay_scale),
            (dt_bias_hbm, dt_bias),
            (beta_shift_hbm, beta_shift),
            (norm_gain_hbm, norm_gain),
        )
    ):
        load_small.append(pltpu.make_async_copy(source, target, small_sem.at[i]))
    for copy in load_in:
        copy.start()

    greeted = 7 + jnp.where(owner, 3 + lax.rem(z, 2) + jnp.where(z >= 2, 1, 0) + jnp.where(z >= 6, 1, 0) + jnp.where(z == 6, 1, 0), 0)
    greeted = greeted + jnp.where(both_of(owner, both_of(last_x, z > 0)), 1, 0)
    pl.semaphore_wait(barrier, greeted)

    pl.when(both_of(owner, odd))(functools.partial(signal, ready_sem, column_device(z - 1)))
    pl.when(both_of(owner, both_of(z >= 2, z < 4)))(functools.partial(signal, ready_sem, column_device(1)))
    pl.when(both_of(owner, z >= 4))(functools.partial(signal, ready_sem, column_device(3)))
    pl.when(both_of(owner, z >= 6))(functools.partial(signal, ready_sem, column_device(5)))
    pl.when(both_of(owner, z == 6))(functools.partial(signal, ready_sem, column_device(4)))

    @pl.when(both_of(owner, both_of(last_x, z > 0)))
    def _():
        for core in range(2):
            signal(halo_ready_sem, ((z - 1) * NX + x, y * 2 + core))

    load_tok.wait()

    pending = []

    def finish():
        for wait in pending:
            wait()

    sends = []

    body, tail = pl.ds(0, ROWS - HALO), pl.ds(ROWS - HALO, HALO)

    def send_tok(source, target, core, device):
        copy = remote(
            tok.at[source, core, body],
            tok.at[target, core, body],
            tok_send.at[len(sends)],
            tok_recv.at[target, core],
            device,
        )
        copy.start()
        sends.append(copy)

    def send_tail(n, source, target, core, device):
        copy = remote(
            tok.at[source, core, tail],
            tok.at[target, core, tail],
            tail_send.at[n],
            tail_recv.at[target, core],
            device,
        )
        copy.start()
        pending.append(copy.wait_send)

    def wait_tok(i, core):
        remote(
            tok.at[i, core, body], tok.at[i, core, body], tok_send.at[0], tok_recv.at[i, core], sibling
        ).wait_recv()

    up, down, far = CHIPS.index(1), CHIPS.index(3), CHIPS.index(2)
    away = ((down, above), (up, below), (far, across), (0, sibling))
    for n, (target, device) in enumerate(away):
        send_tail(n, 0, target, c, device)
    for target, device in away:
        send_tok(0, target, c, device)
    for copy in load_small + load_out:
        copy.start()

    def tokens_of(i):
        return jnp.concatenate([tok[i, 0], tok[i, 1]], 1)

    def project(chips, start):
        def tile(j, carry):
            columns = pl.ds(pl.multiple_of(j * 256, 256), 256)
            part = jnp.zeros((ROWS, 256), F32) if start else acc[j]
            for i in chips:
                part = part + matmul(tokens_of(i), w_in[i, :, columns])
            acc[j] = part
            return carry

        lax.fori_loop(0, TILES, tile, 0)

    def wait_tail(i, core):
        remote(
            tok.at[i, core, tail], tok.at[i, core, tail], tail_send.at[0], tail_recv.at[i, core], sibling
        ).wait_recv()

    wait_tail(0, 1 - c)
    wait_tok(0, 1 - c)
    load_in[0].wait()
    project((0,), True)
    for n, i in enumerate((up, down, far)):
        wait_tail(i, 1 - c)
        send_tail(4 + n, i, i, 1 - c, sibling)
    for i in (up, down, far):
        wait_tail(i, c)
    for i in (up, down, far):
        load_in[i].wait()
    for g in range(GROUPS):
        for n in range(2):
            columns = pl.ds((3 * g + n) * 256, 256)
            part = jnp.zeros((HALO, 256), F32)
            for i in range(NY):
                rows = jnp.concatenate([tok[i, 0, tail], tok[i, 1, tail]], 1)
                part = part + matmul(rows, w_in[i, :, columns])
            halo_out[:, (2 * g + n) * 256 : (2 * g + n + 1) * 256] = part.astype(BF16)

    for i in (down, up):
        wait_tok(i, 1 - c)
        send_tok(i, i, 1 - c, sibling)

    next_seq = lax.rem(seq + 1, NX * NZ)
    send_halo = remote(halo_out, halo_in, halo_sem.at[0], halo_sem.at[1], (next_seq, head))

    @pl.when(jnp.logical_and(last_x, not_top))
    def _():
        pl.semaphore_wait(halo_ready_sem, 1)

    pl.when(seq < NX * NZ - 1)(send_halo.start)
    pending.append(lambda: pl.when(seq < NX * NZ - 1)(send_halo.wait_send))
    wait_tok(down, c)
    wait_tok(up, c)
    project((up, down), False)
    for copy in load_small:
        copy.wait()

    def gating_of(i):
        weight = gate_weight[:, pair_of(CHIPS[i])]
        weight = jnp.concatenate([weight, jnp.zeros((HEAD - weight.shape[0], 2 * FEATURES), BF16)], 0)
        return matmul_t(tokens_of(i), weight)

    gating = gating_of(0) + gating_of(up) + gating_of(down)
    wait_tok(far, 1 - c)
    send_tok(far, far, 1 - c, sibling)
    wait_tok(far, c)
    pending.extend(copy.wait_send for copy in sends)

    for g in range(GROUPS):
        for n in range(2):
            j = 3 * g + n
            part = acc[j] + matmul(tokens_of(far), w_in[far, :, j * 256 : (j + 1) * 256])
            for block in range(2):
                columns = part[:, block * HEAD : (block + 1) * HEAD].astype(BF16)
                ext[4 * g + 2 * n + block, 8:, :] = columns.astype(F32)

    gating = gating + gating_of(far)
    lane = lax.broadcasted_iota(jnp.int32, (1, HEAD), 1)
    shift = jnp.zeros((1, HEAD), F32)
    bias = jnp.zeros((1, HEAD), F32)
    scale = jnp.zeros((1, HEAD), F32)
    for h in range(VALUE_HEADS):
        g, r = divmod(h, 2)
        shift = jnp.where(lane == 4 * g + r, beta_shift[h], shift)
        bias = jnp.where(lane == 4 * g + 2 + r, dt_bias[h], bias)
        scale = jnp.where(lane == 4 * g + 2 + r, decay_scale[h], scale)
    strength = jax.nn.sigmoid(gating - shift)
    shifted = gating + bias
    softplus = jnp.maximum(shifted, 0.0) + jnp.log1p(jnp.exp(-jnp.abs(shifted)))
    log_gate = -scale * softplus
    row_id = lax.broadcasted_iota(jnp.int32, (ROWS, ROWS), 0)
    col_id = lax.broadcasted_iota(jnp.int32, (ROWS, ROWS), 1)
    ones = jnp.where(col_id <= row_id, 1.0, 0.0).astype(BF16)
    cumulative = jnp.zeros((ROWS, HEAD), F32)
    rest = log_gate
    for _ in range(3):
        piece = rest.astype(BF16)
        cumulative = cumulative + matmul(ones, piece)
        rest = rest - piece.astype(F32)
    cumulative_t = jnp.transpose(cumulative)
    gates[0] = strength
    gates[1] = cumulative

    def convolve(first, count):
        for g in range(GROUPS):
            for block in range(CONV // HEAD):
                total = jnp.zeros((count, HEAD), F32)
                for tap in range(4):
                    weight = conv_weight[tap, g : g + 1, block * HEAD : (block + 1) * HEAD].astype(F32)
                    total = total + weight * ext[4 * g + block, pl.ds(first + 5 + tap, count), :]
                value = silu(total)
                rows = pl.ds(first, count)
                if block < 2:
                    norm = lax.rsqrt(jnp.sum(value * value, -1, keepdims=True) + EPSILON)
                    if block == 0:
                        qn[g, rows, :] = (value * (norm * HEAD**-0.5)).astype(BF16)
                    else:
                        kn[g, rows, :] = (value * norm).astype(BF16)
                else:
                    vn[2 * g + block - 2, rows, :] = value.astype(BF16)

    pl.when(seq > 0)(send_halo.wait_recv)

    @pl.when(seq == 0)
    def _():
        halo_in[...] = jnp.zeros_like(halo_in)

    for block in range(8):
        ext[block, 0:8, :] = halo_in[:, block * HEAD : (block + 1) * HEAD].astype(F32)[HALO - 8 :]
    convolve(0, ROWS)
    for g in range(GROUPS):
        j = 3 * g + 2
        part = acc[j] + matmul(tokens_of(far), w_in[far, :, j * 256 : (j + 1) * 256])
        out_gate[g] = silu(part.astype(BF16).astype(F32))
    row = lax.broadcasted_iota(jnp.int32, (HEAD, HEAD), 0)
    col = lax.broadcasted_iota(jnp.int32, (HEAD, HEAD), 1)
    on_lower = col <= row
    below_diag = col < row
    for h in range(VALUE_HEADS):
        g, r = divmod(h, 2)
        lane_c = 4 * g + 2 + r
        cum = cumulative[:, lane_c : lane_c + 1]
        cum_t = cumulative_t[lane_c : lane_c + 1, :]
        for n, (i, j) in enumerate(BLOCKS):
            gap = cum[i * HEAD : (i + 1) * HEAD] - cum_t[:, j * HEAD : (j + 1) * HEAD]
            if i == j:
                decays[h, n] = jnp.where(on_lower, jnp.exp(jnp.where(on_lower, gap, 0.0)), 0.0)
            else:
                decays[h, n] = jnp.exp(gap)


    unit = jnp.where(col == row, 1.0, 0.0)
    unit_b = unit.astype(BF16)

    def within(wide, narrow):
        keep = (lax.div(row, wide) == lax.div(col, wide)) & (lax.div(row, narrow) != lax.div(col, narrow))
        return jnp.where(keep & below_diag, 1.0, 0.0).astype(BF16)

    masks = [within(4 * b, b) for b in (2, 8, 32)]

    inner = []
    for g in range(GROUPS):
        inner.append(matmul_t(kn[g], kn[g]))
    systems = []
    for h in range(VALUE_HEADS):
        g, r = divmod(h, 2)
        lane_b, lane_c = 4 * g + r, 4 * g + 2 + r
        beta = gates[0][:, lane_b : lane_b + 1]
        system = {}
        for n, (i, j) in enumerate(BLOCKS):
            ri, cj = slice(i * HEAD, (i + 1) * HEAD), slice(j * HEAD, (j + 1) * HEAD)
            ratio = decays[h, n]
            system[i, j] = (beta[ri] * ratio * inner[g][ri, cj]).astype(BF16)
        systems.append(system)
    keys = [(h, i) for h in range(VALUE_HEADS) for i in range(2)]
    pairs = within(2, 1)
    inverses = {key: unit_b - pairs * systems[key[0]][key[1], key[1]] for key in keys}
    for mask in masks:
        moved = {k: matmul(inverses[k], mask * systems[k[0]][k[1], k[1]]).astype(BF16) for k in keys}
        once = {k: inverses[k].astype(F32) - matmul(moved[k], inverses[k]) for k in keys}
        twice = {k: matmul(moved[k], moved[k]).astype(BF16) for k in keys}
        inverses = {k: (once[k] + matmul(twice[k], once[k].astype(BF16))).astype(BF16) for k in keys}

    def solve(h):
        g, r = divmod(h, 2)
        lane_b, lane_c = 4 * g + r, 4 * g + 2 + r
        beta = gates[0][:, lane_b : lane_b + 1]
        cum = gates[1][:, lane_c : lane_c + 1]
        right = jnp.concatenate([beta * jnp.exp(cum) * kn[g].astype(F32), beta * vn[h].astype(F32)], 1)
        first = matmul(inverses[h, 0], right[:HEAD].astype(BF16)).astype(BF16)
        across_parts = matmul(inverses[h, 1], systems[h][1, 0]).astype(BF16)
        second = matmul(inverses[h, 1], right[HEAD:].astype(BF16))
        second = (second - matmul(across_parts, first)).astype(BF16)
        both = jnp.concatenate([first, second], 0)
        last = cum[ROWS - 1 :, :]
        end_keys = (jnp.exp(last - cum) * kn[g].astype(F32)).astype(BF16)
        grown = lax.dot_general(end_keys, both, (((0,), (0,)), ((), ())), preferred_element_type=F32)
        change = (jnp.exp(last) - 1.0) * unit - grown[:, :HEAD]
        maps[h] = jnp.concatenate([change, grown[:, HEAD:]], 1).astype(BF16)
        return both

    def hand_over(h):
        stays = jnp.logical_and(x == h, owner)
        row_copy = remote(
            maps.at[h], row_maps.at[c, x], row_send.at[h], row_recv.at[c, x], (z * NX + h, y * 2 + 1)
        )
        pl.when(jnp.logical_not(stays))(row_copy.start)
        pending.append(functools.partial(pl.when(jnp.logical_not(stays)), row_copy.wait_send))

        @pl.when(stays)
        def _():
            row_maps[1, h] = maps[h]

    solved = []
    for heads in ((0, 1), (2, 3)):
        solved += [solve(h) for h in heads]
        for h in heads:
            hand_over(h)

    inner = [matmul_t(qn[g], kn[g]) for g in range(GROUPS)]
    for h in range(VALUE_HEADS):
        g, r = divmod(h, 2)
        lane_c = 4 * g + 2 + r
        cum = gates[1][:, lane_c : lane_c + 1]
        score = {}
        for n, (i, j) in enumerate(BLOCKS):
            ri, cj = slice(i * HEAD, (i + 1) * HEAD), slice(j * HEAD, (j + 1) * HEAD)
            score[i, j] = (decays[h, n] * inner[g][ri, cj]).astype(BF16)
        top = matmul(score[0, 0], solved[h][:HEAD])
        low = matmul(jnp.concatenate([score[1, 0], score[1, 1]], 1), solved[h])
        out = jnp.concatenate([top, low], 0)
        qeff[h] = (jnp.exp(cum) * qn[g].astype(F32) - out[:, :HEAD]).astype(BF16)
        loc[h] = out[:, HEAD:]

    def compose(later, earlier):
        return earlier + later + matmul(later[:, :HEAD].astype(BF16), earlier.astype(BF16))

    def apply(change, shift, before):
        return before + shift.astype(F32) + matmul(change, before.astype(BF16))

    def total_copy(k):
        return remote(row_total.at[k], total_in.at[k], total_send.at[k], total_recv.at[k], column_device(z + 1))

    def shift_copy(k):
        return remote(
            row_total.at[k, 1], total_in.at[k, 1], total_send.at[k], total_recv.at[k], column_device(z + 1)
        )

    def skip_copy(k):
        return remote(row_total.at[k], pair_in.at[k], pair_send.at[k], pair_recv.at[k], column_device(z + 2))

    def pair_copy(k):
        return remote(pair_out.at[k], pair_in.at[k], pair_send.at[k], pair_recv.at[k], column_device(z + 2))

    def state_copy(d, k):
        return remote(
            state_out.at[k], state_in.at[k], state_send.at[k, d - 1], state_recv.at[k], column_device(z + d)
        )

    def back_copy(core, i):
        return remote(
            row_states.at[core, i], states.at[x], back_send.at[core, i], back_recv.at[x], (z * NX + i, y * 2 + core)
        )

    def leaves(core, i):
        return jnp.logical_not(jnp.logical_and(core == 1, x == i))

    @pl.when(owner)
    def _():
        answers = jnp.where(jnp.logical_or(odd, z == 4), 2, 1)

        @pl.when(z != 7)
        def _():
            pl.semaphore_wait(ready_sem, jnp.where(z == 3, 4, answers))


        for core in range(2):
            for i in range(NX):
                row_copy = remote(
                    maps.at[0], row_maps.at[core, i], row_send.at[0], row_recv.at[core, i], sibling
                )
                pl.when(leaves(core, i))(row_copy.wait_recv)
        row_map = [[row_maps[core, i].astype(F32) for i in range(NX)] for core in range(2)]
        first_two = [compose(row_map[core][1], row_map[core][0]) for core in range(2)]
        last_two = [compose(row_map[core][3], row_map[core][2]) for core in range(2)]
        for core in range(2):
            total = compose(last_two[core], first_two[core]).astype(BF16)
            row_total[core, 0] = total[:, :HEAD]
            row_total[core, 1] = total[:, HEAD:]
        for core in range(2):
            pl.when(z == 0)(shift_copy(core).start)
            pl.when(both_of(z > 0, jnp.logical_or(even, z == 5)))(total_copy(core).start)
        for core in range(2):
            pl.when(z == 4)(skip_copy(core).start)
        for core in range(2):
            prefix[core, 0] = row_map[core][0]
            prefix[core, 1] = first_two[core]
            prefix[core, 2] = compose(row_map[core][2], first_two[core])

        def joined(ref, k):
            return jnp.concatenate([ref[k, 0], ref[k, 1]], 1).astype(F32)

        @pl.when(z == 0)
        def _():
            state_before[...] = jnp.zeros_like(state_before)

        @pl.when(z == 1)
        def _():
            for core in range(2):
                shift_copy(core).wait_recv()
                shift = total_in[core, 1].astype(F32)
                state_before[core] = shift
                state_out[core] = apply(row_total[core, 0], row_total[core, 1], shift).astype(BF16)
                state_copy(2, core).start()
                state_copy(1, core).start()

        @pl.when(both_of(even, both_of(z > 0, z < 6)))
        def _():
            for core in range(2):
                state_copy(1, core).wait_recv()
                state_before[core] = state_in[core].astype(F32)

        @pl.when(both_of(odd, both_of(z > 1, z < 6)))
        def _():
            for core in range(2):
                total_copy(core).wait_recv()
                pair = compose(joined(row_total, core), joined(total_in, core)).astype(BF16)
                pair_out[core, 0] = pair[:, :HEAD]
                pair_out[core, 1] = pair[:, HEAD:]
                pl.when(z == 5)(pair_copy(core).start)
            for core in range(2):
                state_copy(1, core).wait_recv()
                state = state_in[core].astype(F32)

                @pl.when(z == 3)
                def _():
                    state_out[core] = apply(pair_out[core, 0], pair_out[core, 1], state).astype(BF16)
                    for d in (4, 3, 2, 1):
                        state_copy(d, core).start()

                state_before[core] = apply(total_in[core, 0], total_in[core, 1], state)

        @pl.when(z == 6)
        def _():
            both = []
            for core in range(2):
                pair_copy(core).wait_recv()
                total_copy(core).wait_recv()
                both.append(compose(joined(total_in, core), joined(pair_in, core)))
            for core in range(2):
                state_copy(1, core).wait_recv()
                change = both[core][:, :HEAD].astype(BF16)
                state_before[core] = apply(change, both[core][:, HEAD:], state_in[core].astype(F32))

        @pl.when(z == 7)
        def _():
            for core in range(2):
                state_copy(1, core).wait_recv()
                pair_copy(core).wait_recv()
                total_copy(core).wait_recv()
                state = apply(pair_in[core, 0], pair_in[core, 1], state_in[core].astype(F32))
                state_before[core] = apply(total_in[core, 0], total_in[core, 1], state)

        for core in range(2):
            state = state_before[core]
            row_states[core, 0] = state.astype(BF16)
            pl.when(leaves(core, 0))(back_copy(core, 0).start)
            for i in range(1, NX):
                before_i = prefix[core, i - 1]
                row_states[core, i] = apply(
                    before_i[:, :HEAD].astype(BF16), before_i[:, HEAD:], state
                ).astype(BF16)
            for i in range(1, NX):
                pl.when(leaves(core, i))(back_copy(core, i).start)
        states[pl.ds(x, 1)] = row_states[1, pl.ds(x, 1)]

    def wait_owner():
        for core in range(2):
            pl.when(z == 0)(shift_copy(core).wait_send)
            pl.when(both_of(z > 0, jnp.logical_or(even, z == 5)))(total_copy(core).wait_send)
            pl.when(z == 4)(skip_copy(core).wait_send)
            pl.when(z == 5)(pair_copy(core).wait_send)
            for d in (1, 2):
                pl.when(z == 1)(state_copy(d, core).wait_send)
            for d in range(1, 5):
                pl.when(z == 3)(state_copy(d, core).wait_send)
        for core in range(2):
            for i in range(NX):
                pl.when(leaves(core, i))(back_copy(core, i).wait_send)

    pending.append(lambda: pl.when(owner)(wait_owner))
    for h in range(VALUE_HEADS):
        arrival = remote(
            row_states.at[0, 0], states.at[h], back_send.at[0, 0], back_recv.at[h], sibling
        )
        pl.when(jnp.logical_not(jnp.logical_and(owner, x == h)))(arrival.wait_recv)

    gain = norm_gain[...]
    hidden = []
    for h in range(VALUE_HEADS):
        g, r = divmod(h, 2)
        attended = loc[h] + matmul(qeff[h], states[h])
        back = lax.rsqrt(jnp.mean(attended * attended, -1, keepdims=True) + EPSILON)
        gate = out_gate[g, :, r * HEAD : (r + 1) * HEAD]
        hidden.append((attended * back * gain * gate).astype(BF16))
    hidden = jnp.concatenate(hidden, 1)

    def partial_for(r, core):
        columns = pl.ds(pl.multiple_of(core * FEATURES, FEATURES), FEATURES)
        return matmul(hidden, w_out[CHIPS.index(r), :, columns])

    def sibling_copy(r):
        return remote(sib_out.at[r], sib_in.at[r], sib_send.at[r], sib_recv.at[r], sibling)

    ring = {
        r: remote(ring_out.at[r - 1], ring_in.at[r - 1], ring_send.at[r - 1], ring_recv.at[r - 1], device)
        for r, device in ((1, above), (2, across), (3, below))
    }
    for copy in load_out:
        copy.wait()
    def send_sibling(r):
        sib_out[r] = partial_for(r, 1 - c if r == 0 else c).astype(BF16)
        sibling_copy(r).start()

    def send_ring(r):
        mine = partial_for(r, 1 - c)
        sibling_copy(r).wait_recv()
        ring_out[r - 1] = (mine + sib_in[r].astype(F32)).astype(BF16)
        ring[r].start()

    send_sibling(2)
    send_sibling(1)
    send_ring(2)
    send_sibling(3)
    send_ring(1)
    send_ring(3)
    send_sibling(0)
    total = partial_for(0, c)
    sibling_copy(0).wait_recv()
    total = total + sib_in[0].astype(F32)
    finish()
    for r in (2, 1, 3):
        ring[r].wait_recv()
        total = total + ring_in[r - 1].astype(F32)
    out_ref[...] = total.astype(BF16)

    for r in range(NY):
        sibling_copy(r).wait_send()
    for copy in ring.values():
        copy.wait_send()


def per_device(
    tokens,
    in_weight,
    gate_weight,
    conv_weight,
    decay_scale,
    dt_bias,
    beta_shift,
    norm_gain,
    out_weight,
):
    anywhere = pl.BlockSpec(memory_space=pltpu.HBM)
    vmem = pl.BlockSpec(memory_space=pltpu.VMEM)
    dma = pltpu.SemaphoreType.DMA
    return pl.pallas_call(
        kernel,
        out_shape=pltpu.VMEM((ROWS, FEATURES), BF16),
        in_specs=[anywhere] * 9,
        out_specs=vmem,
        scratch_shapes=[
            pltpu.VMEM((2 * VALUE_HEADS, 8 * FEATURES), BF16),
            pltpu.VMEM((4, GROUPS, CONV), BF16),
            pltpu.SMEM((VALUE_HEADS,), F32),
            pltpu.SMEM((VALUE_HEADS,), F32),
            pltpu.SMEM((VALUE_HEADS,), F32),
            pltpu.VMEM((1, HEAD), F32),
            pltpu.VMEM((NY, 2, ROWS, FEATURES), BF16),
            pltpu.VMEM((NY, 2 * FEATURES, GROUPS * GROUP), BF16),
            pltpu.VMEM((NY, VALUE_HEADS * HEAD, 2 * FEATURES), BF16),
            pltpu.VMEM((TILES, ROWS, 256), F32),
            pltpu.VMEM((8, 8 + ROWS, HEAD), F32),
            pltpu.VMEM((HALO, GROUPS * CONV), BF16),
            pltpu.VMEM((HALO, GROUPS * CONV), BF16),
            pltpu.VMEM((2, ROWS, HEAD), F32),
            pltpu.VMEM((GROUPS, ROWS, HEAD), BF16),
            pltpu.VMEM((GROUPS, ROWS, HEAD), BF16),
            pltpu.VMEM((VALUE_HEADS, ROWS, HEAD), BF16),
            pltpu.VMEM((VALUE_HEADS, HEAD, 2 * HEAD), BF16),
            pltpu.VMEM((2, NX, HEAD, 2 * HEAD), BF16),
            pltpu.VMEM((2, NX - 1, HEAD, 2 * HEAD), F32),
            pltpu.VMEM((2, 2, HEAD, HEAD), BF16),
            pltpu.VMEM((2, 2, HEAD, HEAD), BF16),
            pltpu.VMEM((2, 2, HEAD, HEAD), BF16),
            pltpu.VMEM((2, 2, HEAD, HEAD), BF16),
            pltpu.VMEM((2, HEAD, HEAD), BF16),
            pltpu.VMEM((2, HEAD, HEAD), BF16),
            pltpu.VMEM((2, HEAD, HEAD), F32),
            pltpu.VMEM((GROUPS, ROWS, 2 * HEAD), F32),
            pltpu.VMEM((VALUE_HEADS, len(BLOCKS), HEAD, HEAD), F32),
            pltpu.VMEM((2, NX, HEAD, HEAD), BF16),
            pltpu.VMEM((VALUE_HEADS, HEAD, HEAD), BF16),
            pltpu.VMEM((VALUE_HEADS, ROWS, HEAD), F32),
            pltpu.VMEM((VALUE_HEADS, ROWS, HEAD), BF16),
            pltpu.VMEM((NY, ROWS, FEATURES), BF16),
            pltpu.VMEM((NY, ROWS, FEATURES), BF16),
            pltpu.VMEM((NY - 1, ROWS, FEATURES), BF16),
            pltpu.VMEM((NY - 1, ROWS, FEATURES), BF16),
            dma,
            dma((6,)),
            dma((NY,)),
            dma((NY,)),
            dma((7,)),
            dma((NY, 2)),
            dma((7,)),
            dma((NY, 2)),
            dma((2,)),
            dma((NX,)),
            dma((2, NX)),
            dma((2,)),
            dma((2,)),
            dma((2,)),
            dma((2,)),
            dma((2, 4)),
            dma((2,)),
            pltpu.SemaphoreType.REGULAR,
            pltpu.SemaphoreType.REGULAR,
            dma((2, NX)),
            dma((NX,)),
            dma((NY,)),
            dma((NY,)),
            dma((NY - 1,)),
            dma((NY - 1,)),
        ],
        compiler_params=pltpu.CompilerParams(
            collective_id=0, has_side_effects=True, vmem_limit_bytes=60 * 1024 * 1024
        ),
    )(
        tokens,
        in_weight,
        gate_weight.T,
        conv_weight,
        decay_scale,
        dt_bias,
        beta_shift,
        norm_gain.reshape(1, HEAD),
        out_weight,
    )


def solution(mesh):
    in_specs = (
        P("seq", "head"),
        P(None, "head"),
        P(None, "head"),
        P(None, "head", None),
        P("head"),
        P("head"),
        P("head"),
        P(),
        P("head", None),
    )
    out_specs = P("seq", "head")
    return jax.shard_map(
        per_device, mesh=mesh, in_specs=in_specs, out_specs=out_specs, check_vma=False
    )
```

```python
import functools

import jax
import jax.numpy as jnp
from jax import lax
from jax.experimental import pallas as pl
from jax.experimental.pallas import tpu as pltpu
from jax.sharding import PartitionSpec as P

F32 = jnp.float32
BF16 = jnp.bfloat16
EPSILON = 1e-06

ROWS = 256
HEAD = 128
FEATURES = 256
GROUPS = 2
VALUE_HEADS = 4
BLOCKS = ((0, 0), (1, 0), (1, 1))
TILES = 6
CONV = 512
GROUP = 768
HALO = 16
NX = 4
NZ = 8
NY = 4

CHIPS = (0, 1, 3, 2)


def matmul(a, b):
    return jnp.dot(a, b, preferred_element_type=F32)


def matmul_t(a, b):
    return lax.dot_general(a, b, (((1,), (1,)), ((), ())), preferred_element_type=F32)


def silu(v):
    return 0.5 * v * (1.0 + jnp.tanh(0.5 * v))


def kernel(
    tokens_hbm,
    in_weight_hbm,
    gate_weight_hbm,
    conv_weight_hbm,
    decay_scale_hbm,
    dt_bias_hbm,
    beta_shift_hbm,
    norm_gain_hbm,
    out_weight_hbm,
    out_ref,
    gate_weight,
    conv_weight,
    decay_scale,
    dt_bias,
    beta_shift,
    norm_gain,
    tok,
    w_in,
    w_out,
    acc,
    ext,
    halo_out,
    halo_in,
    gates,
    qn,
    kn,
    vn,
    maps,
    row_maps,
    prefix,
    row_total,
    total_in,
    pair_in,
    pair_out,
    state_in,
    state_out,
    state_before,
    out_gate,
    decays,
    row_states,
    states,
    loc,
    qeff,
    sib_out,
    sib_in,
    ring_out,
    ring_in,
    load_sem,
    small_sem,
    win_sem,
    wout_sem,
    tok_send,
    tok_recv,
    tail_send,
    tail_recv,
    halo_sem,
    row_send,
    row_recv,
    total_send,
    total_recv,
    pair_send,
    pair_recv,
    state_send,
    state_recv,
    ready_sem,
    halo_ready_sem,
    back_send,
    back_recv,
    sib_send,
    sib_recv,
    ring_send,
    ring_recv,
):
    seq = lax.axis_index("seq")
    head = lax.axis_index("head")
    z, x = lax.div(seq, NX), lax.rem(seq, NX)
    y, c = lax.div(head, 2), lax.rem(head, 2)

    def chip_at(r):
        return lax.rem(y + r, NY)

    above = (seq, chip_at(1) * 2 + 1 - c)
    below = (seq, chip_at(3) * 2 + 1 - c)
    across = (seq, chip_at(2) * 2 + 1 - c)
    sibling = (seq, y * 2 + 1 - c)

    def remote(src, dst, send, recv, device):
        return pltpu.make_async_remote_copy(
            src_ref=src,
            dst_ref=dst,
            send_sem=send,
            recv_sem=recv,
            device_id=device,
            device_id_type=pl.DeviceIdType.MESH,
        )

    load_tok = pltpu.make_async_copy(tokens_hbm, tok.at[0, c], load_sem)
    load_tok.start()

    barrier = pltpu.get_barrier_semaphore()
    owner = c == 1

    def row_device(r, core):
        return (z * NX + lax.rem(x + r, NX), y * 2 + core)

    def column_device(there):
        return (lax.rem(there + NZ, NZ) * NX + x, head)

    def signal(semaphore, device):
        pl.semaphore_signal(semaphore, inc=1, device_id=device, device_id_type=pl.DeviceIdType.MESH)

    odd = lax.rem(z, 2) == 1
    even = jnp.logical_not(odd)
    both_of = jnp.logical_and
    last_x = x == NX - 1
    not_top = z < NZ - 1
    for device in [above, below, across, sibling] + [row_device(r, 1) for r in range(1, NX)]:
        signal(barrier, device)
    for r in range(1, NX):
        pl.when(owner)(functools.partial(signal, barrier, row_device(r, 0)))

    pl.when(both_of(owner, even))(functools.partial(signal, barrier, column_device(z + 1)))
    for d in (1, 2):
        pl.when(both_of(owner, both_of(odd, not_top)))(functools.partial(signal, barrier, column_device(z + d)))
    pl.when(both_of(owner, z == 4))(functools.partial(signal, barrier, column_device(z + 2)))
    for d in (3, 4):
        pl.when(both_of(owner, z == 3))(functools.partial(signal, barrier, column_device(z + d)))

    @pl.when(both_of(c == 0, both_of(last_x, not_top)))
    def _():
        signal(barrier, ((z + 1) * NX + x, y * 2 + 1))

    def pair_of(r):
        return pl.ds(pl.multiple_of(chip_at(r) * 2 * FEATURES, 2 * FEATURES), 2 * FEATURES)

    load_in, load_out, load_small = [], [], []
    for i, r in enumerate(CHIPS):
        load_in.append(pltpu.make_async_copy(in_weight_hbm.at[pair_of(r)], w_in.at[i], win_sem.at[i]))
        load_out.append(
            pltpu.make_async_copy(out_weight_hbm.at[:, pair_of(r)], w_out.at[i], wout_sem.at[i])
        )
    for i, (source, target) in enumerate(
        (
            (gate_weight_hbm, gate_weight),
            (conv_weight_hbm, conv_weight),
            (decay_scale_hbm, decay_scale),
            (dt_bias_hbm, dt_bias),
            (beta_shift_hbm, beta_shift),
            (norm_gain_hbm, norm_gain),
        )
    ):
        load_small.append(pltpu.make_async_copy(source, target, small_sem.at[i]))
    for copy in load_in:
        copy.start()

    greeted = 7 + jnp.where(owner, 3 + lax.rem(z, 2) + jnp.where(z >= 2, 1, 0) + jnp.where(z >= 6, 1, 0) + jnp.where(z == 6, 1, 0), 0)
    greeted = greeted + jnp.where(both_of(owner, both_of(last_x, z > 0)), 1, 0)
    pl.semaphore_wait(barrier, greeted)

    pl.when(both_of(owner, odd))(functools.partial(signal, ready_sem, column_device(z - 1)))
    pl.when(both_of(owner, both_of(z >= 2, z < 4)))(functools.partial(signal, ready_sem, column_device(1)))
    pl.when(both_of(owner, z >= 4))(functools.partial(signal, ready_sem, column_device(3)))
    pl.when(both_of(owner, z >= 6))(functools.partial(signal, ready_sem, column_device(5)))
    pl.when(both_of(owner, z == 6))(functools.partial(signal, ready_sem, column_device(4)))

    @pl.when(both_of(owner, both_of(last_x, z > 0)))
    def _():
        for core in range(2):
            signal(halo_ready_sem, ((z - 1) * NX + x, y * 2 + core))

    load_tok.wait()

    pending = []

    def finish():
        for wait in pending:
            wait()

    sends = []

    body, tail = pl.ds(0, ROWS - HALO), pl.ds(ROWS - HALO, HALO)

    def send_tok(source, target, core, device):
        copy = remote(
            tok.at[source, core, body],
            tok.at[target, core, body],
            tok_send.at[len(sends)],
            tok_recv.at[target, core],
            device,
        )
        copy.start()
        sends.append(copy)

    def send_tail(n, source, target, core, device):
        copy = remote(
            tok.at[source, core, tail],
            tok.at[target, core, tail],
            tail_send.at[n],
            tail_recv.at[target, core],
            device,
        )
        copy.start()
        pending.append(copy.wait_send)

    def wait_tok(i, core):
        remote(
            tok.at[i, core, body], tok.at[i, core, body], tok_send.at[0], tok_recv.at[i, core], sibling
        ).wait_recv()

    up, down, far = CHIPS.index(1), CHIPS.index(3), CHIPS.index(2)
    away = ((down, above), (up, below), (far, across), (0, sibling))
    for n, (target, device) in enumerate(away):
        send_tail(n, 0, target, c, device)
    for target, device in away:
        send_tok(0, target, c, device)
    for copy in load_small + load_out:
        copy.start()

    def tokens_of(i):
        return jnp.concatenate([tok[i, 0], tok[i, 1]], 1)

    def project(chips, start):
        def tile(j, carry):
            columns = pl.ds(pl.multiple_of(j * 256, 256), 256)
            part = jnp.zeros((ROWS, 256), F32) if start else acc[j]
            for i in chips:
                part = part + matmul(tokens_of(i), w_in[i, :, columns])
            acc[j] = part
            return carry

        lax.fori_loop(0, TILES, tile, 0)

    def wait_tail(i, core):
        remote(
            tok.at[i, core, tail], tok.at[i, core, tail], tail_send.at[0], tail_recv.at[i, core], sibling
        ).wait_recv()

    wait_tail(0, 1 - c)
    wait_tok(0, 1 - c)
    load_in[0].wait()
    project((0,), True)
    for n, i in enumerate((up, down, far)):
        wait_tail(i, 1 - c)
        send_tail(4 + n, i, i, 1 - c, sibling)
    for i in (up, down, far):
        wait_tail(i, c)
    for i in (up, down, far):
        load_in[i].wait()
    for g in range(GROUPS):
        for n in range(2):
            columns = pl.ds((3 * g + n) * 256, 256)
            part = jnp.zeros((HALO, 256), F32)
            for i in range(NY):
                rows = jnp.concatenate([tok[i, 0, tail], tok[i, 1, tail]], 1)
                part = part + matmul(rows, w_in[i, :, columns])
            halo_out[:, (2 * g + n) * 256 : (2 * g + n + 1) * 256] = part.astype(BF16)

    for i in (down, up):
        wait_tok(i, 1 - c)
        send_tok(i, i, 1 - c, sibling)

    next_seq = lax.rem(seq + 1, NX * NZ)
    send_halo = remote(halo_out, halo_in, halo_sem.at[0], halo_sem.at[1], (next_seq, head))

    @pl.when(jnp.logical_and(last_x, not_top))
    def _():
        pl.semaphore_wait(halo_ready_sem, 1)

    pl.when(seq < NX * NZ - 1)(send_halo.start)
    pending.append(lambda: pl.when(seq < NX * NZ - 1)(send_halo.wait_send))
    wait_tok(down, c)
    wait_tok(up, c)
    project((up, down), False)
    for copy in load_small:
        copy.wait()

    def gating_of(i):
        weight = gate_weight[:, pair_of(CHIPS[i])]
        weight = jnp.concatenate([weight, jnp.zeros((HEAD - weight.shape[0], 2 * FEATURES), BF16)], 0)
        return matmul_t(tokens_of(i), weight)

    gating = gating_of(0) + gating_of(up) + gating_of(down)
    wait_tok(far, 1 - c)
    send_tok(far, far, 1 - c, sibling)
    wait_tok(far, c)
    pending.extend(copy.wait_send for copy in sends)

    for g in range(GROUPS):
        for n in range(2):
            j = 3 * g + n
            part = acc[j] + matmul(tokens_of(far), w_in[far, :, j * 256 : (j + 1) * 256])
            for block in range(2):
                columns = part[:, block * HEAD : (block + 1) * HEAD].astype(BF16)
                ext[4 * g + 2 * n + block, 8:, :] = columns.astype(F32)

    gating = gating + gating_of(far)
    lane = lax.broadcasted_iota(jnp.int32, (1, HEAD), 1)
    shift = jnp.zeros((1, HEAD), F32)
    bias = jnp.zeros((1, HEAD), F32)
    scale = jnp.zeros((1, HEAD), F32)
    for h in range(VALUE_HEADS):
        g, r = divmod(h, 2)
        shift = jnp.where(lane == 4 * g + r, beta_shift[h], shift)
        bias = jnp.where(lane == 4 * g + 2 + r, dt_bias[h], bias)
        scale = jnp.where(lane == 4 * g + 2 + r, decay_scale[h], scale)
    strength = jax.nn.sigmoid(gating - shift)
    shifted = gating + bias
    softplus = jnp.maximum(shifted, 0.0) + jnp.log1p(jnp.exp(-jnp.abs(shifted)))
    log_gate = -scale * softplus
    row_id = lax.broadcasted_iota(jnp.int32, (ROWS, ROWS), 0)
    col_id = lax.broadcasted_iota(jnp.int32, (ROWS, ROWS), 1)
    ones = jnp.where(col_id <= row_id, 1.0, 0.0).astype(BF16)
    cumulative = jnp.zeros((ROWS, HEAD), F32)
    rest = log_gate
    for _ in range(3):
        piece = rest.astype(BF16)
        cumulative = cumulative + matmul(ones, piece)
        rest = rest - piece.astype(F32)
    cumulative_t = jnp.transpose(cumulative)
    gates[0] = strength
    gates[1] = cumulative

    def convolve(first, count):
        for g in range(GROUPS):
            for block in range(CONV // HEAD):
                total = jnp.zeros((count, HEAD), F32)
                for tap in range(4):
                    weight = conv_weight[tap, g : g + 1, block * HEAD : (block + 1) * HEAD].astype(F32)
                    total = total + weight * ext[4 * g + block, pl.ds(first + 5 + tap, count), :]
                value = silu(total)
                rows = pl.ds(first, count)
                if block < 2:
                    norm = lax.rsqrt(jnp.sum(value * value, -1, keepdims=True) + EPSILON)
                    if block == 0:
                        qn[g, rows, :] = (value * (norm * HEAD**-0.5)).astype(BF16)
                    else:
                        kn[g, rows, :] = (value * norm).astype(BF16)
                else:
                    vn[2 * g + block - 2, rows, :] = value.astype(BF16)

    pl.when(seq > 0)(send_halo.wait_recv)

    @pl.when(seq == 0)
    def _():
        halo_in[...] = jnp.zeros_like(halo_in)

    for block in range(8):
        ext[block, 0:8, :] = halo_in[:, block * HEAD : (block + 1) * HEAD].astype(F32)[HALO - 8 :]
    convolve(0, ROWS)
    for g in range(GROUPS):
        j = 3 * g + 2
        part = acc[j] + matmul(tokens_of(far), w_in[far, :, j * 256 : (j + 1) * 256])
        out_gate[g] = silu(part.astype(BF16).astype(F32))
    row = lax.broadcasted_iota(jnp.int32, (HEAD, HEAD), 0)
    col = lax.broadcasted_iota(jnp.int32, (HEAD, HEAD), 1)
    on_lower = col <= row
    below_diag = col < row
    for h in range(VALUE_HEADS):
        g, r = divmod(h, 2)
        lane_c = 4 * g + 2 + r
        cum = cumulative[:, lane_c : lane_c + 1]
        cum_t = cumulative_t[lane_c : lane_c + 1, :]
        for n, (i, j) in enumerate(BLOCKS):
            gap = cum[i * HEAD : (i + 1) * HEAD] - cum_t[:, j * HEAD : (j + 1) * HEAD]
            if i == j:
                decays[h, n] = jnp.where(on_lower, jnp.exp(jnp.where(on_lower, gap, 0.0)), 0.0)
            else:
                decays[h, n] = jnp.exp(gap)


    unit = jnp.where(col == row, 1.0, 0.0)
    unit_b = unit.astype(BF16)

    def within(wide, narrow):
        keep = (lax.div(row, wide) == lax.div(col, wide)) & (lax.div(row, narrow) != lax.div(col, narrow))
        return jnp.where(keep & below_diag, 1.0, 0.0).astype(BF16)

    masks = [within(4 * b, b) for b in (2, 8, 32)]

    inner = []
    for g in range(GROUPS):
        inner.append(matmul_t(kn[g], kn[g]))
    systems = []
    for h in range(VALUE_HEADS):
        g, r = divmod(h, 2)
        lane_b, lane_c = 4 * g + r, 4 * g + 2 + r
        beta = gates[0][:, lane_b : lane_b + 1]
        system = {}
        for n, (i, j) in enumerate(BLOCKS):
            ri, cj = slice(i * HEAD, (i + 1) * HEAD), slice(j * HEAD, (j + 1) * HEAD)
            ratio = decays[h, n]
            system[i, j] = (beta[ri] * ratio * inner[g][ri, cj]).astype(BF16)
        systems.append(system)
    keys = [(h, i) for h in range(VALUE_HEADS) for i in range(2)]
    pairs = within(2, 1)
    inverses = {key: unit_b - pairs * systems[key[0]][key[1], key[1]] for key in keys}
    for mask in masks:
        moved = {k: matmul(inverses[k], mask * systems[k[0]][k[1], k[1]]).astype(BF16) for k in keys}
        once = {k: inverses[k].astype(F32) - matmul(moved[k], inverses[k]) for k in keys}
        twice = {k: matmul(moved[k], moved[k]).astype(BF16) for k in keys}
        inverses = {k: (once[k] + matmul(twice[k], once[k].astype(BF16))).astype(BF16) for k in keys}

    def solve(h):
        g, r = divmod(h, 2)
        lane_b, lane_c = 4 * g + r, 4 * g + 2 + r
        beta = gates[0][:, lane_b : lane_b + 1]
        cum = gates[1][:, lane_c : lane_c + 1]
        right = jnp.concatenate([beta * jnp.exp(cum) * kn[g].astype(F32), beta * vn[h].astype(F32)], 1)
        first = matmul(inverses[h, 0], right[:HEAD].astype(BF16)).astype(BF16)
        across_parts = matmul(inverses[h, 1], systems[h][1, 0]).astype(BF16)
        second = matmul(inverses[h, 1], right[HEAD:].astype(BF16))
        second = (second - matmul(across_parts, first)).astype(BF16)
        both = jnp.concatenate([first, second], 0)
        last = cum[ROWS - 1 :, :]
        end_keys = (jnp.exp(last - cum) * kn[g].astype(F32)).astype(BF16)
        grown = lax.dot_general(end_keys, both, (((0,), (0,)), ((), ())), preferred_element_type=F32)
        change = (jnp.exp(last) - 1.0) * unit - grown[:, :HEAD]
        maps[h] = jnp.concatenate([change, grown[:, HEAD:]], 1).astype(BF16)
        return both

    def hand_over(h):
        stays = jnp.logical_and(x == h, owner)
        row_copy = remote(
            maps.at[h], row_maps.at[c, x], row_send.at[h], row_recv.at[c, x], (z * NX + h, y * 2 + 1)
        )
        pl.when(jnp.logical_not(stays))(row_copy.start)
        pending.append(functools.partial(pl.when(jnp.logical_not(stays)), row_copy.wait_send))

        @pl.when(stays)
        def _():
            row_maps[1, h] = maps[h]

    solved = []
    for heads in ((0, 1), (2, 3)):
        solved += [solve(h) for h in heads]
        for h in heads:
            hand_over(h)

    inner = [matmul_t(qn[g], kn[g]) for g in range(GROUPS)]
    for h in range(VALUE_HEADS):
        g, r = divmod(h, 2)
        lane_c = 4 * g + 2 + r
        cum = gates[1][:, lane_c : lane_c + 1]
        score = {}
        for n, (i, j) in enumerate(BLOCKS):
            ri, cj = slice(i * HEAD, (i + 1) * HEAD), slice(j * HEAD, (j + 1) * HEAD)
            score[i, j] = (decays[h, n] * inner[g][ri, cj]).astype(BF16)
        top = matmul(score[0, 0], solved[h][:HEAD])
        low = matmul(jnp.concatenate([score[1, 0], score[1, 1]], 1), solved[h])
        out = jnp.concatenate([top, low], 0)
        qeff[h] = (jnp.exp(cum) * qn[g].astype(F32) - out[:, :HEAD]).astype(BF16)
        loc[h] = out[:, HEAD:]

    def compose(later, earlier):
        return earlier + later + matmul(later[:, :HEAD].astype(BF16), earlier.astype(BF16))

    def apply(change, shift, before):
        return before + shift.astype(F32) + matmul(change, before.astype(BF16))

    def total_copy(k):
        return remote(row_total.at[k], total_in.at[k], total_send.at[k], total_recv.at[k], column_device(z + 1))

    def shift_copy(k):
        return remote(
            row_total.at[k, 1], total_in.at[k, 1], total_send.at[k], total_recv.at[k], column_device(z + 1)
        )

    def skip_copy(k):
        return remote(row_total.at[k], pair_in.at[k], pair_send.at[k], pair_recv.at[k], column_device(z + 2))

    def pair_copy(k):
        return remote(pair_out.at[k], pair_in.at[k], pair_send.at[k], pair_recv.at[k], column_device(z + 2))

    def state_copy(d, k):
        return remote(
            state_out.at[k], state_in.at[k], state_send.at[k, d - 1], state_recv.at[k], column_device(z + d)
        )

    def back_copy(core, i):
        return remote(
            row_states.at[core, i], states.at[x], back_send.at[core, i], back_recv.at[x], (z * NX + i, y * 2 + core)
        )

    def leaves(core, i):
        return jnp.logical_not(jnp.logical_and(core == 1, x == i))

    @pl.when(owner)
    def _():
        answers = jnp.where(jnp.logical_or(odd, z == 4), 2, 1)

        @pl.when(z != 7)
        def _():
            pl.semaphore_wait(ready_sem, jnp.where(z == 3, 4, answers))


        for core in range(2):
            for i in range(NX):
                row_copy = remote(
                    maps.at[0], row_maps.at[core, i], row_send.at[0], row_recv.at[core, i], sibling
                )
                pl.when(leaves(core, i))(row_copy.wait_recv)
        row_map = [[row_maps[core, i].astype(F32) for i in range(NX)] for core in range(2)]
        first_two = [compose(row_map[core][1], row_map[core][0]) for core in range(2)]
        last_two = [compose(row_map[core][3], row_map[core][2]) for core in range(2)]
        for core in range(2):
            total = compose(last_two[core], first_two[core]).astype(BF16)
            row_total[core, 0] = total[:, :HEAD]
            row_total[core, 1] = total[:, HEAD:]
        for core in range(2):
            pl.when(z == 0)(shift_copy(core).start)
            pl.when(both_of(z > 0, even))(total_copy(core).start)
        for core in range(2):
            pl.when(z == 4)(skip_copy(core).start)
        for core in range(2):
            prefix[core, 0] = row_map[core][0]
            prefix[core, 1] = first_two[core]
            prefix[core, 2] = compose(row_map[core][2], first_two[core])

        def joined(ref, k):
            return jnp.concatenate([ref[k, 0], ref[k, 1]], 1).astype(F32)

        @pl.when(z == 0)
        def _():
            state_before[...] = jnp.zeros_like(state_before)

        @pl.when(z == 1)
        def _():
            for core in range(2):
                shift_copy(core).wait_recv()
                shift = total_in[core, 1].astype(F32)
                state_before[core] = shift
                state_out[core] = apply(row_total[core, 0], row_total[core, 1], shift).astype(BF16)
                state_copy(2, core).start()
                state_copy(1, core).start()

        @pl.when(both_of(even, both_of(z > 0, z < 6)))
        def _():
            for core in range(2):
                state_copy(1, core).wait_recv()
                state_before[core] = state_in[core].astype(F32)

        @pl.when(both_of(odd, both_of(z > 1, z < 6)))
        def _():
            for core in range(2):
                total_copy(core).wait_recv()
                pair = compose(joined(row_total, core), joined(total_in, core)).astype(BF16)
                pair_out[core, 0] = pair[:, :HEAD]
                pair_out[core, 1] = pair[:, HEAD:]
                pl.when(z == 5)(pair_copy(core).start)
            for core in range(2):
                pl.when(z == 5)(total_copy(core).start)
            for core in range(2):
                state_copy(1, core).wait_recv()
                state = state_in[core].astype(F32)

                @pl.when(z == 3)
                def _():
                    state_out[core] = apply(pair_out[core, 0], pair_out[core, 1], state).astype(BF16)
                    for d in (4, 3, 2, 1):
                        state_copy(d, core).start()

                state_before[core] = apply(total_in[core, 0], total_in[core, 1], state)

        @pl.when(z == 6)
        def _():
            both = []
            for core in range(2):
                pair_copy(core).wait_recv()
                total_copy(core).wait_recv()
                both.append(compose(joined(total_in, core), joined(pair_in, core)))
            for core in range(2):
                state_copy(1, core).wait_recv()
                change = both[core][:, :HEAD].astype(BF16)
                state_before[core] = apply(change, both[core][:, HEAD:], state_in[core].astype(F32))

        @pl.when(z == 7)
        def _():
            for core in range(2):
                state_copy(1, core).wait_recv()
                pair_copy(core).wait_recv()
                total_copy(core).wait_recv()
                state = apply(pair_in[core, 0], pair_in[core, 1], state_in[core].astype(F32))
                state_before[core] = apply(total_in[core, 0], total_in[core, 1], state)

        for core in range(2):
            state = state_before[core]
            row_states[core, 0] = state.astype(BF16)
            pl.when(leaves(core, 0))(back_copy(core, 0).start)
            for i in range(1, NX):
                before_i = prefix[core, i - 1]
                row_states[core, i] = apply(
                    before_i[:, :HEAD].astype(BF16), before_i[:, HEAD:], state
                ).astype(BF16)
            for i in range(1, NX):
                pl.when(leaves(core, i))(back_copy(core, i).start)
        states[pl.ds(x, 1)] = row_states[1, pl.ds(x, 1)]

    def wait_owner():
        for core in range(2):
            pl.when(z == 0)(shift_copy(core).wait_send)
            pl.when(both_of(z > 0, jnp.logical_or(even, z == 5)))(total_copy(core).wait_send)
            pl.when(z == 4)(skip_copy(core).wait_send)
            pl.when(z == 5)(pair_copy(core).wait_send)
            for d in (1, 2):
                pl.when(z == 1)(state_copy(d, core).wait_send)
            for d in range(1, 5):
                pl.when(z == 3)(state_copy(d, core).wait_send)
        for core in range(2):
            for i in range(NX):
                pl.when(leaves(core, i))(back_copy(core, i).wait_send)

    pending.append(lambda: pl.when(owner)(wait_owner))
    for h in range(VALUE_HEADS):
        arrival = remote(
            row_states.at[0, 0], states.at[h], back_send.at[0, 0], back_recv.at[h], sibling
        )
        pl.when(jnp.logical_not(jnp.logical_and(owner, x == h)))(arrival.wait_recv)

    gain = norm_gain[...]
    hidden = []
    for h in range(VALUE_HEADS):
        g, r = divmod(h, 2)
        attended = loc[h] + matmul(qeff[h], states[h])
        back = lax.rsqrt(jnp.mean(attended * attended, -1, keepdims=True) + EPSILON)
        gate = out_gate[g, :, r * HEAD : (r + 1) * HEAD]
        hidden.append((attended * back * gain * gate).astype(BF16))
    hidden = jnp.concatenate(hidden, 1)

    def partial_for(r, core):
        columns = pl.ds(pl.multiple_of(core * FEATURES, FEATURES), FEATURES)
        return matmul(hidden, w_out[CHIPS.index(r), :, columns])

    def sibling_copy(r):
        return remote(sib_out.at[r], sib_in.at[r], sib_send.at[r], sib_recv.at[r], sibling)

    ring = {
        r: remote(ring_out.at[r - 1], ring_in.at[r - 1], ring_send.at[r - 1], ring_recv.at[r - 1], device)
        for r, device in ((1, above), (2, across), (3, below))
    }
    for copy in load_out:
        copy.wait()
    def send_sibling(r):
        sib_out[r] = partial_for(r, 1 - c if r == 0 else c).astype(BF16)
        sibling_copy(r).start()

    def send_ring(r):
        mine = partial_for(r, 1 - c)
        sibling_copy(r).wait_recv()
        ring_out[r - 1] = (mine + sib_in[r].astype(F32)).astype(BF16)
        ring[r].start()

    send_sibling(2)
    send_sibling(1)
    send_ring(2)
    send_sibling(3)
    send_ring(1)
    send_ring(3)
    send_sibling(0)
    total = partial_for(0, c)
    sibling_copy(0).wait_recv()
    total = total + sib_in[0].astype(F32)
    finish()
    for r in (2, 1, 3):
        ring[r].wait_recv()
        total = total + ring_in[r - 1].astype(F32)
    out_ref[...] = total.astype(BF16)

    for r in range(NY):
        sibling_copy(r).wait_send()
    for copy in ring.values():
        copy.wait_send()


def per_device(
    tokens,
    in_weight,
    gate_weight,
    conv_weight,
    decay_scale,
    dt_bias,
    beta_shift,
    norm_gain,
    out_weight,
):
    anywhere = pl.BlockSpec(memory_space=pltpu.HBM)
    vmem = pl.BlockSpec(memory_space=pltpu.VMEM)
    dma = pltpu.SemaphoreType.DMA
    return pl.pallas_call(
        kernel,
        out_shape=pltpu.VMEM((ROWS, FEATURES), BF16),
        in_specs=[anywhere] * 9,
        out_specs=vmem,
        scratch_shapes=[
            pltpu.VMEM((2 * VALUE_HEADS, 8 * FEATURES), BF16),
            pltpu.VMEM((4, GROUPS, CONV), BF16),
            pltpu.SMEM((VALUE_HEADS,), F32),
            pltpu.SMEM((VALUE_HEADS,), F32),
            pltpu.SMEM((VALUE_HEADS,), F32),
            pltpu.VMEM((1, HEAD), F32),
            pltpu.VMEM((NY, 2, ROWS, FEATURES), BF16),
            pltpu.VMEM((NY, 2 * FEATURES, GROUPS * GROUP), BF16),
            pltpu.VMEM((NY, VALUE_HEADS * HEAD, 2 * FEATURES), BF16),
            pltpu.VMEM((TILES, ROWS, 256), F32),
            pltpu.VMEM((8, 8 + ROWS, HEAD), F32),
            pltpu.VMEM((HALO, GROUPS * CONV), BF16),
            pltpu.VMEM((HALO, GROUPS * CONV), BF16),
            pltpu.VMEM((2, ROWS, HEAD), F32),
            pltpu.VMEM((GROUPS, ROWS, HEAD), BF16),
            pltpu.VMEM((GROUPS, ROWS, HEAD), BF16),
            pltpu.VMEM((VALUE_HEADS, ROWS, HEAD), BF16),
            pltpu.VMEM((VALUE_HEADS, HEAD, 2 * HEAD), BF16),
            pltpu.VMEM((2, NX, HEAD, 2 * HEAD), BF16),
            pltpu.VMEM((2, NX - 1, HEAD, 2 * HEAD), F32),
            pltpu.VMEM((2, 2, HEAD, HEAD), BF16),
            pltpu.VMEM((2, 2, HEAD, HEAD), BF16),
            pltpu.VMEM((2, 2, HEAD, HEAD), BF16),
            pltpu.VMEM((2, 2, HEAD, HEAD), BF16),
            pltpu.VMEM((2, HEAD, HEAD), BF16),
            pltpu.VMEM((2, HEAD, HEAD), BF16),
            pltpu.VMEM((2, HEAD, HEAD), F32),
            pltpu.VMEM((GROUPS, ROWS, 2 * HEAD), F32),
            pltpu.VMEM((VALUE_HEADS, len(BLOCKS), HEAD, HEAD), F32),
            pltpu.VMEM((2, NX, HEAD, HEAD), BF16),
            pltpu.VMEM((VALUE_HEADS, HEAD, HEAD), BF16),
            pltpu.VMEM((VALUE_HEADS, ROWS, HEAD), F32),
            pltpu.VMEM((VALUE_HEADS, ROWS, HEAD), BF16),
            pltpu.VMEM((NY, ROWS, FEATURES), BF16),
            pltpu.VMEM((NY, ROWS, FEATURES), BF16),
            pltpu.VMEM((NY - 1, ROWS, FEATURES), BF16),
            pltpu.VMEM((NY - 1, ROWS, FEATURES), BF16),
            dma,
            dma((6,)),
            dma((NY,)),
            dma((NY,)),
            dma((7,)),
            dma((NY, 2)),
            dma((7,)),
            dma((NY, 2)),
            dma((2,)),
            dma((NX,)),
            dma((2, NX)),
            dma((2,)),
            dma((2,)),
            dma((2,)),
            dma((2,)),
            dma((2, 4)),
            dma((2,)),
            pltpu.SemaphoreType.REGULAR,
            pltpu.SemaphoreType.REGULAR,
            dma((2, NX)),
            dma((NX,)),
            dma((NY,)),
            dma((NY,)),
            dma((NY - 1,)),
            dma((NY - 1,)),
        ],
        compiler_params=pltpu.CompilerParams(
            collective_id=0, has_side_effects=True, vmem_limit_bytes=60 * 1024 * 1024
        ),
    )(
        tokens,
        in_weight,
        gate_weight.T,
        conv_weight,
        decay_scale,
        dt_bias,
        beta_shift,
        norm_gain.reshape(1, HEAD),
        out_weight,
    )


def solution(mesh):
    in_specs = (
        P("seq", "head"),
        P(None, "head"),
        P(None, "head"),
        P(None, "head", None),
        P("head"),
        P("head"),
        P("head"),
        P(),
        P("head", None),
    )
    out_specs = P("seq", "head")
    return jax.shard_map(
        per_device, mesh=mesh, in_specs=in_specs, out_specs=out_specs, check_vma=False
    )
```
